32 devices in a mesh: bead: 16 (over z, y, x), slab: 2 (over core).
Axes of the slice: x: 2, y: 2, z: 4, core: 2. Of those that a mesh axis runs over, the one named last changes fastest.
Arguments:
- positions: float32 [3, 16, 256], P(None, 'bead', 'slab'), may hold values from -5 to 5
- velocities: float32 [3, 16, 256], P(None, 'bead', 'slab'), may hold values from -5 to 5
- atom_types: int32 [256], P('slab'), may hold values from 0 to 1
- live_atoms: int32 [2], P('slab'), may hold values from 16 to 128, as said below
- halo_rows: int32 [2, 128], P('slab'), may hold values from 0 to 127, as said below
- neighbours: int32 [256, 128], P('slab'), may hold values from -1 to 255, as said below
- type_scale: float32 [2, 25], replicated, may hold values from -4 to 4
- type_shift: float32 [2, 25], replicated, may hold values from -4 to 4
- embed_two: bfloat16 [25, 50], replicated, may hold values from -1.25 to 1.25
- embed_bias_two: float32 [50], replicated, may hold values from -3 to 3
- embed_three: bfloat16 [50, 100], replicated, may hold values from -0.875 to 0.875
- embed_bias_three: float32 [100], replicated, may hold values from -3 to 3
- fit_first: bfloat16 [1600, 240], replicated, may hold values from -0.625 to 0.625
- fit_bias_first: float32 [240], replicated, may hold values from -3 to 3
- fit_second: bfloat16 [240, 240], replicated, may hold values from -0.375 to 0.375
- fit_bias_second: float32 [240], replicated, may hold values from -3 to 3
- fit_third: bfloat16 [240, 240], replicated, may hold values from -0.375 to 0.375
- fit_bias_third: float32 [240], replicated, may hold values from -3 to 3
- fit_readout: float32 [2, 240], replicated, may hold values from -0.375 to 0.375
Outputs:
- positions_new: float32 [3, 16, 256], P(None, 'bead', 'slab')
- velocities_new: float32 [3, 16, 256], P(None, 'bead', 'slab')
- forces: float32 [3, 16, 256], P(None, 'bead', 'slab')
The draws below stay inside these ranges and needn't reach their ends.
Inputs may be any that keep to these rules, and one draw needn't show every extreme that they name: Slab s holds atoms in its first live_atoms[s] rows; one slab is full. The system is a water film with vacuum on both sides, so slabs crossing the vacuum hold few atoms. `halo_rows`: each entry is an occupied row of its slab; the first 64 of a slab go to the slab one lower (cyclic), the other 64 to the slab one higher. `neighbours`: -1 marks an empty slot; entries below 128 are occupied own rows of the slab, never the atom itself; entries from 128 on index the extended list's halo part. Rows at or past a slab's live count are all empty; an occupied row has between 64 and 128 filled slots, first, and some row of each slab has 128.
All inputs are finite; a program needn't handle non-finite values.
Results may differ from the reference program's by a relative error of at most 0.014.
Values sent between devices are 32-bit elements; how exact they have to be, the bound alone decides.
No kernel may reach another device: no remote copies, remote signals or barrier semaphores. Data moves between devices by JAX's collectives and lax.ppermute only.
A program may use at most 64 MiB of HBM per device.

```python
import jax
import jax.numpy as jnp
from jax import lax

E1 = 25
E2 = 50
E3 = 100
M2 = 16
FIT = 240
NEIGH = 128
BLOCK = 32
ATOMS_DEV = 128
HALO = 64
ATOMS = 256
BEADS = 16
N_SLAB = 2


def slab_live(key):
    slab_total = ATOMS // ATOMS_DEV
    spread = jax.random.randint(jax.random.fold_in(key, 101), (slab_total,), ATOMS_DEV // 8, ATOMS_DEV // 2 + 1)
    fullest = jax.random.randint(jax.random.fold_in(key, 102), (), 0, slab_total)
    return jnp.where(jnp.arange(slab_total) == fullest, ATOMS_DEV, spread).astype(jnp.int32)


def draw_live_atoms(key, part):
    return slab_live(key)


def draw_halo_rows(key, part):
    living = slab_live(key)
    slab_total = living.shape[0]
    return jax.random.randint(jax.random.fold_in(key, 103), (slab_total, 2 * HALO), 0, living[:, None]).astype(jnp.int32)


def draw_neighbours(key, part):
    living = slab_live(key)
    slab_total = living.shape[0]
    atom_rows = jnp.arange(ATOMS_DEV)[None, :]
    listed = jax.random.randint(jax.random.fold_in(key, 104), (slab_total, ATOMS_DEV), NEIGH // 2, NEIGH + 1)
    listed = jnp.where(atom_rows == 0, NEIGH, listed)
    listed = jnp.where(atom_rows < living[:, None], listed, 0)
    live_wide = living[:, None, None]
    chosen = jax.random.randint(jax.random.fold_in(key, 105), (slab_total, ATOMS_DEV, NEIGH), 0, live_wide + 2 * HALO)
    own_row = atom_rows[:, :, None]
    chosen = jnp.where(chosen == own_row, (own_row + 1) % live_wide, chosen)
    entries = jnp.where(chosen < live_wide, chosen, ATOMS_DEV + chosen - live_wide)
    slot_index = jnp.arange(NEIGH)[None, None, :]
    entries = jnp.where(slot_index < listed[:, :, None], entries, -1)
    return entries.reshape(slab_total * ATOMS_DEV, NEIGH).astype(jnp.int32)


def touch_ends(result, own_key, low, top_value):
    index_at = [jax.random.randint(jax.random.fold_in(own_key, axis), (), 0, length) for axis, length in enumerate(result.shape)]
    main_axis = result.shape.index(max(result.shape))
    neighbour = index_at[:main_axis] + [(index_at[main_axis] + 1) % result.shape[main_axis]] + index_at[main_axis + 1:]
    return result.at[tuple(index_at)].set(low).at[tuple(neighbour)].set(top_value)


def level_of(rng, extent, pieces, least, top_value):
    level = 1.0
    for dim, shards_of in pieces:
        draws = jax.random.uniform(jax.random.fold_in(jax.random.fold_in(rng, 6), dim), (shards_of,), jnp.float32, least / len(pieces), top_value / len(pieces))
        level = level * jnp.repeat(jnp.exp(draws), extent[dim] // shards_of).reshape((-1,) + (1,) * (len(extent) - 1 - dim))
    return level


def normal_values(key, shape, scale, limit, cuts=(), held_as=jnp.bfloat16):
    array = jax.random.normal(key, shape, jnp.float32) * scale
    if len(cuts) > 0:
        array = level_of(key, shape, cuts, -0.22, 0.18) * array
    return jnp.clip(array, min=-limit, max=limit).astype(held_as)


def setup_inputs(seed: int = 0) -> dict:
    arg_keys = jax.random.split(jax.random.key(seed), 20)
    return {
        "positions": normal_values(arg_keys[0], (3, BEADS, ATOMS), 1.0, 5.0, ((1, 16), (2, 2)), jnp.float32),
        "velocities": normal_values(arg_keys[1], (3, BEADS, ATOMS), 1.0, 5.0, ((1, 16), (2, 2)), jnp.float32),
        "atom_types": touch_ends(jax.random.randint(arg_keys[2], (ATOMS,), 0, 2), jax.random.fold_in(arg_keys[2], 1), 0, 1).astype(jnp.int32),
        "live_atoms": draw_live_atoms(jax.random.fold_in(arg_keys[19], 71), 0),
        "halo_rows": draw_halo_rows(jax.random.fold_in(arg_keys[19], 71), 0),
        "neighbours": draw_neighbours(jax.random.fold_in(arg_keys[19], 71), 0),
        "type_scale": normal_values(arg_keys[6], (2, E1), 1.0, 4.0, (), jnp.float32),
        "type_shift": normal_values(arg_keys[7], (2, E1), 1.0, 4.0, (), jnp.float32),
        "embed_two": normal_values(arg_keys[8], (E1, E2), E1 ** -0.5, 1.25),
        "embed_bias_two": normal_values(arg_keys[9], (E2,), 0.5, 3.0, (), jnp.float32),
        "embed_three": normal_values(arg_keys[10], (E2, E3), E2 ** -0.5, 0.875),
        "embed_bias_three": normal_values(arg_keys[11], (E3,), 0.5, 3.0, (), jnp.float32),
        "fit_first": normal_values(arg_keys[12], (E3 * M2, FIT), (E3 * M2 // 16) ** -0.5, 0.625),
        "fit_bias_first": normal_values(arg_keys[13], (FIT,), 0.5, 3.0, (), jnp.float32),
        "fit_second": normal_values(arg_keys[14], (FIT, FIT), FIT ** -0.5, 0.375),
        "fit_bias_second": normal_values(arg_keys[15], (FIT,), 0.5, 3.0, (), jnp.float32),
        "fit_third": normal_values(arg_keys[16], (FIT, FIT), FIT ** -0.5, 0.375),
        "fit_bias_third": normal_values(arg_keys[17], (FIT,), 0.5, 3.0, (), jnp.float32),
        "fit_readout": normal_values(arg_keys[18], (2, FIT), FIT ** -0.5, 0.375, (), jnp.float32),
    }


step_size = 0.25
phase_rate = 1.2
cutoff_sq = 16.0
softening = 0.25
heavy_mass = 16.0
highest = lax.Precision.HIGHEST

def mode_tables(bead_count):
    indices = jnp.arange(bead_count)
    bead_rows = indices[:, None].astype(jnp.float32)
    mode_cols = indices[None, :]
    mode_float = mode_cols.astype(jnp.float32)
    angles = 2.0 * jnp.pi * bead_rows * mode_float / bead_count
    norm_scale = jnp.sqrt(2.0 / bead_count)
    middle = bead_count // 2
    edge_value = 1.0 / jnp.sqrt(1.0 * bead_count)
    mode_basis = jnp.where(mode_cols == 0, edge_value, jnp.where(mode_cols < middle, norm_scale * jnp.cos(angles), jnp.where(mode_cols == middle, jnp.cos(jnp.pi * bead_rows) * edge_value, norm_scale * jnp.sin(angles))))
    sine_part = jnp.sin(jnp.pi * indices.astype(jnp.float32) / bead_count)
    ratio = 2.0 * sine_part
    phases = phase_rate * bead_count * sine_part
    guarded = jnp.where(indices == 0, 1.0, ratio)
    cosine = jnp.cos(phases)
    travel = jnp.where(indices == 0, 1.0, jnp.sin(phases) / guarded)
    spring = ratio * jnp.sin(phases)
    return (mode_basis, cosine, travel, spring)

def bead_matrices(bead_count):
    mode_basis, cosine, travel, spring = mode_tables(bead_count)

    def assemble(diagonal):
        return jnp.dot(mode_basis * diagonal[None, :], mode_basis.T, preferred_element_type=jnp.float32, precision=highest)
    return (assemble(cosine), assemble(travel), assemble(spring))

def block_energy(centre, beside_all, around_hydrogen, filled, centre_hydrogen, living, weights):
    type_scale, type_shift, embed_two, embed_bias_two, embed_three, embed_bias_three, fit_first, fit_bias_first, fit_second, fit_bias_second, fit_third, fit_bias_third, fit_readout = weights
    offsets = beside_all - centre[:, :, None]
    dist_sq = lax.optimization_barrier(jnp.sum(offsets * offsets, axis=0))
    softened = jnp.sqrt(dist_sq + softening)
    switch = jnp.maximum(1.0 - dist_sq / cutoff_sq, 0.0)
    strength = filled * switch * switch / softened
    environ = jnp.concatenate([strength[None], strength[None] * offsets / softened[None]], axis=0)
    block_rows, slot_count = strength.shape
    input_scale = type_scale[0] + around_hydrogen[..., None] * (type_scale[1] - type_scale[0])
    input_shift = type_shift[0] + around_hydrogen[..., None] * (type_shift[1] - type_shift[0])
    layer_one = jnp.tanh(strength[..., None] * input_scale + input_shift).reshape(block_rows * slot_count, -1)
    layer_two = jnp.tanh(jnp.dot(layer_one.astype(jnp.bfloat16), embed_two, preferred_element_type=jnp.float32) + embed_bias_two)
    layer_two = layer_two + jnp.concatenate([layer_one, layer_one], axis=1)
    layer_three = jnp.tanh(jnp.dot(layer_two.astype(jnp.bfloat16), embed_three, preferred_element_type=jnp.float32) + embed_bias_three)
    layer_three = layer_three + jnp.concatenate([layer_two, layer_two], axis=1)
    layer_three = layer_three.reshape(block_rows, slot_count, -1)
    features = jnp.einsum('bke,cbk->bec', layer_three, environ, precision=highest) / slot_count
    descriptor = jnp.einsum('bec,bfc->bef', features, features[:, :M2], precision=highest).reshape(block_rows, -1)
    fit_one = jnp.tanh(jnp.dot(descriptor.astype(jnp.bfloat16), fit_first, preferred_element_type=jnp.float32) + fit_bias_first)
    fit_two = jnp.tanh(jnp.dot(fit_one.astype(jnp.bfloat16), fit_second, preferred_element_type=jnp.float32) + fit_bias_second) + fit_one
    fit_three = jnp.tanh(jnp.dot(fit_two.astype(jnp.bfloat16), fit_third, preferred_element_type=jnp.float32) + fit_bias_third) + fit_two
    readout = fit_readout[0] + centre_hydrogen[:, None] * (fit_readout[1] - fit_readout[0])
    return jnp.sum(living * lax.optimization_barrier(jnp.sum(fit_three * readout, axis=1)))

def slab_gradient(extended, wide_hydrogen, slab_lists, live_count, block_count, weights):

    def add_block(block_index, gradient):
        first_row = block_index * BLOCK
        centre = lax.dynamic_slice_in_dim(extended, first_row, BLOCK, 1)
        listed = lax.dynamic_slice_in_dim(slab_lists, first_row, BLOCK, 0)
        filled = (listed >= 0).astype(jnp.float32)
        flat_rows = jnp.where(listed >= 0, listed, 0).reshape(-1).astype(jnp.int32)
        beside_all = extended[:, flat_rows].reshape(3, BLOCK, -1)
        around_hydrogen = wide_hydrogen[flat_rows].reshape(BLOCK, -1)
        centre_hydrogen = lax.dynamic_slice_in_dim(wide_hydrogen, first_row, BLOCK, 0)
        row_numbers = first_row + jnp.arange(BLOCK).astype(jnp.int32)
        living = (row_numbers < live_count).astype(jnp.float32)

        def energy_of(centre_in, around_in):
            return block_energy(centre_in, around_in, around_hydrogen, filled, centre_hydrogen, living, weights)
        energy, backward = jax.vjp(energy_of, centre, beside_all)
        grad_centre, grad_around = backward(jnp.ones_like(energy))
        gradient = gradient.at[:, flat_rows].add(grad_around.reshape(3, -1))
        current = lax.dynamic_slice_in_dim(gradient, first_row, BLOCK, 1)
        return lax.dynamic_update_slice_in_dim(gradient, current + grad_centre, first_row, 1)
    zeroed = jnp.zeros(extended.shape, jnp.float32)
    return lax.fori_loop(0, block_count, add_block, zeroed)

def reference(positions, velocities, atom_types, live_atoms, halo_rows, neighbours, type_scale, type_shift, embed_two, embed_bias_two, embed_three, embed_bias_three, fit_first, fit_bias_first, fit_second, fit_bias_second, fit_third, fit_bias_third, fit_readout):
    weights = (type_scale, type_shift, embed_two, embed_bias_two, embed_three, embed_bias_three, fit_first, fit_bias_first, fit_second, fit_bias_second, fit_third, fit_bias_third, fit_readout)
    hydrogen = (atom_types == 1).astype(jnp.float32)
    gradient_total = jnp.zeros((BEADS, 3, ATOMS), jnp.float32)
    for slab_index in range(N_SLAB):
        before = (slab_index - 1) % N_SLAB
        following = (slab_index + 1) % N_SLAB
        own_rows = jnp.arange(ATOMS_DEV).astype(jnp.int32) + slab_index * ATOMS_DEV
        rows_before = halo_rows[before, HALO:].astype(jnp.int32) + before * ATOMS_DEV
        rows_after = halo_rows[following, :HALO].astype(jnp.int32) + following * ATOMS_DEV
        gathered = jnp.concatenate([own_rows, rows_before, rows_after]).astype(jnp.int32)
        wide_hydrogen = hydrogen[gathered]
        slab_lists = neighbours[slab_index * ATOMS_DEV:(slab_index + 1) * ATOMS_DEV]
        live_count = live_atoms[slab_index]
        block_count = (live_count + BLOCK - 1) // BLOCK
        bead_fields = jnp.transpose(positions[:, :, gathered], (1, 0, 2))

        def bead_force(bead_field):
            return slab_gradient(bead_field, wide_hydrogen, slab_lists, live_count, block_count, weights)
        gradients = lax.map(bead_force, bead_fields)
        gradient_total = gradient_total.at[:, :, gathered].add(gradients)
    forces = -jnp.transpose(gradient_total, (1, 0, 2))
    inverse_mass = jnp.where(atom_types == 1, 1.0, 1.0 / heavy_mass)
    kicked = velocities + step_size * inverse_mass[None, None, :] * forces
    rot_cos, rot_travel, rot_spring = bead_matrices(BEADS)
    positions_new = jnp.einsum('ij,cja->cia', rot_cos, positions, precision=highest) + jnp.einsum('ij,cja->cia', rot_travel, kicked, precision=highest)
    velocities_new = jnp.einsum('ij,cja->cia', -rot_spring, positions, precision=highest) + jnp.einsum('ij,cja->cia', rot_cos, kicked, precision=highest)
    return (positions_new, velocities_new, forces)
```

```python
import functools
import math

import jax
import jax.numpy as jnp
import numpy as np
from jax import lax
from jax.experimental import pallas as pl
from jax.experimental.pallas import tpu as pltpu
from jax.sharding import PartitionSpec as P

M2 = 16
step_size = 0.25
phase_rate = 1.2
cutoff_sq = 16.0
softening = 0.25
heavy_mass = 16.0

F32 = jnp.float32
BF16 = jnp.bfloat16
LANES = 128
OCTET = 8
CHUNK = 32
ONE_AT = 20.0
VMEM_LIMIT = 48 * 1024 * 1024


def bead_tables(count):
    index = np.arange(count)
    angles = 2.0 * np.pi * np.outer(index, index) / count
    norm = math.sqrt(2.0 / count)
    edge = 1.0 / math.sqrt(count)
    middle = count // 2
    basis = np.where(
        index[None, :] == 0,
        edge,
        np.where(
            index[None, :] < middle,
            norm * np.cos(angles),
            np.where(
                index[None, :] == middle, np.cos(np.pi * index)[:, None] * edge, norm * np.sin(angles)
            ),
        ),
    )
    sine = np.sin(np.pi * index / count)
    ratio = 2.0 * sine
    phases = phase_rate * count * sine
    travel = np.where(index == 0, 1.0, np.sin(phases) / np.where(index == 0, 1.0, ratio))

    def assemble(diagonal):
        return (basis * diagonal[None, :]) @ basis.T

    return np.concatenate(
        [assemble(np.cos(phases)), assemble(travel), assemble(ratio * np.sin(phases))], axis=1
    ).astype(np.float32)


def lookup(table, indices):
    return jnp.take_along_axis(table, indices, axis=1, mode="promise_in_bounds")


def outgoing_kernel(positions_ref, types_ref, rows_ref, own_ref, send_ref):
    hydrogen = (types_ref[...] == 1).astype(F32)
    atoms = hydrogen.shape[1]
    own = jnp.concatenate(
        [positions_ref[0], positions_ref[1], positions_ref[2], hydrogen]
        + [jnp.zeros((OCTET - 4, atoms), F32)],
        axis=0,
    )
    own_ref[...] = own
    send_ref[...] = lookup(own, jnp.broadcast_to(rows_ref[...], own.shape))


def force_kernel(
    live_ref,
    own_ref,
    halo_ref,
    listed_ref,
    scale_ref,
    shift_ref,
    two_ref,
    bias_two_ref,
    three_ref,
    bias_three_ref,
    first_ref,
    fit_bias_first_ref,
    second_ref,
    fit_bias_second_ref,
    third_ref,
    fit_bias_third_ref,
    readout_ref,
    out_ref,
    own_t,
    padded,
    two_in,
    two_out,
    three_in,
    three_out,
    consts,
    environ,
    offset,
    around,
    kept_one,
    kept_two,
    kept_three,
    kept_sum,
    features,
    features_t,
    descriptor,
    grad_descriptor,
    grad_environ,
    grad_strength,
    grad_terms,
    centre_terms,
    scattered,
):
    live = live_ref[0]
    octets = (live + (OCTET - 1)) // OCTET
    atoms, slots = listed_ref.shape
    e1 = scale_ref.shape[1]
    e2 = two_ref.shape[1]
    e3 = three_ref.shape[1]
    rows_one, rows_two, rows_three = two_in.shape[0], three_in.shape[0], three_out.shape[0]
    copies_two, copies_three = e2 // e1, e3 // e1

    def split_bias(bias):
        high = bias.astype(BF16).astype(F32)
        return high, bias - high

    padded[...] = jnp.zeros_like(padded)
    bias_high, bias_low = split_bias(bias_two_ref[...])
    for k in range(copies_two):
        cols = slice(k * e1, (k + 1) * e1)
        padded[0:e1, k * CHUNK : k * CHUNK + e1] = two_ref[:, cols].astype(F32)
        padded[e1 : e1 + 1, k * CHUNK : k * CHUNK + e1] = bias_high[:, cols]
        padded[e1 + 1 : e1 + 2, k * CHUNK : k * CHUNK + e1] = bias_low[:, cols]
    table = padded[...]
    two_in[...] = table[:rows_one, :rows_two].astype(BF16)
    two_out[...] = table.T[:rows_two, :rows_one].astype(BF16)

    padded[...] = jnp.zeros_like(padded)
    bias_high, bias_low = split_bias(bias_three_ref[...])
    for k in range(copies_three):
        cols = slice(k * e1, (k + 1) * e1)
        for m in range(copies_two):
            padded[m * CHUNK : m * CHUNK + e1, k * CHUNK : k * CHUNK + e1] = three_ref[
                m * e1 : (m + 1) * e1, cols
            ].astype(F32)
        padded[e1 : e1 + 1, k * CHUNK : k * CHUNK + e1] = bias_high[:, cols]
        padded[e1 + 1 : e1 + 2, k * CHUNK : k * CHUNK + e1] = bias_low[:, cols]
    table = padded[...]
    three_in[...] = table[:rows_two, :rows_three].astype(BF16)
    three_out[...] = table.T[:rows_three, :rows_two].astype(BF16)

    padded[...] = jnp.zeros_like(padded)
    padded[0:2, 0:e1] = scale_ref[...]
    padded[2:4, 0:e1] = shift_ref[...]
    padded[2:3, e1 : e1 + 2] = jnp.full((1, 2), ONE_AT, F32)
    padded[3:4, e1 : e1 + 2] = jnp.full((1, 2), ONE_AT, F32)
    table = padded[...].T
    for k in range(4):
        column = table[:CHUNK, k : k + 1]
        if k % 2 == 1:
            column = column - table[:CHUNK, k - 1 : k]
        consts[k] = jnp.broadcast_to(column, (CHUNK, slots))

    padded[...] = jnp.zeros_like(padded)
    padded[0:OCTET, :] = own_ref[...]
    own_t[...] = padded[...].T

    features[...] = jnp.zeros_like(features)
    upper = lax.broadcasted_iota(jnp.int32, (OCTET, LANES), 0) < 4

    def pair_blocks(tile):
        zero = jnp.zeros_like(tile)
        return jnp.concatenate(
            [jnp.where(upper, tile, zero), jnp.where(upper, zero, tile)], axis=1
        ).astype(BF16)

    def gather_octet(first):
        listed = listed_ref[pl.ds(first, OCTET), :]
        low = jnp.bitwise_and(listed, LANES - 1)
        is_own = listed < atoms
        centre = own_t[pl.ds(first, OCTET), :]
        fetched = []
        for c in range(4):
            near = lookup(jnp.broadcast_to(own_ref[c : c + 1, :], (OCTET, LANES)), low)
            far = lookup(jnp.broadcast_to(halo_ref[c : c + 1, :], (OCTET, LANES)), low)
            fetched.append(jnp.where(is_own, near, far))
        deltas = [fetched[c] - centre[:, c : c + 1] for c in range(3)]
        return listed, deltas, fetched[3]

    def geometry(listed, deltas):
        filled = (listed >= 0).astype(F32)
        dist_sq = deltas[0] * deltas[0] + deltas[1] * deltas[1] + deltas[2] * deltas[2]
        inverse = lax.rsqrt(dist_sq + softening)
        switch = jnp.maximum(1.0 - dist_sq * (1.0 / cutoff_sq), 0.0)
        base = filled * switch * inverse
        return inverse, switch, base, base * switch

    def forward(octet, carry):
        first = pl.multiple_of(octet * OCTET, OCTET)
        listed, deltas, hydrogen = gather_octet(first)
        inverse, _, _, strength = geometry(listed, deltas)
        around[pl.ds(first, OCTET), :] = hydrogen
        scaled = strength * inverse
        environ[pl.ds(first * 4, OCTET, stride=4), :] = strength
        for c in range(3):
            offset[c, pl.ds(first, OCTET), :] = deltas[c]
            environ[pl.ds(first * 4 + 1 + c, OCTET, stride=4), :] = scaled * deltas[c]
        for pair in range(OCTET // 2):
            halves = []
            for a in (2 * pair, 2 * pair + 1):
                row, kind = strength[a : a + 1], hydrogen[a : a + 1]
                halves.append(
                    row * consts[0] + consts[2] + kind * (row * consts[1] + consts[3])
                )
            one = jnp.tanh(jnp.concatenate(halves, axis=1))
            two = jnp.tanh(jnp.dot(two_out[...], one.astype(BF16), preferred_element_type=F32))
            sum_two = two + jnp.concatenate([one] * copies_two, axis=0)
            three = jnp.tanh(
                jnp.dot(three_out[...], sum_two.astype(BF16), preferred_element_type=F32)
            )
            sum_three = (three + jnp.concatenate([sum_two] * 2, axis=0)).astype(BF16)
            at = octet * (OCTET // 2) + pair
            kept_one[at] = one
            kept_two[at] = two
            kept_three[at] = three
            kept_sum[at] = sum_three
            rows = pl.ds(pl.multiple_of(first * 4 + OCTET * pair, OCTET), OCTET)
            features[rows, :] = lax.dot_general(
                pair_blocks(environ[rows, :]),
                sum_three,
                (((1,), (1,)), ((), ())),
                preferred_element_type=F32,
            )
        return carry

    lax.fori_loop(0, octets, forward, 0)

    for c in range(4):
        features_t[c] = features[pl.ds(c, atoms, stride=4), :].T * (1.0 / slots)

    def descriptor_rows(r, carry):
        for q in range(copies_three):
            total = None
            for c in range(4):
                term = features_t[c, pl.ds(q * CHUNK + r, 1), :] * features_t[c, 0:M2, :]
                total = term if total is None else total + term
            at = pl.multiple_of((q * e1 + r) * M2, M2)
            descriptor[pl.ds(at, M2), :] = total.astype(BF16)
        return carry

    lax.fori_loop(0, e1, descriptor_rows, 0)

    fit_one = jnp.tanh(
        lax.dot_general(
            descriptor[...], first_ref[...], (((0,), (0,)), ((), ())), preferred_element_type=F32
        )
        + fit_bias_first_ref[...]
    )
    tanh_two = jnp.tanh(
        jnp.dot(fit_one.astype(BF16), second_ref[...], preferred_element_type=F32)
        + fit_bias_second_ref[...]
    )
    fit_two = tanh_two + fit_one
    tanh_three = jnp.tanh(
        jnp.dot(fit_two.astype(BF16), third_ref[...], preferred_element_type=F32)
        + fit_bias_third_ref[...]
    )
    living = (lax.broadcasted_iota(jnp.int32, (atoms, 1), 0) < live).astype(F32)
    readout = readout_ref[0:1, :] + own_t[:, 3:4] * (readout_ref[1:2, :] - readout_ref[0:1, :])
    grad = living * readout
    contract_last = (((1,), (1,)), ((), ()))
    inner = (grad * (1.0 - tanh_three * tanh_three)).astype(BF16)
    grad = grad + lax.dot_general(inner, third_ref[...], contract_last, preferred_element_type=F32)
    inner = (grad * (1.0 - tanh_two * tanh_two)).astype(BF16)
    grad = grad + lax.dot_general(inner, second_ref[...], contract_last, preferred_element_type=F32)
    inner = (grad * (1.0 - fit_one * fit_one)).astype(BF16)
    grad_descriptor[0 : e3 * M2, :] = lax.dot_general(
        first_ref[...], inner, contract_last, preferred_element_type=F32
    )

    def second_factor(r, carry):
        totals = list(carry)
        for q in range(copies_three):
            at = pl.multiple_of((q * e1 + r) * M2, M2)
            rows = grad_descriptor[pl.ds(at, M2), :]
            for c in range(4):
                totals[c] = totals[c] + rows * features_t[c, pl.ds(q * CHUNK + r, 1), :]
        return tuple(totals)

    shared = lax.fori_loop(
        0, e1, second_factor, tuple(jnp.zeros((M2, atoms), F32) for _ in range(4))
    )
    valid = lax.broadcasted_iota(jnp.int32, (CHUNK, atoms), 0) < e1
    by_column = [[] for _ in range(4)]
    for q in range(copies_three):
        totals = [jnp.zeros((CHUNK, atoms), F32) for _ in range(4)]
        for f in range(M2):
            rows = grad_descriptor[pl.ds(q * e1 * M2 + f, CHUNK, stride=M2), :]
            for c in range(4):
                totals[c] = totals[c] + rows * features_t[c, f : f + 1, :]
        for c in range(4):
            part = jnp.where(valid, totals[c], 0.0)
            if q == 0:
                part = part + jnp.concatenate(
                    [shared[c], jnp.zeros((CHUNK - M2, atoms), F32)], axis=0
                )
            by_column[c].append(part)
    for c in range(4):
        features[pl.ds(c, atoms, stride=4), :] = (
            jnp.concatenate(by_column[c], axis=0) * (1.0 / slots)
        ).T

    scattered[...] = jnp.zeros_like(scattered)
    centre_terms[...] = jnp.zeros_like(centre_terms)
    entries = scattered.shape[1]
    lane = lax.broadcasted_iota(jnp.int32, (OCTET, LANES), 1)

    def backward(octet, carry):
        first = pl.multiple_of(octet * OCTET, OCTET)
        grad_rows = features[pl.ds(pl.multiple_of(first * 4, OCTET * 4), OCTET * 4), :]
        grad_cols = grad_rows.T.astype(BF16)
        grad_rows = grad_rows.astype(BF16)
        listed = listed_ref[pl.ds(first, OCTET), :]
        for pair in range(OCTET // 2):
            at = octet * (OCTET // 2) + pair
            rows = pl.ds(pl.multiple_of(first * 4 + OCTET * pair, OCTET), OCTET)
            blocks = pair_blocks(environ[rows, :])
            grad_three = jnp.dot(
                grad_cols[:, OCTET * pair : OCTET * (pair + 1)], blocks, preferred_element_type=F32
            )
            both = jnp.dot(
                grad_rows[OCTET * pair : OCTET * (pair + 1), :],
                kept_sum[at],
                preferred_element_type=F32,
            )
            grad_environ[rows, :] = jnp.where(upper, both[:, :LANES], both[:, LANES:])
            three = kept_three[at]
            inner = (grad_three * (1.0 - three * three)).astype(BF16)
            grad_two = (
                jnp.dot(three_in[...], inner, preferred_element_type=F32)
                + grad_three[:rows_two]
                + grad_three[rows_two:]
            )
            two = kept_two[at]
            inner = (grad_two * (1.0 - two * two)).astype(BF16)
            grad_one = jnp.dot(two_in[...], inner, preferred_element_type=F32)
            for k in range(copies_two):
                grad_one = grad_one + grad_two[k * CHUNK : (k + 1) * CHUNK]
            one = kept_one[at]
            grad_one = grad_one * (1.0 - one * one)
            for half in range(2):
                row = first + 2 * pair + half
                kind = around[pl.ds(row, 1), :]
                weighed = grad_one[:, half * LANES : (half + 1) * LANES] * (
                    consts[0] + kind * consts[1]
                )
                grad_strength[pl.ds(row, 1), :] = jnp.sum(weighed, axis=0, keepdims=True)

        deltas = [offset[c, pl.ds(first, OCTET), :] for c in range(3)]
        inverse, switch, base, strength = geometry(listed, deltas)
        by_environ = [
            grad_environ[pl.ds(first * 4 + c, OCTET, stride=4), :] for c in range(4)
        ]
        along = (
            by_environ[1] * deltas[0] + by_environ[2] * deltas[1] + by_environ[3] * deltas[2]
        )
        by_strength = (
            grad_strength[pl.ds(first, OCTET), :] + by_environ[0] + along * inverse
        )
        filled = (listed >= 0).astype(F32)
        by_inverse = strength * along + filled * switch * switch * by_strength
        by_dist = (-2.0 / cutoff_sq) * base * by_strength - (
            0.5 * inverse * inverse * inverse
        ) * by_inverse
        scaled = strength * inverse
        centre = jnp.zeros((OCTET, LANES), F32)
        for c in range(3):
            term = by_environ[1 + c] * scaled + 2.0 * deltas[c] * by_dist
            grad_terms[pl.ds(first * 4 + c, OCTET, stride=4), :] = term
            centre = jnp.where(lane == c, jnp.sum(term, axis=1, keepdims=True), centre)
        grad_terms[pl.ds(first * 4 + 3, OCTET, stride=4), :] = jnp.zeros((OCTET, LANES), F32)
        centre_terms[pl.ds(first, OCTET), :] = centre
        total = jnp.zeros((OCTET, entries), F32)
        numbers = lax.broadcasted_iota(jnp.int32, (entries, LANES), 0)
        for pair in range(OCTET // 2):
            rows = pl.ds(pl.multiple_of(first * 4 + OCTET * pair, OCTET), OCTET)
            hits = jnp.concatenate(
                [
                    (numbers == listed[a : a + 1, :]).astype(F32).astype(BF16)
                    for a in (2 * pair, 2 * pair + 1)
                ],
                axis=1,
            )
            total = total + lax.dot_general(
                pair_blocks(grad_terms[rows, :]), hits, contract_last, preferred_element_type=F32
            )
        scattered[...] += total
        return carry

    lax.fori_loop(0, octets, backward, 0)
    total = scattered[0:4, :] + scattered[4:8, :]
    centre = centre_terms[...].T[0:4, :]
    out_ref[0:4, 0:atoms] = centre - total[:, 0:atoms]
    out_ref[0:4, atoms:] = -total[:, atoms:]
    out_ref[4:8, :] = jnp.zeros((4, entries), F32)


def kick_kernel(part_ref, back_ref, rows_ref, types_ref, positions_ref, velocities_ref, forces_ref, out_ref):
    atoms = types_ref.shape[1]
    rows = rows_ref[...]
    hits = (
        lax.broadcasted_iota(jnp.int32, (atoms, rows.shape[1]), 0) == rows
    ).astype(F32)
    returned = lax.dot_general(
        back_ref[...],
        hits,
        (((1,), (1,)), ((), ())),
        preferred_element_type=F32,
        precision=lax.Precision.HIGHEST,
    )
    force = part_ref[:, 0:atoms] + returned
    inverse_mass = jnp.where(types_ref[...] == 1, 1.0, 1.0 / heavy_mass)
    rows = []
    for c in range(3):
        forces_ref[c] = force[c : c + 1]
        rows.append(positions_ref[c])
    for c in range(3):
        rows.append(velocities_ref[c] + step_size * inverse_mass * force[c : c + 1])
    tile = jnp.concatenate(rows + [jnp.zeros((2, atoms), F32)], axis=0)
    for b in range(out_ref.shape[0]):
        out_ref[b] = tile


def mix_kernel(bead_ref, table_ref, gathered_ref, positions_ref, velocities_ref):
    mine = bead_ref[0]
    count = gathered_ref.shape[0]
    tile_shape = gathered_ref.shape[1:]
    is_position = lax.broadcasted_iota(jnp.int32, tile_shape, 0) < 3
    turned = jnp.zeros(tile_shape, F32)
    crossed = jnp.zeros(tile_shape, F32)
    for b in range(count):
        tile = gathered_ref[b]
        turned = turned + table_ref[mine, b] * tile
        crossed = crossed + jnp.where(
            is_position, -table_ref[mine, 2 * count + b], table_ref[mine, count + b]
        ) * tile
    for c in range(3):
        positions_ref[c] = turned[c : c + 1] + crossed[3 + c : 4 + c]
        velocities_ref[c] = turned[3 + c : 4 + c] + crossed[c : c + 1]


VMEM_SPEC = pl.BlockSpec(memory_space=pltpu.VMEM)
SMEM_SPEC = pl.BlockSpec(memory_space=pltpu.SMEM)


def shape(*dims, dtype=F32):
    return jax.ShapeDtypeStruct(dims, dtype)


def call_force(live_atoms, own, halo, neighbours, weights):
    atoms, slots = neighbours.shape
    entries = atoms + halo.shape[1]
    e1 = weights[0].shape[1]
    e2 = weights[2].shape[1]
    e3 = weights[4].shape[1]
    rows_two = e2 // e1 * CHUNK
    rows_three = e3 // e1 * CHUNK
    assert slots == LANES and atoms == LANES and entries == 2 * LANES
    assert e3 == 2 * e2 and e2 == 2 * e1 and rows_three <= LANES and M2 <= e1
    pairs = atoms // 2
    return pl.pallas_call(
        force_kernel,
        out_shape=shape(OCTET, entries),
        in_specs=[SMEM_SPEC] + [VMEM_SPEC] * (3 + len(weights)),
        out_specs=VMEM_SPEC,
        scratch_shapes=[
            pltpu.VMEM((atoms, LANES), F32),
            pltpu.VMEM((LANES, LANES), F32),
            pltpu.VMEM((CHUNK, rows_two), BF16),
            pltpu.VMEM((rows_two, CHUNK), BF16),
            pltpu.VMEM((rows_two, rows_three), BF16),
            pltpu.VMEM((rows_three, rows_two), BF16),
            pltpu.VMEM((4, CHUNK, slots), F32),
            pltpu.VMEM((4 * atoms, slots), F32),
            pltpu.VMEM((3, atoms, slots), F32),
            pltpu.VMEM((atoms, slots), F32),
            pltpu.VMEM((pairs, CHUNK, 2 * slots), F32),
            pltpu.VMEM((pairs, rows_two, 2 * slots), F32),
            pltpu.VMEM((pairs, rows_three, 2 * slots), F32),
            pltpu.VMEM((pairs, rows_three, 2 * slots), BF16),
            pltpu.VMEM((4 * atoms, rows_three), F32),
            pltpu.VMEM((4, rows_three, atoms), F32),
            pltpu.VMEM((e3 * M2, atoms), BF16),
            pltpu.VMEM(((e3 + CHUNK) * M2, atoms), F32),
            pltpu.VMEM((4 * atoms, slots), F32),
            pltpu.VMEM((atoms, slots), F32),
            pltpu.VMEM((4 * atoms, slots), F32),
            pltpu.VMEM((atoms, LANES), F32),
            pltpu.VMEM((OCTET, entries), F32),
        ],
        compiler_params=pltpu.CompilerParams(vmem_limit_bytes=VMEM_LIMIT),
        name="force",
    )(live_atoms, own, halo, neighbours, *weights)


def row(array):
    return array.reshape(1, -1)


def local(
    positions,
    velocities,
    atom_types,
    live_atoms,
    halo_rows,
    neighbours,
    type_scale,
    type_shift,
    embed_two,
    embed_bias_two,
    embed_three,
    embed_bias_three,
    fit_first,
    fit_bias_first,
    fit_second,
    fit_bias_second,
    fit_third,
    fit_bias_third,
    fit_readout,
):
    weights = (
        type_scale,
        type_shift,
        embed_two,
        row(embed_bias_two),
        embed_three,
        row(embed_bias_three),
        fit_first,
        row(fit_bias_first),
        fit_second,
        row(fit_bias_second),
        fit_third,
        row(fit_bias_third),
        fit_readout,
    )
    atoms = positions.shape[2]
    half = halo_rows.shape[1] // 2
    beads = lax.axis_size("bead")
    slabs = lax.axis_size("slab")
    to_next = [(i, (i + 1) % slabs) for i in range(slabs)]
    to_last = [((i + 1) % slabs, i) for i in range(slabs)]

    def exchange(outgoing, up, down):
        if slabs == 2:
            return lax.ppermute(outgoing, "slab", to_next)
        return jnp.concatenate(
            [
                lax.ppermute(outgoing[:, up], "slab", to_next),
                lax.ppermute(outgoing[:, down], "slab", to_last),
            ],
            axis=1,
        )

    low, high = slice(0, half), slice(half, 2 * half)
    rows = jnp.concatenate([halo_rows[:, high], halo_rows[:, low]], axis=1)
    types = row(atom_types)
    own, sent = pl.pallas_call(
        outgoing_kernel,
        out_shape=(shape(OCTET, atoms), shape(OCTET, 2 * half)),
        in_specs=[VMEM_SPEC] * 3,
        out_specs=(VMEM_SPEC, VMEM_SPEC),
        name="outgoing",
    )(positions, types, rows)
    halo = exchange(sent, low, high)
    part = call_force(live_atoms, own, halo, neighbours, weights)
    back = exchange(part[:, atoms:], high, low)
    if slabs != 2:
        back = jnp.concatenate([back[:, high], back[:, low]], axis=1)
    forces, kicked = pl.pallas_call(
        kick_kernel,
        out_shape=(shape(*positions.shape), shape(beads, OCTET, atoms)),
        in_specs=[VMEM_SPEC] * 6,
        out_specs=(VMEM_SPEC, VMEM_SPEC),
        name="kick",
    )(part, back, rows, types, positions, velocities)
    gathered = lax.all_to_all(kicked, "bead", split_axis=0, concat_axis=0, tiled=True)
    table = jnp.asarray(bead_tables(beads))
    mine = lax.axis_index("bead").astype(jnp.int32).reshape(1)
    positions_new, velocities_new = pl.pallas_call(
        mix_kernel,
        out_shape=(shape(*positions.shape), shape(*positions.shape)),
        in_specs=[SMEM_SPEC, SMEM_SPEC, VMEM_SPEC],
        out_specs=(VMEM_SPEC, VMEM_SPEC),
        name="mix",
    )(mine, table, gathered)
    return positions_new, velocities_new, forces


def solution(mesh):
    sharded = P(None, "bead", "slab")
    return jax.shard_map(
        local,
        mesh=mesh,
        in_specs=(
            sharded,
            sharded,
            P("slab"),
            P("slab"),
            P("slab", None),
            P("slab", None),
        )
        + (P(),) * 13,
        out_specs=(sharded, sharded, sharded),
        check_vma=False,
    )
```

```python
import functools
import math

import jax
import jax.numpy as jnp
import numpy as np
from jax import lax
from jax.experimental import pallas as pl
from jax.experimental.pallas import tpu as pltpu
from jax.sharding import PartitionSpec as P

M2 = 16
step_size = 0.25
phase_rate = 1.2
cutoff_sq = 16.0
softening = 0.25
heavy_mass = 16.0

F32 = jnp.float32
BF16 = jnp.bfloat16
LANES = 128
OCTET = 8
UNROLL = 8
DIGIT = 16
GROUP = 8
CHUNK = 32
ONE_AT = 20.0
VMEM_LIMIT = 40 * 1024 * 1024
SMALL_LIMIT = 4 * 1024 * 1024


def bead_tables(count):
    index = np.arange(count)
    angles = 2.0 * np.pi * np.outer(index, index) / count
    norm = math.sqrt(2.0 / count)
    edge = 1.0 / math.sqrt(count)
    middle = count // 2
    basis = np.where(
        index[None, :] == 0,
        edge,
        np.where(
            index[None, :] < middle,
            norm * np.cos(angles),
            np.where(
                index[None, :] == middle, np.cos(np.pi * index)[:, None] * edge, norm * np.sin(angles)
            ),
        ),
    )
    sine = np.sin(np.pi * index / count)
    ratio = 2.0 * sine
    phases = phase_rate * count * sine
    travel = np.where(index == 0, 1.0, np.sin(phases) / np.where(index == 0, 1.0, ratio))

    def assemble(diagonal):
        return (basis * diagonal[None, :]) @ basis.T

    return np.concatenate(
        [assemble(np.cos(phases)), assemble(travel), assemble(ratio * np.sin(phases))], axis=1
    ).astype(np.float32)


def lookup(table, indices):
    return jnp.take_along_axis(table, indices, axis=1, mode="promise_in_bounds")


def turned_rows(rows_ref):
    rows = rows_ref[...]
    half = rows.shape[1] // 2
    return jnp.concatenate([rows[:, half:], rows[:, :half]], axis=1)


def outgoing_kernel(positions_ref, types_ref, rows_ref, own_ref, send_ref):
    hydrogen = (types_ref[...] == 1).astype(F32)
    atoms = hydrogen.shape[1]
    own = jnp.concatenate(
        [positions_ref[0], positions_ref[1], positions_ref[2], hydrogen]
        + [jnp.zeros((OCTET - 4, atoms), F32)],
        axis=0,
    )
    own_ref[...] = own
    send_ref[...] = lookup(own, jnp.broadcast_to(turned_rows(rows_ref), own.shape))


def force_kernel(
    live_ref,
    own_ref,
    halo_ref,
    listed_ref,
    scale_ref,
    shift_ref,
    two_ref,
    bias_two_ref,
    three_ref,
    bias_three_ref,
    first_ref,
    fit_bias_first_ref,
    second_ref,
    fit_bias_second_ref,
    third_ref,
    fit_bias_third_ref,
    readout_ref,
    velocities_ref,
    out_ref,
    parcels_ref,
    own_t,
    padded,
    two_in,
    two_out,
    three_in,
    three_out,
    consts,
    environ,
    offset,
    around,
    kept_one,
    kept_two,
    kept_three,
    kept_sum,
    features,
    features_t,
    descriptor,
    grad_descriptor,
    first_rows,
    products,
    grad_environ,
    grad_strength,
    centre_terms,
    scattered,
):
    live = live_ref[0]
    octets = (live + (OCTET - 1)) // OCTET
    atoms, slots = listed_ref.shape
    e1 = scale_ref.shape[1]
    e2 = two_ref.shape[1]
    e3 = three_ref.shape[1]
    rows_one, rows_two, rows_three = two_in.shape[0], three_in.shape[0], three_out.shape[0]
    copies_two, copies_three = e2 // e1, e3 // e1

    first_rows[...] = first_ref[...].T

    def split_bias(bias):
        high = bias.astype(BF16).astype(F32)
        return high, bias - high

    padded[...] = jnp.zeros_like(padded)
    bias_high, bias_low = split_bias(bias_two_ref[...])
    for k in range(copies_two):
        cols = slice(k * e1, (k + 1) * e1)
        padded[0:e1, k * CHUNK : k * CHUNK + e1] = two_ref[:, cols].astype(F32)
        padded[e1 : e1 + 1, k * CHUNK : k * CHUNK + e1] = bias_high[:, cols]
        padded[e1 + 1 : e1 + 2, k * CHUNK : k * CHUNK + e1] = bias_low[:, cols]
    table = padded[...]
    two_in[...] = table[:rows_one, :rows_two].astype(BF16)
    two_out[...] = table.T[:rows_two, :rows_one].astype(BF16)

    padded[...] = jnp.zeros_like(padded)
    bias_high, bias_low = split_bias(bias_three_ref[...])
    for k in range(copies_three):
        cols = slice(k * e1, (k + 1) * e1)
        for m in range(copies_two):
            padded[m * CHUNK : m * CHUNK + e1, k * CHUNK : k * CHUNK + e1] = three_ref[
                m * e1 : (m + 1) * e1, cols
            ].astype(F32)
        padded[e1 : e1 + 1, k * CHUNK : k * CHUNK + e1] = bias_high[:, cols]
        padded[e1 + 1 : e1 + 2, k * CHUNK : k * CHUNK + e1] = bias_low[:, cols]
    table = padded[...]
    three_in[...] = table[:rows_two, :rows_three].astype(BF16)
    three_out[...] = table.T[:rows_three, :rows_two].astype(BF16)

    padded[...] = jnp.zeros_like(padded)
    padded[0:2, 0:e1] = scale_ref[...]
    padded[2:4, 0:e1] = shift_ref[...]
    padded[2:3, e1 : e1 + 2] = jnp.full((1, 2), ONE_AT, F32)
    padded[3:4, e1 : e1 + 2] = jnp.full((1, 2), ONE_AT, F32)
    table = padded[...].T
    for k in range(4):
        column = table[:CHUNK, k : k + 1]
        if k % 2 == 1:
            column = column - table[:CHUNK, k - 1 : k]
        consts[k] = jnp.broadcast_to(column, (CHUNK, slots))

    padded[...] = jnp.zeros_like(padded)
    padded[0:OCTET, :] = own_ref[...]
    own_t[...] = padded[...].T

    features[...] = jnp.zeros_like(features)
    def gather_octet(first):
        listed = listed_ref[pl.ds(first, OCTET), :]
        low = jnp.bitwise_and(listed, LANES - 1)
        is_own = listed < atoms
        centre = own_t[pl.ds(first, OCTET), :]
        fetched = []
        for c in range(4):
            near = lookup(jnp.broadcast_to(own_ref[c : c + 1, :], (OCTET, LANES)), low)
            far = lookup(jnp.broadcast_to(halo_ref[c : c + 1, :], (OCTET, LANES)), low)
            fetched.append(jnp.where(is_own, near, far))
        deltas = [fetched[c] - centre[:, c : c + 1] for c in range(3)]
        return listed, deltas, fetched[3]

    def geometry(listed, deltas):
        filled = (listed >= 0).astype(F32)
        dist_sq = deltas[0] * deltas[0] + deltas[1] * deltas[1] + deltas[2] * deltas[2]
        inverse = lax.rsqrt(dist_sq + softening)
        switch = jnp.maximum(1.0 - dist_sq * (1.0 / cutoff_sq), 0.0)
        base = filled * switch * inverse
        return inverse, switch, base, base * switch

    def run_octets(step, carry=0):
        def body(turn, carry):
            for u in range(UNROLL):
                carry = step(turn * UNROLL + u, carry)
            return carry

        return lax.fori_loop(0, (octets + UNROLL - 1) // UNROLL, body, carry)

    def surround(octet, carry):
        first = pl.multiple_of(octet * OCTET, OCTET)
        listed, deltas, hydrogen = gather_octet(first)
        inverse, _, _, strength = geometry(listed, deltas)
        around[pl.ds(first, OCTET), :] = hydrogen
        scaled = strength * inverse
        environ[pl.ds(first * 4, OCTET, stride=4), :] = strength
        for c in range(3):
            offset[c, pl.ds(first, OCTET), :] = deltas[c]
            environ[pl.ds(first * 4 + 1 + c, OCTET, stride=4), :] = scaled * deltas[c]
        return carry

    run_octets(surround)

    def forward(octet, carry):
        first = pl.multiple_of(octet * OCTET, OCTET)
        hydrogen = around[pl.ds(first, OCTET), :]
        rows = pl.ds(pl.multiple_of(first * 4, OCTET * 4), OCTET * 4)
        groups = range(OCTET // GROUP)
        ones, twos, threes = [], [], []
        for g in groups:
            inputs = []
            for a in range(g * GROUP, (g + 1) * GROUP):
                line, kind = environ[pl.ds(first * 4 + 4 * a, 1), :], hydrogen[a : a + 1]
                inputs.append(
                    line * consts[0] + consts[2] + kind * (line * consts[1] + consts[3])
                )
            ones.append(jnp.tanh(jnp.concatenate(inputs, axis=1).astype(BF16)))
        for g in groups:
            kept_one[octet * len(groups) + g] = ones[g]
            two = jnp.tanh(
                jnp.dot(two_out[...], ones[g], preferred_element_type=F32).astype(BF16)
            )
            kept_two[octet * len(groups) + g] = two
            twos.append(two + jnp.concatenate([ones[g]] * copies_two, axis=0))
        by_slot = environ[rows, :].T.astype(BF16)
        column = lax.broadcasted_iota(jnp.int32, by_slot.shape, 1) // 4
        total = jnp.zeros((rows_three, OCTET * 4), F32)
        for g in groups:
            three = jnp.tanh(
                jnp.dot(three_out[...], twos[g], preferred_element_type=F32).astype(BF16)
            )
            kept_three[octet * len(groups) + g] = three
            sum_three = three + jnp.concatenate([twos[g]] * 2, axis=0)
            kept_sum[octet * len(groups) + g] = sum_three
            blocks = jnp.concatenate(
                [
                    jnp.where(column == a, by_slot, jnp.zeros_like(by_slot))
                    for a in range(g * GROUP, (g + 1) * GROUP)
                ],
                axis=0,
            )
            total = total + jnp.dot(sum_three, blocks, preferred_element_type=F32)
        features[rows, :] = total.T
        return carry

    run_octets(forward)

    for c in range(4):
        features_t[c] = features[pl.ds(c, atoms, stride=4), :].T * (1.0 / slots)

    unit_rows = [q * CHUNK + r for q in range(copies_three) for r in range(e1)]
    leading = [features_t[c, 0:M2, :] for c in range(4)]
    for e, at in enumerate(unit_rows):
        total = None
        for c in range(4):
            term = features_t[c, at : at + 1, :] * leading[c]
            total = term if total is None else total + term
        descriptor[e * M2 : (e + 1) * M2, :] = total.astype(BF16)

    fit_one = jnp.tanh(
        jnp.dot(first_ref[...], descriptor[...], preferred_element_type=F32).T
        + fit_bias_first_ref[...]
    )
    tanh_two = jnp.tanh(
        jnp.dot(fit_one.astype(BF16), second_ref[...], preferred_element_type=F32)
        + fit_bias_second_ref[...]
    )
    fit_two = tanh_two + fit_one
    tanh_three = jnp.tanh(
        jnp.dot(fit_two.astype(BF16), third_ref[...], preferred_element_type=F32)
        + fit_bias_third_ref[...]
    )
    living = (lax.broadcasted_iota(jnp.int32, (atoms, 1), 0) < live).astype(F32)
    readout = readout_ref[0:1, :] + own_t[:, 3:4] * (readout_ref[1:2, :] - readout_ref[0:1, :])
    grad = living * readout
    contract_last = (((1,), (1,)), ((), ()))
    inner = (grad * (1.0 - tanh_three * tanh_three)).astype(BF16)
    grad = grad + lax.dot_general(inner, third_ref[...], contract_last, preferred_element_type=F32)
    inner = (grad * (1.0 - tanh_two * tanh_two)).astype(BF16)
    grad = grad + lax.dot_general(inner, second_ref[...], contract_last, preferred_element_type=F32)
    inner = (grad * (1.0 - fit_one * fit_one)).astype(BF16)
    grad_descriptor[...] = lax.dot_general(
        first_rows[...], inner, contract_last, preferred_element_type=F32
    )

    shared = [jnp.zeros((M2, atoms), F32) for _ in range(4)]
    short = [tile.astype(BF16) for tile in leading]
    for e, at in enumerate(unit_rows):
        rows = grad_descriptor[e * M2 : (e + 1) * M2, :]
        packed = rows.astype(BF16)
        for c in range(4):
            shared[c] = shared[c] + rows * features_t[c, at : at + 1, :]
            products[e * M2 : (e + 1) * M2, c * atoms : (c + 1) * atoms] = packed * short[c]
    unit = lax.broadcasted_iota(jnp.int32, (rows_three, e3 * M2), 0)
    unit = jnp.where(unit % CHUNK < e1, unit // CHUNK * e1 + unit % CHUNK, -1)
    gather = (lax.broadcasted_iota(jnp.int32, (rows_three, e3 * M2), 1) // M2 == unit).astype(F32)
    sums = jnp.dot(gather.astype(BF16), products[...], preferred_element_type=F32)
    for c in range(4):
        total = sums[:, c * atoms : (c + 1) * atoms] + jnp.concatenate(
            [shared[c], jnp.zeros((rows_three - M2, atoms), F32)], axis=0
        )
        features[pl.ds(c, atoms, stride=4), :] = (total * (1.0 / slots)).T

    scattered[...] = jnp.zeros_like(scattered)
    centre_terms[...] = jnp.zeros_like(centre_terms)
    lane = lax.broadcasted_iota(jnp.int32, (OCTET, LANES), 1)

    def backward(octet, carry):
        first = pl.multiple_of(octet * OCTET, OCTET)
        grad_rows = features[pl.ds(pl.multiple_of(first * 4, OCTET * 4), OCTET * 4), :]
        grad_cols = grad_rows.T.astype(BF16)
        grad_rows = grad_rows.astype(BF16)
        groups = range(OCTET // GROUP)
        rows = pl.ds(pl.multiple_of(first * 4, OCTET * 4), OCTET * 4)
        quads = environ[rows, :]
        owner = lax.broadcasted_iota(jnp.int32, quads.shape, 0) // 4
        by_quad = jnp.zeros_like(quads)
        inners, grad_threes, grad_twos = [], [], []
        for g in groups:
            at = octet * len(groups) + g
            blocks = jnp.concatenate(
                [
                    jnp.where(owner == a, quads, 0.0).astype(BF16)
                    for a in range(g * GROUP, (g + 1) * GROUP)
                ],
                axis=1,
            )
            grad_three = jnp.dot(grad_cols, blocks, preferred_element_type=F32).astype(BF16)
            three = kept_three[at]
            inners.append(grad_three * (1.0 - three * three))
            grad_threes.append(grad_three[:rows_two] + grad_three[rows_two:])
        for g in groups:
            at = octet * len(groups) + g
            grad_two = (
                jnp.dot(three_in[...], inners[g], preferred_element_type=F32).astype(BF16)
                + grad_threes[g]
            )
            two = kept_two[at]
            inners[g] = grad_two * (1.0 - two * two)
            folded = grad_two[:CHUNK]
            for k in range(1, copies_two):
                folded = folded + grad_two[k * CHUNK : (k + 1) * CHUNK]
            grad_twos.append(folded)
            both = jnp.dot(grad_rows, kept_sum[at], preferred_element_type=F32)
            for k in range(GROUP):
                by_quad = jnp.where(
                    owner == g * GROUP + k, both[:, k * LANES : (k + 1) * LANES], by_quad
                )
        grad_environ[rows, :] = by_quad
        for g in groups:
            at = octet * len(groups) + g
            grad_one = jnp.dot(two_in[...], inners[g], preferred_element_type=F32) + grad_twos[g]
            one = kept_one[at].astype(F32)
            grad_one = grad_one * (1.0 - one * one)
            for k in range(GROUP):
                line = first + g * GROUP + k
                kind = around[pl.ds(line, 1), :]
                weighed = grad_one[:, k * LANES : (k + 1) * LANES] * (
                    consts[0] + kind * consts[1]
                )
                grad_strength[pl.ds(line, 1), :] = jnp.sum(weighed, axis=0, keepdims=True)

        return carry

    run_octets(backward)

    numbers = lax.broadcasted_iota(jnp.int32, (DIGIT, LANES), 0).astype(F32).astype(BF16)

    def tall(line):
        return jnp.broadcast_to(line, (DIGIT, LANES)).astype(BF16)

    def disperse(octet, total):
        first = pl.multiple_of(octet * OCTET, OCTET)
        listed = listed_ref[pl.ds(first, OCTET), :]
        deltas = [offset[c, pl.ds(first, OCTET), :] for c in range(3)]
        inverse, switch, base, strength = geometry(listed, deltas)
        by_environ = [
            grad_environ[pl.ds(first * 4 + c, OCTET, stride=4), :] for c in range(4)
        ]
        along = (
            by_environ[1] * deltas[0] + by_environ[2] * deltas[1] + by_environ[3] * deltas[2]
        )
        by_strength = (
            grad_strength[pl.ds(first, OCTET), :] + by_environ[0] + along * inverse
        )
        filled = (listed >= 0).astype(F32)
        by_inverse = strength * along + filled * switch * switch * by_strength
        by_dist = (-2.0 / cutoff_sq) * base * by_strength - (
            0.5 * inverse * inverse * inverse
        ) * by_inverse
        scaled = strength * inverse
        centre = jnp.zeros((OCTET, LANES), F32)
        terms = []
        for c in range(3):
            term = by_environ[1 + c] * scaled + 2.0 * deltas[c] * by_dist
            terms.append(term)
            centre = jnp.where(lane == c, jnp.sum(term, axis=1, keepdims=True), centre)
        centre_terms[pl.ds(first, OCTET), :] = centre
        upper_digit = (listed // DIGIT).astype(F32)
        lower_digit = jnp.bitwise_and(listed, DIGIT - 1).astype(F32)
        spread, hits = [], []
        for a in range(OCTET):
            here = numbers == tall(upper_digit[a : a + 1])
            zero = jnp.zeros((DIGIT, LANES), BF16)
            spread.append(
                jnp.concatenate([jnp.where(here, tall(t[a : a + 1]), zero) for t in terms], axis=0)
            )
            hits.append(
                jnp.where(numbers == tall(lower_digit[a : a + 1]), jnp.ones_like(zero), zero)
            )
        return total + lax.dot_general(
            jnp.concatenate(spread, axis=1),
            jnp.concatenate(hits, axis=1),
            contract_last,
            preferred_element_type=F32,
        )

    total = run_octets(disperse, jnp.zeros((3 * DIGIT, DIGIT), F32))
    for c in range(3):
        for d in range(DIGIT):
            scattered[c : c + 1, d * DIGIT : (d + 1) * DIGIT] = total[
                c * DIGIT + d : c * DIGIT + d + 1, :
            ]
    total = scattered[0:OCTET, :]
    force = centre_terms[...].T[0:OCTET, :] - total[:, 0:atoms]
    beyond = -total[:, atoms:]
    out_ref[:, 0:atoms] = force
    out_ref[:, atoms:] = beyond
    if parcels_ref.shape[0] > 1:
        mine = live_ref[1]
        kick = step_size * jnp.where(own_ref[3:4, :] == 1.0, 1.0, 1.0 / heavy_mass)
        moving = [own_ref[c : c + 1, :] for c in range(3)] + [
            velocities_ref[c] + kick * force[c : c + 1] for c in range(3)
        ]
        moving = jnp.concatenate(moving + [jnp.zeros((OCTET - 6, atoms), F32)], axis=0)
        for s in range(2):
            tile = jnp.where(mine == s, moving, beyond)
            for b in range(parcels_ref.shape[0] // 2):
                parcels_ref[2 * b + s] = tile


def kick_kernel(part_ref, back_ref, rows_ref, types_ref, positions_ref, velocities_ref, forces_ref, out_ref):
    atoms = types_ref.shape[1]
    rows = turned_rows(rows_ref)
    hits = (
        lax.broadcasted_iota(jnp.int32, (atoms, rows.shape[1]), 0) == rows
    ).astype(F32)
    returned = lax.dot_general(
        back_ref[...],
        hits,
        (((1,), (1,)), ((), ())),
        preferred_element_type=F32,
        precision=lax.Precision.HIGHEST,
    )
    force = part_ref[:, 0:atoms] + returned
    inverse_mass = jnp.where(types_ref[...] == 1, 1.0, 1.0 / heavy_mass)
    rows = []
    for c in range(3):
        forces_ref[c] = force[c : c + 1]
        rows.append(positions_ref[c])
    for c in range(3):
        rows.append(velocities_ref[c] + step_size * inverse_mass * force[c : c + 1])
    tile = jnp.concatenate(rows + [jnp.zeros((2, atoms), F32)], axis=0)
    for b in range(out_ref.shape[0]):
        out_ref[b] = tile


def mix_kernel(place_ref, table_ref, gathered_ref, positions_ref, velocities_ref):
    mine = place_ref[0]
    count = gathered_ref.shape[0]
    tile_shape = gathered_ref.shape[1:]
    is_position = lax.broadcasted_iota(jnp.int32, tile_shape, 0) < 3
    turned = jnp.zeros(tile_shape, F32)
    crossed = jnp.zeros(tile_shape, F32)
    for b in range(count):
        tile = gathered_ref[b]
        turned = turned + table_ref[mine, b] * tile
        crossed = crossed + jnp.where(
            is_position, -table_ref[mine, 2 * count + b], table_ref[mine, count + b]
        ) * tile
    for c in range(3):
        positions_ref[c] = turned[c : c + 1] + crossed[3 + c : 4 + c]
        velocities_ref[c] = turned[3 + c : 4 + c] + crossed[c : c + 1]


def settle_kernel(
    place_ref, table_ref, part_ref, gathered_ref, rows_ref, types_ref, positions_ref, velocities_ref, forces_ref
):
    mine, slab = place_ref[0], place_ref[1]
    count = gathered_ref.shape[0] // 2
    tile_shape = gathered_ref.shape[1:]
    is_position = lax.broadcasted_iota(jnp.int32, tile_shape, 0) < 3
    zero = jnp.zeros(tile_shape, F32)
    turned, crossed, halo_turned, halo_travel = zero, zero, zero, zero
    for b in range(count):
        tile = gathered_ref[2 * b + slab]
        beyond = gathered_ref[2 * b + 1 - slab]
        cosine, travel = table_ref[mine, b], table_ref[mine, count + b]
        spring = table_ref[mine, 2 * count + b]
        turned = turned + cosine * tile
        crossed = crossed + jnp.where(is_position, -spring, travel) * tile
        halo_turned = halo_turned + cosine * beyond
        halo_travel = halo_travel + travel * beyond
    rows = turned_rows(rows_ref)
    atoms = types_ref.shape[1]
    hits = (lax.broadcasted_iota(jnp.int32, (atoms, rows.shape[1]), 0) == rows).astype(F32)
    own_beyond = gathered_ref[2 * mine + 1 - slab]
    returned = lax.dot_general(
        jnp.concatenate([halo_travel, halo_turned, own_beyond], axis=0),
        hits,
        (((1,), (1,)), ((), ())),
        preferred_element_type=F32,
        precision=lax.Precision.HIGHEST,
    )
    kick = step_size * jnp.where(types_ref[...] == 1, 1.0, 1.0 / heavy_mass)
    for c in range(3):
        positions_ref[c] = (
            turned[c : c + 1] + crossed[3 + c : 4 + c] + kick * returned[c : c + 1]
        )
        velocities_ref[c] = (
            turned[3 + c : 4 + c]
            + crossed[c : c + 1]
            + kick * returned[OCTET + c : OCTET + c + 1]
        )
        forces_ref[c] = part_ref[c : c + 1, 0:atoms] + returned[2 * OCTET + c : 2 * OCTET + c + 1]


VMEM_SPEC = pl.BlockSpec(memory_space=pltpu.VMEM)
SMEM_SPEC = pl.BlockSpec(memory_space=pltpu.SMEM)
SMALL = pltpu.CompilerParams(vmem_limit_bytes=SMALL_LIMIT)


def shape(*dims, dtype=F32):
    return jax.ShapeDtypeStruct(dims, dtype)


def call_force(live_atoms, own, halo, neighbours, weights, velocities, parcels=1):
    atoms, slots = neighbours.shape
    entries = atoms + halo.shape[1]
    e1 = weights[0].shape[1]
    e2 = weights[2].shape[1]
    e3 = weights[4].shape[1]
    rows_two = e2 // e1 * CHUNK
    rows_three = e3 // e1 * CHUNK
    assert entries <= DIGIT * DIGIT and slots == LANES and atoms == LANES and entries == 2 * LANES
    assert e3 == 2 * e2 and e2 == 2 * e1 and rows_three <= LANES and M2 <= e1
    groups = atoms // GROUP
    return pl.pallas_call(
        force_kernel,
        out_shape=(shape(OCTET, entries), shape(parcels, OCTET, atoms)),
        in_specs=[SMEM_SPEC] + [VMEM_SPEC] * (4 + len(weights)),
        out_specs=(VMEM_SPEC, VMEM_SPEC),
        scratch_shapes=[
            pltpu.VMEM((atoms, LANES), F32),
            pltpu.VMEM((LANES, LANES), F32),
            pltpu.VMEM((CHUNK, rows_two), BF16),
            pltpu.VMEM((rows_two, CHUNK), BF16),
            pltpu.VMEM((rows_two, rows_three), BF16),
            pltpu.VMEM((rows_three, rows_two), BF16),
            pltpu.VMEM((4, CHUNK, slots), F32),
            pltpu.VMEM((4 * atoms, slots), F32),
            pltpu.VMEM((3, atoms, slots), F32),
            pltpu.VMEM((atoms, slots), F32),
            pltpu.VMEM((groups, CHUNK, GROUP * slots), BF16),
            pltpu.VMEM((groups, rows_two, GROUP * slots), BF16),
            pltpu.VMEM((groups, rows_three, GROUP * slots), BF16),
            pltpu.VMEM((groups, rows_three, GROUP * slots), BF16),
            pltpu.VMEM((4 * atoms, rows_three), F32),
            pltpu.VMEM((4, rows_three, atoms), F32),
            pltpu.VMEM((e3 * M2, atoms), BF16),
            pltpu.VMEM((e3 * M2, atoms), F32),
            pltpu.VMEM(weights[6].shape[::-1], BF16),
            pltpu.VMEM((e3 * M2, 4 * atoms), BF16),
            pltpu.VMEM((4 * atoms, slots), F32),
            pltpu.VMEM((atoms, slots), F32),
            pltpu.VMEM((atoms, LANES), F32),
            pltpu.VMEM((OCTET, entries), F32),
        ],
        compiler_params=pltpu.CompilerParams(vmem_limit_bytes=VMEM_LIMIT),
        name="force",
    )(live_atoms, own, halo, neighbours, *weights, velocities)


def row(array):
    return array.reshape(1, -1)


def local(
    positions,
    velocities,
    atom_types,
    live_atoms,
    halo_rows,
    neighbours,
    type_scale,
    type_shift,
    embed_two,
    embed_bias_two,
    embed_three,
    embed_bias_three,
    fit_first,
    fit_bias_first,
    fit_second,
    fit_bias_second,
    fit_third,
    fit_bias_third,
    fit_readout,
):
    weights = (
        type_scale,
        type_shift,
        embed_two,
        row(embed_bias_two),
        embed_three,
        row(embed_bias_three),
        fit_first.T,
        row(fit_bias_first),
        fit_second,
        row(fit_bias_second),
        fit_third,
        row(fit_bias_third),
        fit_readout,
    )
    atoms = positions.shape[2]
    half = halo_rows.shape[1] // 2
    beads = lax.axis_size("bead")
    slabs = lax.axis_size("slab")
    to_next = [(i, (i + 1) % slabs) for i in range(slabs)]
    to_last = [((i + 1) % slabs, i) for i in range(slabs)]

    def exchange(outgoing, up, down):
        if slabs == 2:
            return lax.ppermute(outgoing, "slab", to_next)
        return jnp.concatenate(
            [
                lax.ppermute(outgoing[:, up], "slab", to_next),
                lax.ppermute(outgoing[:, down], "slab", to_last),
            ],
            axis=1,
        )

    low, high = slice(0, half), slice(half, 2 * half)
    types = row(atom_types)
    own, sent = pl.pallas_call(
        outgoing_kernel,
        out_shape=(shape(OCTET, atoms), shape(OCTET, 2 * half)),
        in_specs=[VMEM_SPEC] * 3,
        out_specs=(VMEM_SPEC, VMEM_SPEC),
        compiler_params=SMALL,
        name="outgoing",
    )(positions, types, halo_rows)
    halo = exchange(sent, low, high)
    place = jnp.stack([lax.axis_index("bead"), lax.axis_index("slab")]).astype(jnp.int32)
    scalars = jnp.concatenate([live_atoms, place[1:]])
    table = jnp.asarray(bead_tables(beads))
    sharded_shape = shape(*positions.shape)
    if slabs == 2:
        part, parcels = call_force(
            scalars, own, halo, neighbours, weights, velocities, beads * slabs
        )
        gathered = lax.all_to_all(
            parcels, ("bead", "slab"), split_axis=0, concat_axis=0, tiled=True
        )
        return pl.pallas_call(
            settle_kernel,
            out_shape=(sharded_shape,) * 3,
            in_specs=[SMEM_SPEC] * 2 + [VMEM_SPEC] * 4,
            out_specs=(VMEM_SPEC,) * 3,
            compiler_params=SMALL,
            name="settle",
        )(place, table, part, gathered, halo_rows, types)
    part, _ = call_force(scalars, own, halo, neighbours, weights, velocities)
    back = exchange(part[:, atoms:], high, low)
    back = jnp.concatenate([back[:, high], back[:, low]], axis=1)
    forces, kicked = pl.pallas_call(
        kick_kernel,
        out_shape=(sharded_shape, shape(beads, OCTET, atoms)),
        in_specs=[VMEM_SPEC] * 6,
        out_specs=(VMEM_SPEC, VMEM_SPEC),
        compiler_params=SMALL,
        name="kick",
    )(part, back, halo_rows, types, positions, velocities)
    gathered = lax.all_to_all(kicked, "bead", split_axis=0, concat_axis=0, tiled=True)
    positions_new, velocities_new = pl.pallas_call(
        mix_kernel,
        out_shape=(sharded_shape, sharded_shape),
        in_specs=[SMEM_SPEC, SMEM_SPEC, VMEM_SPEC],
        out_specs=(VMEM_SPEC, VMEM_SPEC),
        compiler_params=SMALL,
        name="mix",
    )(place, table, gathered)
    return positions_new, velocities_new, forces


def solution(mesh):
    sharded = P(None, "bead", "slab")
    return jax.shard_map(
        local,
        mesh=mesh,
        in_specs=(
            sharded,
            sharded,
            P("slab"),
            P("slab"),
            P("slab", None),
            P("slab", None),
        )
        + (P(),) * 13,
        out_specs=(sharded, sharded, sharded),
        check_vma=False,
    )
```

```python
import functools
import math

import jax
import jax.numpy as jnp
import numpy as np
from jax import lax
from jax.experimental import pallas as pl
from jax.experimental.pallas import tpu as pltpu
from jax.sharding import PartitionSpec as P

M2 = 16
step_size = 0.25
phase_rate = 1.2
cutoff_sq = 16.0
softening = 0.25
heavy_mass = 16.0

F32 = jnp.float32
BF16 = jnp.bfloat16
LANES = 128
OCTET = 8
UNROLL = 16
SKEW = 2
DIGIT = 16
GROUP = 2
CHUNK = 32
ONE_AT = 20.0
VMEM_LIMIT = 55168 * 1024
SMALL_LIMIT = 4 * 1024 * 1024


def bead_tables(count):
    index = np.arange(count)
    angles = 2.0 * np.pi * np.outer(index, index) / count
    norm = math.sqrt(2.0 / count)
    edge = 1.0 / math.sqrt(count)
    middle = count // 2
    basis = np.where(
        index[None, :] == 0,
        edge,
        np.where(
            index[None, :] < middle,
            norm * np.cos(angles),
            np.where(
                index[None, :] == middle, np.cos(np.pi * index)[:, None] * edge, norm * np.sin(angles)
            ),
        ),
    )
    sine = np.sin(np.pi * index / count)
    ratio = 2.0 * sine
    phases = phase_rate * count * sine
    travel = np.where(index == 0, 1.0, np.sin(phases) / np.where(index == 0, 1.0, ratio))

    def assemble(diagonal):
        return (basis * diagonal[None, :]) @ basis.T

    return np.concatenate(
        [assemble(np.cos(phases)), assemble(travel), assemble(ratio * np.sin(phases))], axis=1
    ).astype(np.float32)


def lookup(table, indices):
    return jnp.take_along_axis(table, indices, axis=1, mode="promise_in_bounds")


def turned_rows(rows_ref):
    rows = rows_ref[...]
    half = rows.shape[1] // 2
    return jnp.concatenate([rows[:, half:], rows[:, :half]], axis=1)


def outgoing_kernel(positions_ref, types_ref, rows_ref, own_ref, send_ref):
    hydrogen = (types_ref[...] == 1).astype(F32)
    atoms = hydrogen.shape[1]
    own = jnp.concatenate(
        [positions_ref[0], positions_ref[1], positions_ref[2], hydrogen]
        + [jnp.zeros((OCTET - 4, atoms), F32)],
        axis=0,
    )
    own_ref[...] = own
    send_ref[...] = lookup(own, jnp.broadcast_to(turned_rows(rows_ref), own.shape))


def force_kernel(
    live_ref,
    own_ref,
    halo_ref,
    listed_ref,
    scale_ref,
    shift_ref,
    two_ref,
    bias_two_ref,
    three_ref,
    bias_three_ref,
    first_hbm,
    fit_bias_first_hbm,
    second_hbm,
    fit_bias_second_hbm,
    third_hbm,
    fit_bias_third_hbm,
    readout_hbm,
    velocities_ref,
    out_ref,
    parcels_ref,
    own_t,
    padded,
    two_in,
    two_out,
    three_in,
    three_out,
    consts,
    environ,
    offset,
    around,
    kept_one,
    kept_two,
    kept_three,
    kept_sum,
    features,
    features_t,
    descriptor,
    grad_descriptor,
    first_rows,
    products,
    grad_environ,
    grad_strength,
    centre_terms,
    scattered,
    first_ref,
    fit_bias_first_ref,
    second_ref,
    fit_bias_second_ref,
    third_ref,
    fit_bias_third_ref,
    readout_ref,
    arrived,
):
    live = live_ref[0]
    octets = (live + (OCTET - 1)) // OCTET
    atoms, slots = listed_ref.shape
    e1 = scale_ref.shape[1]
    e2 = two_ref.shape[1]
    e3 = three_ref.shape[1]
    rows_one, rows_two, rows_three = two_in.shape[0], three_in.shape[0], three_out.shape[0]
    copies_two, copies_three = e2 // e1, e3 // e1

    late = [
        pltpu.make_async_copy(source, target, arrived.at[k])
        for k, (source, target) in enumerate(
            (
                (first_hbm, first_ref),
                (fit_bias_first_hbm, fit_bias_first_ref),
                (second_hbm, second_ref),
                (fit_bias_second_hbm, fit_bias_second_ref),
                (third_hbm, third_ref),
                (fit_bias_third_hbm, fit_bias_third_ref),
                (readout_hbm, readout_ref),
            )
        )
    ]
    for copy in late:
        copy.start()

    def split_bias(bias):
        high = bias.astype(BF16).astype(F32)
        return high, bias - high

    padded[...] = jnp.zeros_like(padded)
    bias_high, bias_low = split_bias(bias_two_ref[...])
    for k in range(copies_two):
        cols = slice(k * e1, (k + 1) * e1)
        padded[0:e1, k * CHUNK : k * CHUNK + e1] = two_ref[:, cols].astype(F32)
        padded[e1 : e1 + 1, k * CHUNK : k * CHUNK + e1] = bias_high[:, cols]
        padded[e1 + 1 : e1 + 2, k * CHUNK : k * CHUNK + e1] = bias_low[:, cols]
    table = padded[...]
    two_in[...] = table[:rows_one, :rows_two].astype(BF16)
    two_out[...] = table.T[:rows_two, :rows_one].astype(BF16)

    padded[...] = jnp.zeros_like(padded)
    bias_high, bias_low = split_bias(bias_three_ref[...])
    for k in range(copies_three):
        cols = slice(k * e1, (k + 1) * e1)
        for m in range(copies_two):
            padded[m * CHUNK : m * CHUNK + e1, k * CHUNK : k * CHUNK + e1] = three_ref[
                m * e1 : (m + 1) * e1, cols
            ].astype(F32)
        padded[e1 : e1 + 1, k * CHUNK : k * CHUNK + e1] = bias_high[:, cols]
        padded[e1 + 1 : e1 + 2, k * CHUNK : k * CHUNK + e1] = bias_low[:, cols]
    table = padded[...]
    three_in[...] = table[:rows_two, :rows_three].astype(BF16)
    three_out[...] = table.T[:rows_three, :rows_two].astype(BF16)

    padded[...] = jnp.zeros_like(padded)
    padded[0:2, 0:e1] = scale_ref[...]
    padded[2:4, 0:e1] = shift_ref[...]
    padded[2:3, e1 : e1 + 2] = jnp.full((1, 2), ONE_AT, F32)
    padded[3:4, e1 : e1 + 2] = jnp.full((1, 2), ONE_AT, F32)
    table = padded[...].T
    for k in range(4):
        column = table[:CHUNK, k : k + 1]
        if k % 2 == 1:
            column = column - table[:CHUNK, k - 1 : k]
        consts[k] = jnp.broadcast_to(column, (CHUNK, slots))

    padded[...] = jnp.zeros_like(padded)
    padded[0:OCTET, :] = own_ref[...]
    own_t[...] = padded[...].T

    features[...] = jnp.zeros_like(features)
    def gather_octet(first):
        listed = listed_ref[pl.ds(first, OCTET), :]
        low = jnp.bitwise_and(listed, LANES - 1)
        is_own = listed < atoms
        centre = own_t[pl.ds(first, OCTET), :]
        fetched = []
        for c in range(4):
            near = lookup(jnp.broadcast_to(own_ref[c : c + 1, :], (OCTET, LANES)), low)
            far = lookup(jnp.broadcast_to(halo_ref[c : c + 1, :], (OCTET, LANES)), low)
            fetched.append(jnp.where(is_own, near, far))
        deltas = [fetched[c] - centre[:, c : c + 1] for c in range(3)]
        return listed, deltas, fetched[3]

    def geometry(listed, deltas):
        filled = (listed >= 0).astype(F32)
        dist_sq = deltas[0] * deltas[0] + deltas[1] * deltas[1] + deltas[2] * deltas[2]
        inverse = lax.rsqrt(dist_sq + softening)
        switch = jnp.maximum(1.0 - dist_sq * (1.0 / cutoff_sq), 0.0)
        base = filled * switch * inverse
        return inverse, switch, base, base * switch

    def run_octets(step, carry=0):
        def body(turn, carry):
            for u in range(UNROLL):
                carry = step(turn * UNROLL + u, carry)
            return carry

        return lax.fori_loop(0, (octets + UNROLL - 1) // UNROLL, body, carry)

    def run_skewed(stages, skew):
        def body(turn, carry):
            waiting = [stages(turn * UNROLL + u) for u in range(UNROLL)]
            begun = 0
            active = []
            step = 0
            while begun < UNROLL or active:
                if begun < UNROLL and step % skew == 0:
                    active.append(waiting[begun])
                    begun += 1
                still = []
                for one in active:
                    try:
                        next(one)
                        still.append(one)
                    except StopIteration:
                        pass
                active = still
                step += 1
            return carry

        lax.fori_loop(0, (octets + UNROLL - 1) // UNROLL, body, 0)

    def surround(octet, carry):
        first = pl.multiple_of(octet * OCTET, OCTET)
        listed, deltas, hydrogen = gather_octet(first)
        inverse, _, _, strength = geometry(listed, deltas)
        around[pl.ds(first, OCTET), :] = hydrogen
        scaled = strength * inverse
        environ[pl.ds(first * 4, OCTET, stride=4), :] = strength
        for c in range(3):
            offset[c, pl.ds(first, OCTET), :] = deltas[c]
            environ[pl.ds(first * 4 + 1 + c, OCTET, stride=4), :] = scaled * deltas[c]
        return carry

    run_octets(surround)

    def forward(octet):
        first = pl.multiple_of(octet * OCTET, OCTET)
        hydrogen = around[pl.ds(first, OCTET), :]
        rows = pl.ds(pl.multiple_of(first * 4, OCTET * 4), OCTET * 4)
        groups = range(OCTET // GROUP)
        ones, twos, threes = [], [], []
        for g in groups:
            inputs = []
            for a in range(g * GROUP, (g + 1) * GROUP):
                line, kind = environ[pl.ds(first * 4 + 4 * a, 1), :], hydrogen[a : a + 1]
                inputs.append(
                    line * consts[0] + consts[2] + kind * (line * consts[1] + consts[3])
                )
            ones.append(jnp.tanh(jnp.concatenate(inputs, axis=1).astype(BF16)))
            yield
        for g in groups:
            kept_one[octet * len(groups) + g] = ones[g]
            two = jnp.tanh(
                jnp.dot(two_out[...], ones[g], preferred_element_type=F32).astype(BF16)
            )
            kept_two[octet * len(groups) + g] = two
            twos.append(two + jnp.concatenate([ones[g]] * copies_two, axis=0))
            yield
        by_slot = environ[rows, :].T.astype(BF16)
        column = lax.broadcasted_iota(jnp.int32, by_slot.shape, 1) // 4
        total = jnp.zeros((rows_three, OCTET * 4), F32)
        for g in groups:
            three = jnp.tanh(
                jnp.dot(three_out[...], twos[g], preferred_element_type=F32).astype(BF16)
            )
            kept_three[octet * len(groups) + g] = three
            sum_three = three + jnp.concatenate([twos[g]] * 2, axis=0)
            kept_sum[octet * len(groups) + g] = sum_three
            blocks = jnp.concatenate(
                [
                    jnp.where(column == a, by_slot, jnp.zeros_like(by_slot))
                    for a in range(g * GROUP, (g + 1) * GROUP)
                ],
                axis=0,
            )
            total = total + jnp.dot(sum_three, blocks, preferred_element_type=F32)
            yield
        features[rows, :] = total.T

    run_skewed(forward, SKEW)

    for copy in late:
        copy.wait()
    first_rows[...] = first_ref[...].T
    for c in range(4):
        features_t[c] = features[pl.ds(c, atoms, stride=4), :].T * (1.0 / slots)

    unit_rows = [q * CHUNK + r for q in range(copies_three) for r in range(e1)]
    leading = [features_t[c, 0:M2, :] for c in range(4)]
    for e, at in enumerate(unit_rows):
        total = None
        for c in range(4):
            term = features_t[c, at : at + 1, :] * leading[c]
            total = term if total is None else total + term
        descriptor[e * M2 : (e + 1) * M2, :] = total.astype(BF16)

    fit_one = jnp.tanh(
        jnp.dot(first_ref[...], descriptor[...], preferred_element_type=F32).T
        + fit_bias_first_ref[...]
    )
    tanh_two = jnp.tanh(
        jnp.dot(fit_one.astype(BF16), second_ref[...], preferred_element_type=F32)
        + fit_bias_second_ref[...]
    )
    fit_two = tanh_two + fit_one
    tanh_three = jnp.tanh(
        jnp.dot(fit_two.astype(BF16), third_ref[...], preferred_element_type=F32)
        + fit_bias_third_ref[...]
    )
    living = (lax.broadcasted_iota(jnp.int32, (atoms, 1), 0) < live).astype(F32)
    readout = readout_ref[0:1, :] + own_t[:, 3:4] * (readout_ref[1:2, :] - readout_ref[0:1, :])
    grad = living * readout
    contract_last = (((1,), (1,)), ((), ()))
    inner = (grad * (1.0 - tanh_three * tanh_three)).astype(BF16)
    grad = grad + lax.dot_general(inner, third_ref[...], contract_last, preferred_element_type=F32)
    inner = (grad * (1.0 - tanh_two * tanh_two)).astype(BF16)
    grad = grad + lax.dot_general(inner, second_ref[...], contract_last, preferred_element_type=F32)
    inner = (grad * (1.0 - fit_one * fit_one)).astype(BF16)
    grad_descriptor[...] = lax.dot_general(
        first_rows[...], inner, contract_last, preferred_element_type=F32
    )

    shared = [jnp.zeros((M2, atoms), F32) for _ in range(4)]
    short = [tile.astype(BF16) for tile in leading]
    for e, at in enumerate(unit_rows):
        rows = grad_descriptor[e * M2 : (e + 1) * M2, :]
        packed = rows.astype(BF16)
        for c in range(4):
            shared[c] = shared[c] + rows * features_t[c, at : at + 1, :]
            products[e * M2 : (e + 1) * M2, c * atoms : (c + 1) * atoms] = packed * short[c]
    unit = lax.broadcasted_iota(jnp.int32, (rows_three, e3 * M2), 0)
    unit = jnp.where(unit % CHUNK < e1, unit // CHUNK * e1 + unit % CHUNK, -1)
    gather = (lax.broadcasted_iota(jnp.int32, (rows_three, e3 * M2), 1) // M2 == unit).astype(F32)
    sums = jnp.dot(gather.astype(BF16), products[...], preferred_element_type=F32)
    for c in range(4):
        total = sums[:, c * atoms : (c + 1) * atoms] + jnp.concatenate(
            [shared[c], jnp.zeros((rows_three - M2, atoms), F32)], axis=0
        )
        features[pl.ds(c, atoms, stride=4), :] = (total * (1.0 / slots)).T

    scattered[...] = jnp.zeros_like(scattered)
    centre_terms[...] = jnp.zeros_like(centre_terms)
    lane = lax.broadcasted_iota(jnp.int32, (OCTET, LANES), 1)

    def backward(octet):
        first = pl.multiple_of(octet * OCTET, OCTET)
        grad_rows = features[pl.ds(pl.multiple_of(first * 4, OCTET * 4), OCTET * 4), :]
        grad_cols = grad_rows.T.astype(BF16)
        grad_rows = grad_rows.astype(BF16)
        groups = range(OCTET // GROUP)
        rows = pl.ds(pl.multiple_of(first * 4, OCTET * 4), OCTET * 4)
        quads = environ[rows, :]
        owner = lax.broadcasted_iota(jnp.int32, quads.shape, 0) // 4
        by_quad = jnp.zeros_like(quads)
        inners, grad_threes, grad_twos = [], [], []
        for g in groups:
            at = octet * len(groups) + g
            blocks = jnp.concatenate(
                [
                    jnp.where(owner == a, quads, 0.0).astype(BF16)
                    for a in range(g * GROUP, (g + 1) * GROUP)
                ],
                axis=1,
            )
            grad_three = jnp.dot(grad_cols, blocks, preferred_element_type=F32).astype(BF16)
            three = kept_three[at]
            inners.append(grad_three * (1.0 - three * three))
            grad_threes.append(grad_three[:rows_two] + grad_three[rows_two:])
            yield
        for g in groups:
            at = octet * len(groups) + g
            grad_two = (
                jnp.dot(three_in[...], inners[g], preferred_element_type=F32).astype(BF16)
                + grad_threes[g]
            )
            two = kept_two[at]
            inners[g] = grad_two * (1.0 - two * two)
            folded = grad_two[:CHUNK]
            for k in range(1, copies_two):
                folded = folded + grad_two[k * CHUNK : (k + 1) * CHUNK]
            grad_twos.append(folded)
            both = jnp.dot(grad_rows, kept_sum[at], preferred_element_type=F32)
            for k in range(GROUP):
                by_quad = jnp.where(
                    owner == g * GROUP + k, both[:, k * LANES : (k + 1) * LANES], by_quad
                )
            yield
        grad_environ[rows, :] = by_quad
        for g in groups:
            at = octet * len(groups) + g
            grad_one = jnp.dot(two_in[...], inners[g], preferred_element_type=F32) + grad_twos[g]
            one = kept_one[at].astype(F32)
            grad_one = grad_one * (1.0 - one * one)
            for k in range(GROUP):
                line = first + g * GROUP + k
                kind = around[pl.ds(line, 1), :]
                weighed = grad_one[:, k * LANES : (k + 1) * LANES] * (
                    consts[0] + kind * consts[1]
                )
                grad_strength[pl.ds(line, 1), :] = jnp.sum(weighed, axis=0, keepdims=True)


    run_skewed(backward, SKEW)

    numbers = lax.broadcasted_iota(jnp.int32, (DIGIT, LANES), 0).astype(F32).astype(BF16)

    def tall(line):
        return jnp.broadcast_to(line, (DIGIT, LANES)).astype(BF16)

    def disperse(octet, total):
        first = pl.multiple_of(octet * OCTET, OCTET)
        listed = listed_ref[pl.ds(first, OCTET), :]
        deltas = [offset[c, pl.ds(first, OCTET), :] for c in range(3)]
        inverse, switch, base, strength = geometry(listed, deltas)
        by_environ = [
            grad_environ[pl.ds(first * 4 + c, OCTET, stride=4), :] for c in range(4)
        ]
        along = (
            by_environ[1] * deltas[0] + by_environ[2] * deltas[1] + by_environ[3] * deltas[2]
        )
        by_strength = (
            grad_strength[pl.ds(first, OCTET), :] + by_environ[0] + along * inverse
        )
        filled = (listed >= 0).astype(F32)
        by_inverse = strength * along + filled * switch * switch * by_strength
        by_dist = (-2.0 / cutoff_sq) * base * by_strength - (
            0.5 * inverse * inverse * inverse
        ) * by_inverse
        scaled = strength * inverse
        centre = jnp.zeros((OCTET, LANES), F32)
        terms = []
        for c in range(3):
            term = by_environ[1 + c] * scaled + 2.0 * deltas[c] * by_dist
            terms.append(term)
            centre = jnp.where(lane == c, jnp.sum(term, axis=1, keepdims=True), centre)
        centre_terms[pl.ds(first, OCTET), :] = centre
        upper_digit = (listed // DIGIT).astype(F32)
        lower_digit = jnp.bitwise_and(listed, DIGIT - 1).astype(F32)
        spread, hits = [], []
        for a in range(OCTET):
            here = numbers == tall(upper_digit[a : a + 1])
            zero = jnp.zeros((DIGIT, LANES), BF16)
            spread.append(
                jnp.concatenate([jnp.where(here, tall(t[a : a + 1]), zero) for t in terms], axis=0)
            )
            hits.append(
                jnp.where(numbers == tall(lower_digit[a : a + 1]), jnp.ones_like(zero), zero)
            )
        return total + lax.dot_general(
            jnp.concatenate(spread, axis=1),
            jnp.concatenate(hits, axis=1),
            contract_last,
            preferred_element_type=F32,
        )

    total = run_octets(disperse, jnp.zeros((3 * DIGIT, DIGIT), F32))
    for c in range(3):
        for d in range(DIGIT):
            scattered[c : c + 1, d * DIGIT : (d + 1) * DIGIT] = total[
                c * DIGIT + d : c * DIGIT + d + 1, :
            ]
    total = scattered[0:OCTET, :]
    force = centre_terms[...].T[0:OCTET, :] - total[:, 0:atoms]
    beyond = -total[:, atoms:]
    out_ref[:, 0:atoms] = force
    out_ref[:, atoms:] = beyond
    if parcels_ref.shape[0] > 1:
        mine = live_ref[1]
        kick = step_size * jnp.where(own_ref[3:4, :] == 1.0, 1.0, 1.0 / heavy_mass)
        moving = [own_ref[c : c + 1, :] for c in range(3)] + [
            velocities_ref[c] + kick * force[c : c + 1] for c in range(3)
        ]
        moving = jnp.concatenate(moving + [jnp.zeros((OCTET - 6, atoms), F32)], axis=0)
        for s in range(2):
            tile = jnp.where(mine == s, moving, beyond)
            for b in range(parcels_ref.shape[0] // 2):
                parcels_ref[2 * b + s] = tile


def kick_kernel(part_ref, back_ref, rows_ref, types_ref, positions_ref, velocities_ref, forces_ref, out_ref):
    atoms = types_ref.shape[1]
    rows = turned_rows(rows_ref)
    hits = (
        lax.broadcasted_iota(jnp.int32, (atoms, rows.shape[1]), 0) == rows
    ).astype(F32)
    returned = lax.dot_general(
        back_ref[...],
        hits,
        (((1,), (1,)), ((), ())),
        preferred_element_type=F32,
        precision=lax.Precision.HIGHEST,
    )
    force = part_ref[:, 0:atoms] + returned
    inverse_mass = jnp.where(types_ref[...] == 1, 1.0, 1.0 / heavy_mass)
    rows = []
    for c in range(3):
        forces_ref[c] = force[c : c + 1]
        rows.append(positions_ref[c])
    for c in range(3):
        rows.append(velocities_ref[c] + step_size * inverse_mass * force[c : c + 1])
    tile = jnp.concatenate(rows + [jnp.zeros((2, atoms), F32)], axis=0)
    for b in range(out_ref.shape[0]):
        out_ref[b] = tile


def mix_kernel(place_ref, table_ref, gathered_ref, positions_ref, velocities_ref):
    mine = place_ref[0]
    count = gathered_ref.shape[0]
    tile_shape = gathered_ref.shape[1:]
    is_position = lax.broadcasted_iota(jnp.int32, tile_shape, 0) < 3
    turned = jnp.zeros(tile_shape, F32)
    crossed = jnp.zeros(tile_shape, F32)
    for b in range(count):
        tile = gathered_ref[b]
        turned = turned + table_ref[mine, b] * tile
        crossed = crossed + jnp.where(
            is_position, -table_ref[mine, 2 * count + b], table_ref[mine, count + b]
        ) * tile
    for c in range(3):
        positions_ref[c] = turned[c : c + 1] + crossed[3 + c : 4 + c]
        velocities_ref[c] = turned[3 + c : 4 + c] + crossed[c : c + 1]


def settle_kernel(
    place_ref, table_ref, part_ref, gathered_ref, rows_ref, types_ref, positions_ref, velocities_ref, forces_ref
):
    mine, slab = place_ref[0], place_ref[1]
    count = gathered_ref.shape[0] // 2
    tile_shape = gathered_ref.shape[1:]
    is_position = lax.broadcasted_iota(jnp.int32, tile_shape, 0) < 3
    zero = jnp.zeros(tile_shape, F32)
    turned, crossed, halo_turned, halo_travel = zero, zero, zero, zero
    for b in range(count):
        tile = gathered_ref[2 * b + slab]
        beyond = gathered_ref[2 * b + 1 - slab]
        cosine, travel = table_ref[mine, b], table_ref[mine, count + b]
        spring = table_ref[mine, 2 * count + b]
        turned = turned + cosine * tile
        crossed = crossed + jnp.where(is_position, -spring, travel) * tile
        halo_turned = halo_turned + cosine * beyond
        halo_travel = halo_travel + travel * beyond
    rows = turned_rows(rows_ref)
    atoms = types_ref.shape[1]
    hits = (lax.broadcasted_iota(jnp.int32, (atoms, rows.shape[1]), 0) == rows).astype(F32)
    own_beyond = gathered_ref[2 * mine + 1 - slab]
    returned = lax.dot_general(
        jnp.concatenate([halo_travel, halo_turned, own_beyond], axis=0),
        hits,
        (((1,), (1,)), ((), ())),
        preferred_element_type=F32,
        precision=lax.Precision.HIGHEST,
    )
    kick = step_size * jnp.where(types_ref[...] == 1, 1.0, 1.0 / heavy_mass)
    for c in range(3):
        positions_ref[c] = (
            turned[c : c + 1] + crossed[3 + c : 4 + c] + kick * returned[c : c + 1]
        )
        velocities_ref[c] = (
            turned[3 + c : 4 + c]
            + crossed[c : c + 1]
            + kick * returned[OCTET + c : OCTET + c + 1]
        )
        forces_ref[c] = part_ref[c : c + 1, 0:atoms] + returned[2 * OCTET + c : 2 * OCTET + c + 1]


VMEM_SPEC = pl.BlockSpec(memory_space=pltpu.VMEM)
HBM_SPEC = pl.BlockSpec(memory_space=pltpu.HBM)
SMEM_SPEC = pl.BlockSpec(memory_space=pltpu.SMEM)
SMALL = pltpu.CompilerParams(vmem_limit_bytes=SMALL_LIMIT)


def shape(*dims, dtype=F32):
    return jax.ShapeDtypeStruct(dims, dtype)


def call_force(live_atoms, own, halo, neighbours, weights, velocities, parcels=1):
    atoms, slots = neighbours.shape
    entries = atoms + halo.shape[1]
    e1 = weights[0].shape[1]
    e2 = weights[2].shape[1]
    e3 = weights[4].shape[1]
    rows_two = e2 // e1 * CHUNK
    rows_three = e3 // e1 * CHUNK
    assert entries <= DIGIT * DIGIT and slots == LANES and atoms == LANES and entries == 2 * LANES
    assert e3 == 2 * e2 and e2 == 2 * e1 and rows_three <= LANES and M2 <= e1
    groups = atoms // GROUP
    return pl.pallas_call(
        force_kernel,
        out_shape=(shape(OCTET, entries), shape(parcels, OCTET, atoms)),
        in_specs=[SMEM_SPEC]
        + [VMEM_SPEC] * 9
        + [HBM_SPEC] * (len(weights) - 6)
        + [VMEM_SPEC],
        out_specs=(VMEM_SPEC, VMEM_SPEC),
        scratch_shapes=[
            pltpu.VMEM((atoms, LANES), F32),
            pltpu.VMEM((LANES, LANES), F32),
            pltpu.VMEM((CHUNK, rows_two), BF16),
            pltpu.VMEM((rows_two, CHUNK), BF16),
            pltpu.VMEM((rows_two, rows_three), BF16),
            pltpu.VMEM((rows_three, rows_two), BF16),
            pltpu.VMEM((4, CHUNK, slots), F32),
            pltpu.VMEM((4 * atoms, slots), F32),
            pltpu.VMEM((3, atoms, slots), F32),
            pltpu.VMEM((atoms, slots), F32),
            pltpu.VMEM((groups, CHUNK, GROUP * slots), BF16),
            pltpu.VMEM((groups, rows_two, GROUP * slots), BF16),
            pltpu.VMEM((groups, rows_three, GROUP * slots), BF16),
            pltpu.VMEM((groups, rows_three, GROUP * slots), BF16),
            pltpu.VMEM((4 * atoms, rows_three), F32),
            pltpu.VMEM((4, rows_three, atoms), F32),
            pltpu.VMEM((e3 * M2, atoms), BF16),
            pltpu.VMEM((e3 * M2, atoms), F32),
            pltpu.VMEM(weights[6].shape[::-1], BF16),
            pltpu.VMEM((e3 * M2, 4 * atoms), BF16),
            pltpu.VMEM((4 * atoms, slots), F32),
            pltpu.VMEM((atoms, slots), F32),
            pltpu.VMEM((atoms, LANES), F32),
            pltpu.VMEM((OCTET, entries), F32),
        ]
        + [pltpu.VMEM(w.shape, w.dtype) for w in weights[6:]]
        + [pltpu.SemaphoreType.DMA((len(weights) - 6,))],
        compiler_params=pltpu.CompilerParams(vmem_limit_bytes=VMEM_LIMIT),
        name="force",
    )(live_atoms, own, halo, neighbours, *weights, velocities)


def row(array):
    return array.reshape(1, -1)


def local(
    positions,
    velocities,
    atom_types,
    live_atoms,
    halo_rows,
    neighbours,
    type_scale,
    type_shift,
    embed_two,
    embed_bias_two,
    embed_three,
    embed_bias_three,
    fit_first,
    fit_bias_first,
    fit_second,
    fit_bias_second,
    fit_third,
    fit_bias_third,
    fit_readout,
):
    weights = (
        type_scale,
        type_shift,
        embed_two,
        row(embed_bias_two),
        embed_three,
        row(embed_bias_three),
        fit_first.T,
        row(fit_bias_first),
        fit_second,
        row(fit_bias_second),
        fit_third,
        row(fit_bias_third),
        fit_readout,
    )
    atoms = positions.shape[2]
    half = halo_rows.shape[1] // 2
    beads = lax.axis_size("bead")
    slabs = lax.axis_size("slab")
    to_next = [(i, (i + 1) % slabs) for i in range(slabs)]
    to_last = [((i + 1) % slabs, i) for i in range(slabs)]

    def exchange(outgoing, up, down):
        if slabs == 2:
            return lax.ppermute(outgoing, "slab", to_next)
        return jnp.concatenate(
            [
                lax.ppermute(outgoing[:, up], "slab", to_next),
                lax.ppermute(outgoing[:, down], "slab", to_last),
            ],
            axis=1,
        )

    low, high = slice(0, half), slice(half, 2 * half)
    types = row(atom_types)
    own, sent = pl.pallas_call(
        outgoing_kernel,
        out_shape=(shape(OCTET, atoms), shape(OCTET, 2 * half)),
        in_specs=[VMEM_SPEC] * 3,
        out_specs=(VMEM_SPEC, VMEM_SPEC),
        compiler_params=SMALL,
        name="outgoing",
    )(positions, types, halo_rows)
    halo = exchange(sent, low, high)
    place = jnp.stack([lax.axis_index("bead"), lax.axis_index("slab")]).astype(jnp.int32)
    scalars = jnp.concatenate([live_atoms, place[1:]])
    table = jnp.asarray(bead_tables(beads))
    sharded_shape = shape(*positions.shape)
    if slabs == 2:
        part, parcels = call_force(
            scalars, own, halo, neighbours, weights, velocities, beads * slabs
        )
        gathered = lax.all_to_all(
            parcels, ("bead", "slab"), split_axis=0, concat_axis=0, tiled=True
        )
        return pl.pallas_call(
            settle_kernel,
            out_shape=(sharded_shape,) * 3,
            in_specs=[SMEM_SPEC] * 2 + [VMEM_SPEC] * 4,
            out_specs=(VMEM_SPEC,) * 3,
            compiler_params=SMALL,
            name="settle",
        )(place, table, part, gathered, halo_rows, types)
    part, _ = call_force(scalars, own, halo, neighbours, weights, velocities)
    back = exchange(part[:, atoms:], high, low)
    back = jnp.concatenate([back[:, high], back[:, low]], axis=1)
    forces, kicked = pl.pallas_call(
        kick_kernel,
        out_shape=(sharded_shape, shape(beads, OCTET, atoms)),
        in_specs=[VMEM_SPEC] * 6,
        out_specs=(VMEM_SPEC, VMEM_SPEC),
        compiler_params=SMALL,
        name="kick",
    )(part, back, halo_rows, types, positions, velocities)
    gathered = lax.all_to_all(kicked, "bead", split_axis=0, concat_axis=0, tiled=True)
    positions_new, velocities_new = pl.pallas_call(
        mix_kernel,
        out_shape=(sharded_shape, sharded_shape),
        in_specs=[SMEM_SPEC, SMEM_SPEC, VMEM_SPEC],
        out_specs=(VMEM_SPEC, VMEM_SPEC),
        compiler_params=SMALL,
        name="mix",
    )(place, table, gathered)
    return positions_new, velocities_new, forces


def solution(mesh):
    sharded = P(None, "bead", "slab")
    return jax.shard_map(
        local,
        mesh=mesh,
        in_specs=(
            sharded,
            sharded,
            P("slab"),
            P("slab"),
            P("slab", None),
            P("slab", None),
        )
        + (P(),) * 13,
        out_specs=(sharded, sharded, sharded),
        check_vma=False,
    )
```

```python
import functools
import math

import jax
import jax.numpy as jnp
import numpy as np
from jax import lax
from jax.experimental import pallas as pl
from jax.experimental.pallas import tpu as pltpu
from jax.sharding import PartitionSpec as P

M2 = 16
step_size = 0.25
phase_rate = 1.2
cutoff_sq = 16.0
softening = 0.25
heavy_mass = 16.0

F32 = jnp.float32
BF16 = jnp.bfloat16
LANES = 128
OCTET = 8
UNROLL = 16
DIGIT = 16
GROUP = 2
CHUNK = 32
ONE_AT = 20.0
VMEM_LIMIT = 55168 * 1024
SMALL_LIMIT = 4 * 1024 * 1024


def bead_tables(count):
    index = np.arange(count)
    angles = 2.0 * np.pi * np.outer(index, index) / count
    norm = math.sqrt(2.0 / count)
    edge = 1.0 / math.sqrt(count)
    middle = count // 2
    basis = np.where(
        index[None, :] == 0,
        edge,
        np.where(
            index[None, :] < middle,
            norm * np.cos(angles),
            np.where(
                index[None, :] == middle, np.cos(np.pi * index)[:, None] * edge, norm * np.sin(angles)
            ),
        ),
    )
    sine = np.sin(np.pi * index / count)
    ratio = 2.0 * sine
    phases = phase_rate * count * sine
    travel = np.where(index == 0, 1.0, np.sin(phases) / np.where(index == 0, 1.0, ratio))

    def assemble(diagonal):
        return (basis * diagonal[None, :]) @ basis.T

    return np.concatenate(
        [assemble(np.cos(phases)), assemble(travel), assemble(ratio * np.sin(phases))], axis=1
    ).astype(np.float32)


def lookup(table, indices):
    return jnp.take_along_axis(table, indices, axis=1, mode="promise_in_bounds")


def turned_rows(rows_ref):
    rows = rows_ref[...]
    half = rows.shape[1] // 2
    return jnp.concatenate([rows[:, half:], rows[:, :half]], axis=1)


def outgoing_kernel(positions_ref, types_ref, rows_ref, own_ref, send_ref):
    hydrogen = (types_ref[...] == 1).astype(F32)
    atoms = hydrogen.shape[1]
    own = jnp.concatenate(
        [positions_ref[0], positions_ref[1], positions_ref[2], hydrogen]
        + [jnp.zeros((OCTET - 4, atoms), F32)],
        axis=0,
    )
    own_ref[...] = own
    send_ref[...] = lookup(own, jnp.broadcast_to(turned_rows(rows_ref), own.shape))


def force_kernel(
    live_ref,
    own_ref,
    halo_ref,
    listed_ref,
    scale_ref,
    shift_ref,
    two_ref,
    bias_two_ref,
    three_ref,
    bias_three_ref,
    first_hbm,
    fit_bias_first_hbm,
    second_hbm,
    fit_bias_second_hbm,
    third_hbm,
    fit_bias_third_hbm,
    readout_hbm,
    velocities_ref,
    out_ref,
    parcels_ref,
    own_t,
    padded,
    two_in,
    two_out,
    three_in,
    three_out,
    consts,
    environ,
    offset,
    around,
    kept_one,
    kept_two,
    kept_three,
    kept_sum,
    features,
    features_t,
    descriptor,
    grad_descriptor,
    first_rows,
    products,
    grad_environ,
    grad_strength,
    centre_terms,
    scattered,
    first_ref,
    fit_bias_first_ref,
    second_ref,
    fit_bias_second_ref,
    third_ref,
    fit_bias_third_ref,
    readout_ref,
    arrived,
):
    live = live_ref[0]
    octets = (live + (OCTET - 1)) // OCTET
    atoms, slots = listed_ref.shape
    e1 = scale_ref.shape[1]
    e2 = two_ref.shape[1]
    e3 = three_ref.shape[1]
    rows_one, rows_two, rows_three = two_in.shape[0], three_in.shape[0], three_out.shape[0]
    copies_two, copies_three = e2 // e1, e3 // e1

    late = [
        pltpu.make_async_copy(source, target, arrived.at[k])
        for k, (source, target) in enumerate(
            (
                (first_hbm, first_ref),
                (fit_bias_first_hbm, fit_bias_first_ref),
                (second_hbm, second_ref),
                (fit_bias_second_hbm, fit_bias_second_ref),
                (third_hbm, third_ref),
                (fit_bias_third_hbm, fit_bias_third_ref),
                (readout_hbm, readout_ref),
            )
        )
    ]
    for copy in late:
        copy.start()

    def split_bias(bias):
        high = bias.astype(BF16).astype(F32)
        return high, bias - high

    padded[...] = jnp.zeros_like(padded)
    bias_high, bias_low = split_bias(bias_two_ref[...])
    for k in range(copies_two):
        cols = slice(k * e1, (k + 1) * e1)
        padded[0:e1, k * CHUNK : k * CHUNK + e1] = two_ref[:, cols].astype(F32)
        padded[e1 : e1 + 1, k * CHUNK : k * CHUNK + e1] = bias_high[:, cols]
        padded[e1 + 1 : e1 + 2, k * CHUNK : k * CHUNK + e1] = bias_low[:, cols]
    table = padded[...]
    two_in[...] = table[:rows_one, :rows_two].astype(BF16)
    two_out[...] = table.T[:rows_two, :rows_one].astype(BF16)

    padded[...] = jnp.zeros_like(padded)
    bias_high, bias_low = split_bias(bias_three_ref[...])
    for k in range(copies_three):
        cols = slice(k * e1, (k + 1) * e1)
        for m in range(copies_two):
            padded[m * CHUNK : m * CHUNK + e1, k * CHUNK : k * CHUNK + e1] = three_ref[
                m * e1 : (m + 1) * e1, cols
            ].astype(F32)
        padded[e1 : e1 + 1, k * CHUNK : k * CHUNK + e1] = bias_high[:, cols]
        padded[e1 + 1 : e1 + 2, k * CHUNK : k * CHUNK + e1] = bias_low[:, cols]
    table = padded[...]
    three_in[...] = table[:rows_two, :rows_three].astype(BF16)
    three_out[...] = table.T[:rows_three, :rows_two].astype(BF16)

    padded[...] = jnp.zeros_like(padded)
    padded[0:2, 0:e1] = scale_ref[...]
    padded[2:4, 0:e1] = shift_ref[...]
    padded[2:3, e1 : e1 + 2] = jnp.full((1, 2), ONE_AT, F32)
    padded[3:4, e1 : e1 + 2] = jnp.full((1, 2), ONE_AT, F32)
    table = padded[...].T
    for k in range(4):
        column = table[:CHUNK, k : k + 1]
        if k % 2 == 1:
            column = column - table[:CHUNK, k - 1 : k]
        consts[k] = jnp.broadcast_to(column, (CHUNK, slots))

    padded[...] = jnp.zeros_like(padded)
    padded[0:OCTET, :] = own_ref[...]
    own_t[...] = padded[...].T

    features[...] = jnp.zeros_like(features)
    def gather_octet(first):
        listed = listed_ref[pl.ds(first, OCTET), :]
        low = jnp.bitwise_and(listed, LANES - 1)
        is_own = listed < atoms
        centre = own_t[pl.ds(first, OCTET), :]
        fetched = []
        for c in range(4):
            near = lookup(jnp.broadcast_to(own_ref[c : c + 1, :], (OCTET, LANES)), low)
            far = lookup(jnp.broadcast_to(halo_ref[c : c + 1, :], (OCTET, LANES)), low)
            fetched.append(jnp.where(is_own, near, far))
        deltas = [fetched[c] - centre[:, c : c + 1] for c in range(3)]
        return listed, deltas, fetched[3]

    def geometry(listed, deltas):
        filled = (listed >= 0).astype(F32)
        dist_sq = deltas[0] * deltas[0] + deltas[1] * deltas[1] + deltas[2] * deltas[2]
        inverse = lax.rsqrt(dist_sq + softening)
        switch = jnp.maximum(1.0 - dist_sq * (1.0 / cutoff_sq), 0.0)
        base = filled * switch * inverse
        return inverse, switch, base, base * switch

    def run_octets(step, carry=0):
        def body(turn, carry):
            for u in range(UNROLL):
                carry = step(turn * UNROLL + u, carry)
            return carry

        return lax.fori_loop(0, (octets + UNROLL - 1) // UNROLL, body, carry)

    def run_skewed(stages, skew):
        def body(turn, carry):
            waiting = [stages(turn * UNROLL + u) for u in range(UNROLL)]
            begun = 0
            active = []
            step = 0
            while begun < UNROLL or active:
                if begun < UNROLL and step % skew == 0:
                    active.append(waiting[begun])
                    begun += 1
                still = []
                for one in active:
                    try:
                        next(one)
                        still.append(one)
                    except StopIteration:
                        pass
                active = still
                step += 1
            return carry

        lax.fori_loop(0, (octets + UNROLL - 1) // UNROLL, body, 0)

    def surround(octet, carry):
        first = pl.multiple_of(octet * OCTET, OCTET)
        listed, deltas, hydrogen = gather_octet(first)
        inverse, _, _, strength = geometry(listed, deltas)
        around[pl.ds(first, OCTET), :] = hydrogen
        scaled = strength * inverse
        environ[pl.ds(first * 4, OCTET, stride=4), :] = strength
        for c in range(3):
            offset[c, pl.ds(first, OCTET), :] = deltas[c]
            environ[pl.ds(first * 4 + 1 + c, OCTET, stride=4), :] = scaled * deltas[c]
        return carry

    run_octets(surround)

    def forward(octet):
        first = pl.multiple_of(octet * OCTET, OCTET)
        hydrogen = around[pl.ds(first, OCTET), :]
        rows = pl.ds(pl.multiple_of(first * 4, OCTET * 4), OCTET * 4)
        groups = range(OCTET // GROUP)
        ones, twos, threes = [], [], []
        for g in groups:
            inputs = []
            for a in range(g * GROUP, (g + 1) * GROUP):
                line, kind = environ[pl.ds(first * 4 + 4 * a, 1), :], hydrogen[a : a + 1]
                inputs.append(
                    line * consts[0] + consts[2] + kind * (line * consts[1] + consts[3])
                )
            ones.append(jnp.tanh(jnp.concatenate(inputs, axis=1).astype(BF16)))
            yield
        for g in groups:
            kept_one[octet * len(groups) + g] = ones[g]
            two = jnp.tanh(
                jnp.dot(two_out[...], ones[g], preferred_element_type=F32).astype(BF16)
            )
            kept_two[octet * len(groups) + g] = two
            twos.append(two + jnp.concatenate([ones[g]] * copies_two, axis=0))
            yield
        by_slot = environ[rows, :].T.astype(BF16)
        column = lax.broadcasted_iota(jnp.int32, by_slot.shape, 1) // 4
        total = jnp.zeros((rows_three, OCTET * 4), F32)
        for g in groups:
            three = jnp.tanh(
                jnp.dot(three_out[...], twos[g], preferred_element_type=F32).astype(BF16)
            )
            kept_three[octet * len(groups) + g] = three
            sum_three = three + jnp.concatenate([twos[g]] * 2, axis=0)
            kept_sum[octet * len(groups) + g] = sum_three
            blocks = jnp.concatenate(
                [
                    jnp.where(column == a, by_slot, jnp.zeros_like(by_slot))
                    for a in range(g * GROUP, (g + 1) * GROUP)
                ],
                axis=0,
            )
            total = total + jnp.dot(sum_three, blocks, preferred_element_type=F32)
            yield
        features[rows, :] = total.T

    run_skewed(forward, 2)

    for copy in late:
        copy.wait()
    first_rows[...] = first_ref[...].T
    for c in range(4):
        features_t[c] = features[pl.ds(c, atoms, stride=4), :].T * (1.0 / slots)

    unit_rows = [q * CHUNK + r for q in range(copies_three) for r in range(e1)]
    leading = [features_t[c, 0:M2, :] for c in range(4)]
    for e, at in enumerate(unit_rows):
        total = None
        for c in range(4):
            term = features_t[c, at : at + 1, :] * leading[c]
            total = term if total is None else total + term
        descriptor[e * M2 : (e + 1) * M2, :] = total.astype(BF16)

    fit_one = jnp.tanh(
        jnp.dot(first_ref[...], descriptor[...], preferred_element_type=F32).T
        + fit_bias_first_ref[...]
    )
    tanh_two = jnp.tanh(
        jnp.dot(fit_one.astype(BF16), second_ref[...], preferred_element_type=F32)
        + fit_bias_second_ref[...]
    )
    fit_two = tanh_two + fit_one
    tanh_three = jnp.tanh(
        jnp.dot(fit_two.astype(BF16), third_ref[...], preferred_element_type=F32)
        + fit_bias_third_ref[...]
    )
    living = (lax.broadcasted_iota(jnp.int32, (atoms, 1), 0) < live).astype(F32)
    readout = readout_ref[0:1, :] + own_t[:, 3:4] * (readout_ref[1:2, :] - readout_ref[0:1, :])
    grad = living * readout
    contract_last = (((1,), (1,)), ((), ()))
    inner = (grad * (1.0 - tanh_three * tanh_three)).astype(BF16)
    grad = grad + lax.dot_general(inner, third_ref[...], contract_last, preferred_element_type=F32)
    inner = (grad * (1.0 - tanh_two * tanh_two)).astype(BF16)
    grad = grad + lax.dot_general(inner, second_ref[...], contract_last, preferred_element_type=F32)
    inner = (grad * (1.0 - fit_one * fit_one)).astype(BF16)
    grad_descriptor[...] = lax.dot_general(
        first_rows[...], inner, contract_last, preferred_element_type=F32
    )

    shared = [jnp.zeros((M2, atoms), F32) for _ in range(4)]
    short = [tile.astype(BF16) for tile in leading]
    for e, at in enumerate(unit_rows):
        rows = grad_descriptor[e * M2 : (e + 1) * M2, :]
        packed = rows.astype(BF16)
        for c in range(4):
            shared[c] = shared[c] + rows * features_t[c, at : at + 1, :]
            products[e * M2 : (e + 1) * M2, c * atoms : (c + 1) * atoms] = packed * short[c]
    unit = lax.broadcasted_iota(jnp.int32, (rows_three, 1), 0)
    unit = jnp.where(unit % CHUNK < e1, unit // CHUNK * e1 + unit % CHUNK, -1)
    gather = (lax.broadcasted_iota(jnp.int32, (1, e3 * M2), 1) // M2 == unit).astype(F32)
    sums = jnp.dot(gather.astype(BF16), products[...], preferred_element_type=F32)
    for c in range(4):
        total = sums[:, c * atoms : (c + 1) * atoms] + jnp.concatenate(
            [shared[c], jnp.zeros((rows_three - M2, atoms), F32)], axis=0
        )
        features[pl.ds(c, atoms, stride=4), :] = (total * (1.0 / slots)).T

    scattered[...] = jnp.zeros_like(scattered)
    centre_terms[...] = jnp.zeros_like(centre_terms)
    lane = lax.broadcasted_iota(jnp.int32, (OCTET, LANES), 1)

    def backward(octet):
        first = pl.multiple_of(octet * OCTET, OCTET)
        grad_rows = features[pl.ds(pl.multiple_of(first * 4, OCTET * 4), OCTET * 4), :]
        grad_cols = grad_rows.T.astype(BF16)
        grad_rows = grad_rows.astype(BF16)
        groups = range(OCTET // GROUP)
        rows = pl.ds(pl.multiple_of(first * 4, OCTET * 4), OCTET * 4)
        quads = environ[rows, :]
        owner = lax.broadcasted_iota(jnp.int32, quads.shape, 0) // 4
        by_quad = jnp.zeros_like(quads)
        inners, grad_threes, grad_twos = [], [], []
        for g in groups:
            at = octet * len(groups) + g
            blocks = jnp.concatenate(
                [
                    jnp.where(owner == a, quads, 0.0).astype(BF16)
                    for a in range(g * GROUP, (g + 1) * GROUP)
                ],
                axis=1,
            )
            grad_three = jnp.dot(grad_cols, blocks, preferred_element_type=F32).astype(BF16)
            three = kept_three[at]
            inners.append(grad_three * (1.0 - three * three))
            grad_threes.append(grad_three[:rows_two] + grad_three[rows_two:])
            yield
        for g in groups:
            at = octet * len(groups) + g
            grad_two = (
                jnp.dot(three_in[...], inners[g], preferred_element_type=F32).astype(BF16)
                + grad_threes[g]
            )
            two = kept_two[at]
            inners[g] = grad_two * (1.0 - two * two)
            folded = grad_two[:CHUNK]
            for k in range(1, copies_two):
                folded = folded + grad_two[k * CHUNK : (k + 1) * CHUNK]
            grad_twos.append(folded)
            both = jnp.dot(grad_rows, kept_sum[at], preferred_element_type=F32)
            for k in range(GROUP):
                by_quad = jnp.where(
                    owner == g * GROUP + k, both[:, k * LANES : (k + 1) * LANES], by_quad
                )
            yield
        grad_environ[rows, :] = by_quad
        for g in groups:
            at = octet * len(groups) + g
            grad_one = jnp.dot(two_in[...], inners[g], preferred_element_type=F32) + grad_twos[g]
            one = kept_one[at].astype(F32)
            grad_one = grad_one * (1.0 - one * one)
            for k in range(GROUP):
                line = first + g * GROUP + k
                kind = around[pl.ds(line, 1), :]
                weighed = grad_one[:, k * LANES : (k + 1) * LANES] * (
                    consts[0] + kind * consts[1]
                )
                grad_strength[pl.ds(line, 1), :] = jnp.sum(weighed, axis=0, keepdims=True)


    run_skewed(backward, 1)

    numbers = lax.broadcasted_iota(jnp.int32, (DIGIT, LANES), 0).astype(F32).astype(BF16)

    def tall(line):
        return jnp.broadcast_to(line, (DIGIT, LANES)).astype(BF16)

    def disperse(octet, total):
        first = pl.multiple_of(octet * OCTET, OCTET)
        listed = listed_ref[pl.ds(first, OCTET), :]
        deltas = [offset[c, pl.ds(first, OCTET), :] for c in range(3)]
        inverse, switch, base, strength = geometry(listed, deltas)
        by_environ = [
            grad_environ[pl.ds(first * 4 + c, OCTET, stride=4), :] for c in range(4)
        ]
        along = (
            by_environ[1] * deltas[0] + by_environ[2] * deltas[1] + by_environ[3] * deltas[2]
        )
        by_strength = (
            grad_strength[pl.ds(first, OCTET), :] + by_environ[0] + along * inverse
        )
        filled = (listed >= 0).astype(F32)
        by_inverse = strength * along + filled * switch * switch * by_strength
        by_dist = (-2.0 / cutoff_sq) * base * by_strength - (
            0.5 * inverse * inverse * inverse
        ) * by_inverse
        scaled = strength * inverse
        centre = jnp.zeros((OCTET, LANES), F32)
        terms = []
        for c in range(3):
            term = by_environ[1 + c] * scaled + 2.0 * deltas[c] * by_dist
            terms.append(term)
            centre = jnp.where(lane == c, jnp.sum(term, axis=1, keepdims=True), centre)
        centre_terms[pl.ds(first, OCTET), :] = centre
        upper_digit = (listed // DIGIT).astype(F32)
        lower_digit = jnp.bitwise_and(listed, DIGIT - 1).astype(F32)
        spread, hits = [], []
        for a in range(OCTET):
            here = numbers == tall(upper_digit[a : a + 1])
            zero = jnp.zeros((DIGIT, LANES), BF16)
            spread.append(
                jnp.concatenate([jnp.where(here, tall(t[a : a + 1]), zero) for t in terms], axis=0)
            )
            hits.append(
                jnp.where(numbers == tall(lower_digit[a : a + 1]), jnp.ones_like(zero), zero)
            )
        return total + lax.dot_general(
            jnp.concatenate(spread, axis=1),
            jnp.concatenate(hits, axis=1),
            contract_last,
            preferred_element_type=F32,
        )

    total = run_octets(disperse, jnp.zeros((3 * DIGIT, DIGIT), F32))
    for c in range(3):
        for d in range(DIGIT):
            scattered[c : c + 1, d * DIGIT : (d + 1) * DIGIT] = total[
                c * DIGIT + d : c * DIGIT + d + 1, :
            ]
    total = scattered[0:OCTET, :]
    force = centre_terms[...].T[0:OCTET, :] - total[:, 0:atoms]
    beyond = -total[:, atoms:]
    out_ref[:, 0:atoms] = force
    out_ref[:, atoms:] = beyond
    if parcels_ref.shape[0] > 1:
        mine = live_ref[1]
        kick = step_size * jnp.where(own_ref[3:4, :] == 1.0, 1.0, 1.0 / heavy_mass)
        moving = [own_ref[c : c + 1, :] for c in range(3)] + [
            velocities_ref[c] + kick * force[c : c + 1] for c in range(3)
        ]
        moving = jnp.concatenate(moving + [jnp.zeros((OCTET - 6, atoms), F32)], axis=0)
        for s in range(2):
            tile = jnp.where(mine == s, moving, beyond)
            for b in range(parcels_ref.shape[0] // 2):
                parcels_ref[2 * b + s] = tile


def kick_kernel(part_ref, back_ref, rows_ref, types_ref, positions_ref, velocities_ref, forces_ref, out_ref):
    atoms = types_ref.shape[1]
    rows = turned_rows(rows_ref)
    hits = (
        lax.broadcasted_iota(jnp.int32, (atoms, rows.shape[1]), 0) == rows
    ).astype(F32)
    returned = lax.dot_general(
        back_ref[...],
        hits,
        (((1,), (1,)), ((), ())),
        preferred_element_type=F32,
        precision=lax.Precision.HIGHEST,
    )
    force = part_ref[:, 0:atoms] + returned
    inverse_mass = jnp.where(types_ref[...] == 1, 1.0, 1.0 / heavy_mass)
    rows = []
    for c in range(3):
        forces_ref[c] = force[c : c + 1]
        rows.append(positions_ref[c])
    for c in range(3):
        rows.append(velocities_ref[c] + step_size * inverse_mass * force[c : c + 1])
    tile = jnp.concatenate(rows + [jnp.zeros((2, atoms), F32)], axis=0)
    for b in range(out_ref.shape[0]):
        out_ref[b] = tile


def mix_kernel(place_ref, table_ref, gathered_ref, positions_ref, velocities_ref):
    mine = place_ref[0]
    count = gathered_ref.shape[0]
    tile_shape = gathered_ref.shape[1:]
    is_position = lax.broadcasted_iota(jnp.int32, tile_shape, 0) < 3
    turned = jnp.zeros(tile_shape, F32)
    crossed = jnp.zeros(tile_shape, F32)
    for b in range(count):
        tile = gathered_ref[b]
        turned = turned + table_ref[mine, b] * tile
        crossed = crossed + jnp.where(
            is_position, -table_ref[mine, 2 * count + b], table_ref[mine, count + b]
        ) * tile
    for c in range(3):
        positions_ref[c] = turned[c : c + 1] + crossed[3 + c : 4 + c]
        velocities_ref[c] = turned[3 + c : 4 + c] + crossed[c : c + 1]


def settle_kernel(
    place_ref, table_ref, part_ref, gathered_ref, rows_ref, types_ref, positions_ref, velocities_ref, forces_ref
):
    mine, slab = place_ref[0], place_ref[1]
    count = gathered_ref.shape[0] // 2
    tile_shape = gathered_ref.shape[1:]
    is_position = lax.broadcasted_iota(jnp.int32, tile_shape, 0) < 3
    zero = jnp.zeros(tile_shape, F32)
    turned, crossed, halo_turned, halo_travel = zero, zero, zero, zero
    for b in range(count):
        tile = gathered_ref[2 * b + slab]
        beyond = gathered_ref[2 * b + 1 - slab]
        cosine, travel = table_ref[mine, b], table_ref[mine, count + b]
        spring = table_ref[mine, 2 * count + b]
        turned = turned + cosine * tile
        crossed = crossed + jnp.where(is_position, -spring, travel) * tile
        halo_turned = halo_turned + cosine * beyond
        halo_travel = halo_travel + travel * beyond
    rows = turned_rows(rows_ref)
    atoms = types_ref.shape[1]
    hits = lax.broadcasted_iota(jnp.int32, (atoms, rows.shape[1]), 0) == rows
    own_beyond = gathered_ref[2 * mine + 1 - slab]
    rest = jnp.concatenate([halo_travel, halo_turned, own_beyond], axis=0)
    parts = []
    for _ in range(3):
        parts.append(rest.astype(BF16))
        rest = rest - parts[-1].astype(F32)
    sums = lax.dot_general(
        jnp.concatenate(parts, axis=0),
        hits.astype(F32).astype(BF16),
        (((1,), (1,)), ((), ())),
        preferred_element_type=F32,
    )
    tall = 3 * OCTET
    returned = sums[:tall] + sums[tall : 2 * tall] + sums[2 * tall :]
    kick = step_size * jnp.where(types_ref[...] == 1, 1.0, 1.0 / heavy_mass)
    for c in range(3):
        positions_ref[c] = (
            turned[c : c + 1] + crossed[3 + c : 4 + c] + kick * returned[c : c + 1]
        )
        velocities_ref[c] = (
            turned[3 + c : 4 + c]
            + crossed[c : c + 1]
            + kick * returned[OCTET + c : OCTET + c + 1]
        )
        forces_ref[c] = part_ref[c : c + 1, 0:atoms] + returned[2 * OCTET + c : 2 * OCTET + c + 1]


VMEM_SPEC = pl.BlockSpec(memory_space=pltpu.VMEM)
HBM_SPEC = pl.BlockSpec(memory_space=pltpu.HBM)
SMEM_SPEC = pl.BlockSpec(memory_space=pltpu.SMEM)
SMALL = pltpu.CompilerParams(vmem_limit_bytes=SMALL_LIMIT)


def shape(*dims, dtype=F32):
    return jax.ShapeDtypeStruct(dims, dtype)


def call_force(live_atoms, own, halo, neighbours, weights, velocities, parcels=1):
    atoms, slots = neighbours.shape
    entries = atoms + halo.shape[1]
    e1 = weights[0].shape[1]
    e2 = weights[2].shape[1]
    e3 = weights[4].shape[1]
    rows_two = e2 // e1 * CHUNK
    rows_three = e3 // e1 * CHUNK
    assert entries <= DIGIT * DIGIT and slots == LANES and atoms == LANES and entries == 2 * LANES
    assert e3 == 2 * e2 and e2 == 2 * e1 and rows_three <= LANES and M2 <= e1
    groups = atoms // GROUP
    return pl.pallas_call(
        force_kernel,
        out_shape=(shape(OCTET, entries), shape(parcels, OCTET, atoms)),
        in_specs=[SMEM_SPEC]
        + [VMEM_SPEC] * 9
        + [HBM_SPEC] * (len(weights) - 6)
        + [VMEM_SPEC],
        out_specs=(VMEM_SPEC, VMEM_SPEC),
        scratch_shapes=[
            pltpu.VMEM((atoms, LANES), F32),
            pltpu.VMEM((LANES, LANES), F32),
            pltpu.VMEM((CHUNK, rows_two), BF16),
            pltpu.VMEM((rows_two, CHUNK), BF16),
            pltpu.VMEM((rows_two, rows_three), BF16),
            pltpu.VMEM((rows_three, rows_two), BF16),
            pltpu.VMEM((4, CHUNK, slots), F32),
            pltpu.VMEM((4 * atoms, slots), F32),
            pltpu.VMEM((3, atoms, slots), F32),
            pltpu.VMEM((atoms, slots), F32),
            pltpu.VMEM((groups, CHUNK, GROUP * slots), BF16),
            pltpu.VMEM((groups, rows_two, GROUP * slots), BF16),
            pltpu.VMEM((groups, rows_three, GROUP * slots), BF16),
            pltpu.VMEM((groups, rows_three, GROUP * slots), BF16),
            pltpu.VMEM((4 * atoms, rows_three), F32),
            pltpu.VMEM((4, rows_three, atoms), F32),
            pltpu.VMEM((e3 * M2, atoms), BF16),
            pltpu.VMEM((e3 * M2, atoms), F32),
            pltpu.VMEM(weights[6].shape[::-1], BF16),
            pltpu.VMEM((e3 * M2, 4 * atoms), BF16),
            pltpu.VMEM((4 * atoms, slots), F32),
            pltpu.VMEM((atoms, slots), F32),
            pltpu.VMEM((atoms, LANES), F32),
            pltpu.VMEM((OCTET, entries), F32),
        ]
        + [pltpu.VMEM(w.shape, w.dtype) for w in weights[6:]]
        + [pltpu.SemaphoreType.DMA((len(weights) - 6,))],
        compiler_params=pltpu.CompilerParams(vmem_limit_bytes=VMEM_LIMIT),
        name="force",
    )(live_atoms, own, halo, neighbours, *weights, velocities)


def row(array):
    return array.reshape(1, -1)


def local(
    positions,
    velocities,
    atom_types,
    live_atoms,
    halo_rows,
    neighbours,
    type_scale,
    type_shift,
    embed_two,
    embed_bias_two,
    embed_three,
    embed_bias_three,
    fit_first,
    fit_bias_first,
    fit_second,
    fit_bias_second,
    fit_third,
    fit_bias_third,
    fit_readout,
):
    weights = (
        type_scale,
        type_shift,
        embed_two,
        row(embed_bias_two),
        embed_three,
        row(embed_bias_three),
        fit_first.T,
        row(fit_bias_first),
        fit_second,
        row(fit_bias_second),
        fit_third,
        row(fit_bias_third),
        fit_readout,
    )
    atoms = positions.shape[2]
    half = halo_rows.shape[1] // 2
    beads = lax.axis_size("bead")
    slabs = lax.axis_size("slab")
    to_next = [(i, (i + 1) % slabs) for i in range(slabs)]
    to_last = [((i + 1) % slabs, i) for i in range(slabs)]

    def exchange(outgoing, up, down):
        if slabs == 2:
            return lax.ppermute(outgoing, "slab", to_next)
        return jnp.concatenate(
            [
                lax.ppermute(outgoing[:, up], "slab", to_next),
                lax.ppermute(outgoing[:, down], "slab", to_last),
            ],
            axis=1,
        )

    low, high = slice(0, half), slice(half, 2 * half)
    types = row(atom_types)
    own, sent = pl.pallas_call(
        outgoing_kernel,
        out_shape=(shape(OCTET, atoms), shape(OCTET, 2 * half)),
        in_specs=[VMEM_SPEC] * 3,
        out_specs=(VMEM_SPEC, VMEM_SPEC),
        compiler_params=SMALL,
        name="outgoing",
    )(positions, types, halo_rows)
    halo = exchange(sent, low, high)
    place = jnp.stack([lax.axis_index("bead"), lax.axis_index("slab")]).astype(jnp.int32)
    scalars = jnp.concatenate([live_atoms, place[1:]])
    table = jnp.asarray(bead_tables(beads))
    sharded_shape = shape(*positions.shape)
    if slabs == 2:
        part, parcels = call_force(
            scalars, own, halo, neighbours, weights, velocities, beads * slabs
        )
        gathered = lax.all_to_all(
            parcels, ("bead", "slab"), split_axis=0, concat_axis=0, tiled=True
        )
        return pl.pallas_call(
            settle_kernel,
            out_shape=(sharded_shape,) * 3,
            in_specs=[SMEM_SPEC] * 2 + [VMEM_SPEC] * 4,
            out_specs=(VMEM_SPEC,) * 3,
            compiler_params=SMALL,
            name="settle",
        )(place, table, part, gathered, halo_rows, types)
    part, _ = call_force(scalars, own, halo, neighbours, weights, velocities)
    back = exchange(part[:, atoms:], high, low)
    back = jnp.concatenate([back[:, high], back[:, low]], axis=1)
    forces, kicked = pl.pallas_call(
        kick_kernel,
        out_shape=(sharded_shape, shape(beads, OCTET, atoms)),
        in_specs=[VMEM_SPEC] * 6,
        out_specs=(VMEM_SPEC, VMEM_SPEC),
        compiler_params=SMALL,
        name="kick",
    )(part, back, halo_rows, types, positions, velocities)
    gathered = lax.all_to_all(kicked, "bead", split_axis=0, concat_axis=0, tiled=True)
    positions_new, velocities_new = pl.pallas_call(
        mix_kernel,
        out_shape=(sharded_shape, sharded_shape),
        in_specs=[SMEM_SPEC, SMEM_SPEC, VMEM_SPEC],
        out_specs=(VMEM_SPEC, VMEM_SPEC),
        compiler_params=SMALL,
        name="mix",
    )(place, table, gathered)
    return positions_new, velocities_new, forces


def solution(mesh):
    sharded = P(None, "bead", "slab")
    return jax.shard_map(
        local,
        mesh=mesh,
        in_specs=(
            sharded,
            sharded,
            P("slab"),
            P("slab"),
            P("slab", None),
            P("slab", None),
        )
        + (P(),) * 13,
        out_specs=(sharded, sharded, sharded),
        check_vma=False,
    )
```

```python
import functools
import math

import jax
import jax.numpy as jnp
import numpy as np
from jax import lax
from jax.experimental import pallas as pl
from jax.experimental.pallas import tpu as pltpu
from jax.sharding import PartitionSpec as P

M2 = 16
step_size = 0.25
phase_rate = 1.2
cutoff_sq = 16.0
softening = 0.25
heavy_mass = 16.0

F32 = jnp.float32
BF16 = jnp.bfloat16
LANES = 128
OCTET = 8
UNROLL = 16
DIGIT = 16
GROUP = 2
CHUNK = 32
ONE_AT = 20.0
VMEM_LIMIT = 55168 * 1024
SMALL_LIMIT = 4 * 1024 * 1024


def bead_tables(count):
    index = np.arange(count)
    angles = 2.0 * np.pi * np.outer(index, index) / count
    norm = math.sqrt(2.0 / count)
    edge = 1.0 / math.sqrt(count)
    middle = count // 2
    basis = np.where(
        index[None, :] == 0,
        edge,
        np.where(
            index[None, :] < middle,
            norm * np.cos(angles),
            np.where(
                index[None, :] == middle, np.cos(np.pi * index)[:, None] * edge, norm * np.sin(angles)
            ),
        ),
    )
    sine = np.sin(np.pi * index / count)
    ratio = 2.0 * sine
    phases = phase_rate * count * sine
    travel = np.where(index == 0, 1.0, np.sin(phases) / np.where(index == 0, 1.0, ratio))

    def assemble(diagonal):
        return (basis * diagonal[None, :]) @ basis.T

    return np.concatenate(
        [assemble(np.cos(phases)), assemble(travel), assemble(ratio * np.sin(phases))], axis=1
    ).astype(np.float32)


def lookup(table, indices):
    return jnp.take_along_axis(table, indices, axis=1, mode="promise_in_bounds")


def turned_rows(rows_ref):
    rows = rows_ref[...]
    half = rows.shape[1] // 2
    return jnp.concatenate([rows[:, half:], rows[:, :half]], axis=1)


def field_table(positions_ref, types_ref):
    hydrogen = (types_ref[...] == 1).astype(F32)
    return jnp.concatenate(
        [positions_ref[0], positions_ref[1], positions_ref[2], hydrogen]
        + [jnp.zeros((OCTET - 4, hydrogen.shape[1]), F32)],
        axis=0,
    )


def outgoing_kernel(positions_ref, types_ref, rows_ref, own_ref, send_ref):
    own = field_table(positions_ref, types_ref)
    own_ref[...] = own
    send_ref[...] = lookup(own, jnp.broadcast_to(turned_rows(rows_ref), own.shape))


def force_kernel(
    live_ref,
    near_refs,
    far_refs,
    listed_ref,
    scale_ref,
    shift_ref,
    two_ref,
    bias_two_ref,
    three_ref,
    bias_three_ref,
    first_hbm,
    fit_bias_first_hbm,
    second_hbm,
    fit_bias_second_hbm,
    third_hbm,
    fit_bias_third_hbm,
    readout_hbm,
    velocities_ref,
    out_ref,
    parcels_ref,
    own_t,
    padded,
    two_in,
    two_out,
    three_in,
    three_out,
    consts,
    environ,
    offset,
    around,
    kept_one,
    kept_two,
    kept_three,
    kept_sum,
    features,
    features_t,
    descriptor,
    grad_descriptor,
    first_rows,
    products,
    grad_environ,
    grad_strength,
    centre_terms,
    scattered,
    first_ref,
    fit_bias_first_ref,
    second_ref,
    fit_bias_second_ref,
    third_ref,
    fit_bias_third_ref,
    readout_ref,
    own_ref,
    halo_ref,
    arrived,
):
    late = [
        pltpu.make_async_copy(source, target, arrived.at[k])
        for k, (source, target) in enumerate(
            (
                (first_hbm, first_ref),
                (fit_bias_first_hbm, fit_bias_first_ref),
                (second_hbm, second_ref),
                (fit_bias_second_hbm, fit_bias_second_ref),
                (third_hbm, third_ref),
                (fit_bias_third_hbm, fit_bias_third_ref),
                (readout_hbm, readout_ref),
            )
        )
    ]
    for copy in late:
        copy.start()
    if len(near_refs) > 1:
        own_ref[...] = field_table(*near_refs)
        table = field_table(*far_refs[:2])
        halo_ref[...] = lookup(table, jnp.broadcast_to(turned_rows(far_refs[2]), table.shape))
    else:
        own_ref[...] = near_refs[0][...]
        halo_ref[...] = far_refs[0][...]
    live = live_ref[0]
    octets = (live + (OCTET - 1)) // OCTET
    atoms, slots = listed_ref.shape
    e1 = scale_ref.shape[1]
    e2 = two_ref.shape[1]
    e3 = three_ref.shape[1]
    rows_one, rows_two, rows_three = two_in.shape[0], three_in.shape[0], three_out.shape[0]
    copies_two, copies_three = e2 // e1, e3 // e1

    def split_bias(bias):
        high = bias.astype(BF16).astype(F32)
        return high, bias - high

    padded[...] = jnp.zeros_like(padded)
    bias_high, bias_low = split_bias(bias_two_ref[...])
    for k in range(copies_two):
        cols = slice(k * e1, (k + 1) * e1)
        padded[0:e1, k * CHUNK : k * CHUNK + e1] = two_ref[:, cols].astype(F32)
        padded[e1 : e1 + 1, k * CHUNK : k * CHUNK + e1] = bias_high[:, cols]
        padded[e1 + 1 : e1 + 2, k * CHUNK : k * CHUNK + e1] = bias_low[:, cols]
    table = padded[...]
    two_in[...] = table[:rows_one, :rows_two].astype(BF16)
    two_out[...] = table.T[:rows_two, :rows_one].astype(BF16)

    padded[...] = jnp.zeros_like(padded)
    bias_high, bias_low = split_bias(bias_three_ref[...])
    for k in range(copies_three):
        cols = slice(k * e1, (k + 1) * e1)
        for m in range(copies_two):
            padded[m * CHUNK : m * CHUNK + e1, k * CHUNK : k * CHUNK + e1] = three_ref[
                m * e1 : (m + 1) * e1, cols
            ].astype(F32)
        padded[e1 : e1 + 1, k * CHUNK : k * CHUNK + e1] = bias_high[:, cols]
        padded[e1 + 1 : e1 + 2, k * CHUNK : k * CHUNK + e1] = bias_low[:, cols]
    table = padded[...]
    three_in[...] = table[:rows_two, :rows_three].astype(BF16)
    three_out[...] = table.T[:rows_three, :rows_two].astype(BF16)

    padded[...] = jnp.zeros_like(padded)
    padded[0:2, 0:e1] = scale_ref[...]
    padded[2:4, 0:e1] = shift_ref[...]
    padded[2:3, e1 : e1 + 2] = jnp.full((1, 2), ONE_AT, F32)
    padded[3:4, e1 : e1 + 2] = jnp.full((1, 2), ONE_AT, F32)
    table = padded[...].T
    for k in range(4):
        column = table[:CHUNK, k : k + 1]
        if k % 2 == 1:
            column = column - table[:CHUNK, k - 1 : k]
        consts[k] = jnp.broadcast_to(column, (CHUNK, slots))

    padded[...] = jnp.zeros_like(padded)
    padded[0:OCTET, :] = own_ref[...]
    own_t[...] = padded[...].T

    features[...] = jnp.zeros_like(features)
    def gather_octet(first):
        listed = listed_ref[pl.ds(first, OCTET), :]
        low = jnp.bitwise_and(listed, LANES - 1)
        is_own = listed < atoms
        centre = own_t[pl.ds(first, OCTET), :]
        fetched = []
        for c in range(4):
            near = lookup(jnp.broadcast_to(own_ref[c : c + 1, :], (OCTET, LANES)), low)
            far = lookup(jnp.broadcast_to(halo_ref[c : c + 1, :], (OCTET, LANES)), low)
            fetched.append(jnp.where(is_own, near, far))
        deltas = [fetched[c] - centre[:, c : c + 1] for c in range(3)]
        return listed, deltas, fetched[3]

    def geometry(listed, deltas):
        filled = (listed >= 0).astype(F32)
        dist_sq = deltas[0] * deltas[0] + deltas[1] * deltas[1] + deltas[2] * deltas[2]
        inverse = lax.rsqrt(dist_sq + softening)
        switch = jnp.maximum(1.0 - dist_sq * (1.0 / cutoff_sq), 0.0)
        base = filled * switch * inverse
        return inverse, switch, base, base * switch

    def run_octets(step, carry=0):
        def body(turn, carry):
            for u in range(UNROLL):
                carry = step(turn * UNROLL + u, carry)
            return carry

        return lax.fori_loop(0, (octets + UNROLL - 1) // UNROLL, body, carry)

    def run_skewed(stages, skew):
        def body(turn, carry):
            waiting = [stages(turn * UNROLL + u) for u in range(UNROLL)]
            begun = 0
            active = []
            step = 0
            while begun < UNROLL or active:
                if begun < UNROLL and step % skew == 0:
                    active.append(waiting[begun])
                    begun += 1
                still = []
                for one in active:
                    try:
                        next(one)
                        still.append(one)
                    except StopIteration:
                        pass
                active = still
                step += 1
            return carry

        lax.fori_loop(0, (octets + UNROLL - 1) // UNROLL, body, 0)

    def surround(octet, carry):
        first = pl.multiple_of(octet * OCTET, OCTET)
        listed, deltas, hydrogen = gather_octet(first)
        inverse, _, _, strength = geometry(listed, deltas)
        around[pl.ds(first, OCTET), :] = hydrogen
        scaled = strength * inverse
        environ[pl.ds(first * 4, OCTET, stride=4), :] = strength
        for c in range(3):
            offset[c, pl.ds(first, OCTET), :] = deltas[c]
            environ[pl.ds(first * 4 + 1 + c, OCTET, stride=4), :] = scaled * deltas[c]
        return carry

    run_octets(surround)

    def forward(octet):
        first = pl.multiple_of(octet * OCTET, OCTET)
        hydrogen = around[pl.ds(first, OCTET), :]
        rows = pl.ds(pl.multiple_of(first * 4, OCTET * 4), OCTET * 4)
        groups = range(OCTET // GROUP)
        ones, twos, threes = [], [], []
        for g in groups:
            inputs = []
            for a in range(g * GROUP, (g + 1) * GROUP):
                line, kind = environ[pl.ds(first * 4 + 4 * a, 1), :], hydrogen[a : a + 1]
                inputs.append(
                    line * consts[0] + consts[2] + kind * (line * consts[1] + consts[3])
                )
            ones.append(jnp.tanh(jnp.concatenate(inputs, axis=1).astype(BF16)))
            yield
        for g in groups:
            kept_one[octet * len(groups) + g] = ones[g]
            two = jnp.tanh(
                jnp.dot(two_out[...], ones[g], preferred_element_type=F32).astype(BF16)
            )
            kept_two[octet * len(groups) + g] = two
            twos.append(two + jnp.concatenate([ones[g]] * copies_two, axis=0))
            yield
        by_slot = environ[rows, :].T.astype(BF16)
        column = lax.broadcasted_iota(jnp.int32, by_slot.shape, 1) // 4
        total = jnp.zeros((rows_three, OCTET * 4), F32)
        for g in groups:
            three = jnp.tanh(
                jnp.dot(three_out[...], twos[g], preferred_element_type=F32).astype(BF16)
            )
            kept_three[octet * len(groups) + g] = three
            sum_three = three + jnp.concatenate([twos[g]] * 2, axis=0)
            kept_sum[octet * len(groups) + g] = sum_three
            blocks = jnp.concatenate(
                [
                    jnp.where(column == a, by_slot, jnp.zeros_like(by_slot))
                    for a in range(g * GROUP, (g + 1) * GROUP)
                ],
                axis=0,
            )
            total = total + jnp.dot(sum_three, blocks, preferred_element_type=F32)
            yield
        features[rows, :] = total.T

    run_skewed(forward, 2)

    for copy in late:
        copy.wait()
    first_rows[...] = first_ref[...].T
    for c in range(4):
        features_t[c] = features[pl.ds(c, atoms, stride=4), :].T * (1.0 / slots)

    unit_rows = [q * CHUNK + r for q in range(copies_three) for r in range(e1)]
    leading = [features_t[c, 0:M2, :] for c in range(4)]
    for e, at in enumerate(unit_rows):
        total = None
        for c in range(4):
            term = features_t[c, at : at + 1, :] * leading[c]
            total = term if total is None else total + term
        descriptor[e * M2 : (e + 1) * M2, :] = total.astype(BF16)

    fit_one = jnp.tanh(
        jnp.dot(first_ref[...], descriptor[...], preferred_element_type=F32).T
        + fit_bias_first_ref[...]
    )
    tanh_two = jnp.tanh(
        jnp.dot(fit_one.astype(BF16), second_ref[...], preferred_element_type=F32)
        + fit_bias_second_ref[...]
    )
    fit_two = tanh_two + fit_one
    tanh_three = jnp.tanh(
        jnp.dot(fit_two.astype(BF16), third_ref[...], preferred_element_type=F32)
        + fit_bias_third_ref[...]
    )
    living = (lax.broadcasted_iota(jnp.int32, (atoms, 1), 0) < live).astype(F32)
    readout = readout_ref[0:1, :] + own_t[:, 3:4] * (readout_ref[1:2, :] - readout_ref[0:1, :])
    grad = living * readout
    contract_last = (((1,), (1,)), ((), ()))
    inner = (grad * (1.0 - tanh_three * tanh_three)).astype(BF16)
    grad = grad + lax.dot_general(inner, third_ref[...], contract_last, preferred_element_type=F32)
    inner = (grad * (1.0 - tanh_two * tanh_two)).astype(BF16)
    grad = grad + lax.dot_general(inner, second_ref[...], contract_last, preferred_element_type=F32)
    inner = (grad * (1.0 - fit_one * fit_one)).astype(BF16)
    grad_descriptor[...] = lax.dot_general(
        first_rows[...], inner, contract_last, preferred_element_type=F32
    )

    shared = [jnp.zeros((M2, atoms), F32) for _ in range(4)]
    short = [tile.astype(BF16) for tile in leading]
    for e, at in enumerate(unit_rows):
        rows = grad_descriptor[e * M2 : (e + 1) * M2, :]
        packed = rows.astype(BF16)
        for c in range(4):
            shared[c] = shared[c] + rows * features_t[c, at : at + 1, :]
            products[e * M2 : (e + 1) * M2, c * atoms : (c + 1) * atoms] = packed * short[c]
    unit = lax.broadcasted_iota(jnp.int32, (rows_three, 1), 0)
    unit = jnp.where(unit % CHUNK < e1, unit // CHUNK * e1 + unit % CHUNK, -1)
    gather = (lax.broadcasted_iota(jnp.int32, (1, e3 * M2), 1) // M2 == unit).astype(F32)
    sums = jnp.dot(gather.astype(BF16), products[...], preferred_element_type=F32)
    for c in range(4):
        total = sums[:, c * atoms : (c + 1) * atoms] + jnp.concatenate(
            [shared[c], jnp.zeros((rows_three - M2, atoms), F32)], axis=0
        )
        features[pl.ds(c, atoms, stride=4), :] = (total * (1.0 / slots)).T

    scattered[...] = jnp.zeros_like(scattered)
    centre_terms[...] = jnp.zeros_like(centre_terms)
    lane = lax.broadcasted_iota(jnp.int32, (OCTET, LANES), 1)

    def backward(octet):
        first = pl.multiple_of(octet * OCTET, OCTET)
        grad_rows = features[pl.ds(pl.multiple_of(first * 4, OCTET * 4), OCTET * 4), :]
        grad_cols = grad_rows.T.astype(BF16)
        grad_rows = grad_rows.astype(BF16)
        groups = range(OCTET // GROUP)
        rows = pl.ds(pl.multiple_of(first * 4, OCTET * 4), OCTET * 4)
        quads = environ[rows, :]
        owner = lax.broadcasted_iota(jnp.int32, quads.shape, 0) // 4
        by_quad = jnp.zeros_like(quads)
        inners, grad_threes, grad_twos = [], [], []
        for g in groups:
            at = octet * len(groups) + g
            blocks = jnp.concatenate(
                [
                    jnp.where(owner == a, quads, 0.0).astype(BF16)
                    for a in range(g * GROUP, (g + 1) * GROUP)
                ],
                axis=1,
            )
            grad_three = jnp.dot(grad_cols, blocks, preferred_element_type=F32).astype(BF16)
            three = kept_three[at]
            inners.append(grad_three * (1.0 - three * three))
            grad_threes.append(grad_three[:rows_two] + grad_three[rows_two:])
            yield
        for g in groups:
            at = octet * len(groups) + g
            grad_two = (
                jnp.dot(three_in[...], inners[g], preferred_element_type=F32).astype(BF16)
                + grad_threes[g]
            )
            two = kept_two[at]
            inners[g] = grad_two * (1.0 - two * two)
            folded = grad_two[:CHUNK]
            for k in range(1, copies_two):
                folded = folded + grad_two[k * CHUNK : (k + 1) * CHUNK]
            grad_twos.append(folded)
            both = jnp.dot(grad_rows, kept_sum[at], preferred_element_type=F32)
            for k in range(GROUP):
                by_quad = jnp.where(
                    owner == g * GROUP + k, both[:, k * LANES : (k + 1) * LANES], by_quad
                )
            yield
        grad_environ[rows, :] = by_quad
        for g in groups:
            at = octet * len(groups) + g
            grad_one = jnp.dot(two_in[...], inners[g], preferred_element_type=F32) + grad_twos[g]
            one = kept_one[at].astype(F32)
            grad_one = grad_one * (1.0 - one * one)
            for k in range(GROUP):
                line = first + g * GROUP + k
                kind = around[pl.ds(line, 1), :]
                weighed = grad_one[:, k * LANES : (k + 1) * LANES] * (
                    consts[0] + kind * consts[1]
                )
                grad_strength[pl.ds(line, 1), :] = jnp.sum(weighed, axis=0, keepdims=True)


    run_skewed(backward, 1)

    numbers = lax.broadcasted_iota(jnp.int32, (DIGIT, LANES), 0).astype(F32).astype(BF16)

    def tall(line):
        return jnp.broadcast_to(line, (DIGIT, LANES)).astype(BF16)

    def disperse(octet, total):
        first = pl.multiple_of(octet * OCTET, OCTET)
        listed = listed_ref[pl.ds(first, OCTET), :]
        deltas = [offset[c, pl.ds(first, OCTET), :] for c in range(3)]
        inverse, switch, base, strength = geometry(listed, deltas)
        by_environ = [
            grad_environ[pl.ds(first * 4 + c, OCTET, stride=4), :] for c in range(4)
        ]
        along = (
            by_environ[1] * deltas[0] + by_environ[2] * deltas[1] + by_environ[3] * deltas[2]
        )
        by_strength = (
            grad_strength[pl.ds(first, OCTET), :] + by_environ[0] + along * inverse
        )
        filled = (listed >= 0).astype(F32)
        by_inverse = strength * along + filled * switch * switch * by_strength
        by_dist = (-2.0 / cutoff_sq) * base * by_strength - (
            0.5 * inverse * inverse * inverse
        ) * by_inverse
        scaled = strength * inverse
        centre = jnp.zeros((OCTET, LANES), F32)
        terms = []
        for c in range(3):
            term = by_environ[1 + c] * scaled + 2.0 * deltas[c] * by_dist
            terms.append(term)
            centre = jnp.where(lane == c, jnp.sum(term, axis=1, keepdims=True), centre)
        centre_terms[pl.ds(first, OCTET), :] = centre
        upper_digit = (listed // DIGIT).astype(F32)
        lower_digit = jnp.bitwise_and(listed, DIGIT - 1).astype(F32)
        spread, hits = [], []
        for a in range(OCTET):
            here = numbers == tall(upper_digit[a : a + 1])
            zero = jnp.zeros((DIGIT, LANES), BF16)
            spread.append(
                jnp.concatenate([jnp.where(here, tall(t[a : a + 1]), zero) for t in terms], axis=0)
            )
            hits.append(
                jnp.where(numbers == tall(lower_digit[a : a + 1]), jnp.ones_like(zero), zero)
            )
        return total + lax.dot_general(
            jnp.concatenate(spread, axis=1),
            jnp.concatenate(hits, axis=1),
            contract_last,
            preferred_element_type=F32,
        )

    total = run_octets(disperse, jnp.zeros((3 * DIGIT, DIGIT), F32))
    for c in range(3):
        for d in range(DIGIT):
            scattered[c : c + 1, d * DIGIT : (d + 1) * DIGIT] = total[
                c * DIGIT + d : c * DIGIT + d + 1, :
            ]
    total = scattered[0:OCTET, :]
    force = centre_terms[...].T[0:OCTET, :] - total[:, 0:atoms]
    beyond = -total[:, atoms:]
    out_ref[:, 0:atoms] = force
    out_ref[:, atoms:] = beyond
    if parcels_ref.shape[0] > 1:
        mine = live_ref[1]
        kick = step_size * jnp.where(own_ref[3:4, :] == 1.0, 1.0, 1.0 / heavy_mass)
        moving = [own_ref[c : c + 1, :] for c in range(3)] + [
            velocities_ref[c] + kick * force[c : c + 1] for c in range(3)
        ]
        moving = jnp.concatenate(moving + [jnp.zeros((OCTET - 6, atoms), F32)], axis=0)
        for s in range(2):
            tile = jnp.where(mine == s, moving, beyond)
            for b in range(parcels_ref.shape[0] // 2):
                parcels_ref[2 * b + s] = tile


def kick_kernel(part_ref, back_ref, rows_ref, types_ref, positions_ref, velocities_ref, forces_ref, out_ref):
    atoms = types_ref.shape[1]
    rows = turned_rows(rows_ref)
    hits = (
        lax.broadcasted_iota(jnp.int32, (atoms, rows.shape[1]), 0) == rows
    ).astype(F32)
    returned = lax.dot_general(
        back_ref[...],
        hits,
        (((1,), (1,)), ((), ())),
        preferred_element_type=F32,
        precision=lax.Precision.HIGHEST,
    )
    force = part_ref[:, 0:atoms] + returned
    inverse_mass = jnp.where(types_ref[...] == 1, 1.0, 1.0 / heavy_mass)
    rows = []
    for c in range(3):
        forces_ref[c] = force[c : c + 1]
        rows.append(positions_ref[c])
    for c in range(3):
        rows.append(velocities_ref[c] + step_size * inverse_mass * force[c : c + 1])
    tile = jnp.concatenate(rows + [jnp.zeros((2, atoms), F32)], axis=0)
    for b in range(out_ref.shape[0]):
        out_ref[b] = tile


def mix_kernel(place_ref, table_ref, gathered_ref, positions_ref, velocities_ref):
    mine = place_ref[0]
    count = gathered_ref.shape[0]
    tile_shape = gathered_ref.shape[1:]
    is_position = lax.broadcasted_iota(jnp.int32, tile_shape, 0) < 3
    turned = jnp.zeros(tile_shape, F32)
    crossed = jnp.zeros(tile_shape, F32)
    for b in range(count):
        tile = gathered_ref[b]
        turned = turned + table_ref[mine, b] * tile
        crossed = crossed + jnp.where(
            is_position, -table_ref[mine, 2 * count + b], table_ref[mine, count + b]
        ) * tile
    for c in range(3):
        positions_ref[c] = turned[c : c + 1] + crossed[3 + c : 4 + c]
        velocities_ref[c] = turned[3 + c : 4 + c] + crossed[c : c + 1]


def settle_kernel(
    place_ref, table_ref, part_ref, gathered_ref, rows_ref, types_ref, positions_ref, velocities_ref, forces_ref
):
    mine, slab = place_ref[0], place_ref[1]
    count = gathered_ref.shape[0] // 2
    tile_shape = gathered_ref.shape[1:]
    is_position = lax.broadcasted_iota(jnp.int32, tile_shape, 0) < 3
    zero = jnp.zeros(tile_shape, F32)
    turned, crossed, halo_turned, halo_travel = zero, zero, zero, zero
    for b in range(count):
        tile = gathered_ref[2 * b + slab]
        beyond = gathered_ref[2 * b + 1 - slab]
        cosine, travel = table_ref[mine, b], table_ref[mine, count + b]
        spring = table_ref[mine, 2 * count + b]
        turned = turned + cosine * tile
        crossed = crossed + jnp.where(is_position, -spring, travel) * tile
        halo_turned = halo_turned + cosine * beyond
        halo_travel = halo_travel + travel * beyond
    rows = turned_rows(rows_ref)
    atoms = types_ref.shape[1]
    hits = lax.broadcasted_iota(jnp.int32, (atoms, rows.shape[1]), 0) == rows
    own_beyond = gathered_ref[2 * mine + 1 - slab]
    rest = jnp.concatenate([halo_travel, halo_turned, own_beyond], axis=0)
    parts = []
    for _ in range(3):
        parts.append(rest.astype(BF16))
        rest = rest - parts[-1].astype(F32)
    sums = lax.dot_general(
        jnp.concatenate(parts, axis=0),
        hits.astype(F32).astype(BF16),
        (((1,), (1,)), ((), ())),
        preferred_element_type=F32,
    )
    tall = 3 * OCTET
    returned = sums[:tall] + sums[tall : 2 * tall] + sums[2 * tall :]
    kick = step_size * jnp.where(types_ref[...] == 1, 1.0, 1.0 / heavy_mass)
    for c in range(3):
        positions_ref[c] = (
            turned[c : c + 1] + crossed[3 + c : 4 + c] + kick * returned[c : c + 1]
        )
        velocities_ref[c] = (
            turned[3 + c : 4 + c]
            + crossed[c : c + 1]
            + kick * returned[OCTET + c : OCTET + c + 1]
        )
        forces_ref[c] = part_ref[c : c + 1, 0:atoms] + returned[2 * OCTET + c : 2 * OCTET + c + 1]


VMEM_SPEC = pl.BlockSpec(memory_space=pltpu.VMEM)
HBM_SPEC = pl.BlockSpec(memory_space=pltpu.HBM)
SMEM_SPEC = pl.BlockSpec(memory_space=pltpu.SMEM)
SMALL = pltpu.CompilerParams(vmem_limit_bytes=SMALL_LIMIT)


def shape(*dims, dtype=F32):
    return jax.ShapeDtypeStruct(dims, dtype)


def call_force(live_atoms, near, far, neighbours, weights, velocities, parcels=1):
    atoms, slots = neighbours.shape
    entries = atoms + far[-1].shape[1]
    e1 = weights[0].shape[1]
    e2 = weights[2].shape[1]
    e3 = weights[4].shape[1]
    rows_two = e2 // e1 * CHUNK
    rows_three = e3 // e1 * CHUNK
    assert entries <= DIGIT * DIGIT and slots == LANES and atoms == LANES and entries == 2 * LANES
    assert e3 == 2 * e2 and e2 == 2 * e1 and rows_three <= LANES and M2 <= e1
    groups = atoms // GROUP
    return pl.pallas_call(
        force_kernel,
        out_shape=(shape(OCTET, entries), shape(parcels, OCTET, atoms)),
        in_specs=(SMEM_SPEC, (VMEM_SPEC,) * len(near), (VMEM_SPEC,) * len(far))
        + (VMEM_SPEC,) * 7
        + (HBM_SPEC,) * (len(weights) - 6)
        + (VMEM_SPEC,),
        out_specs=(VMEM_SPEC, VMEM_SPEC),
        scratch_shapes=[
            pltpu.VMEM((atoms, LANES), F32),
            pltpu.VMEM((LANES, LANES), F32),
            pltpu.VMEM((CHUNK, rows_two), BF16),
            pltpu.VMEM((rows_two, CHUNK), BF16),
            pltpu.VMEM((rows_two, rows_three), BF16),
            pltpu.VMEM((rows_three, rows_two), BF16),
            pltpu.VMEM((4, CHUNK, slots), F32),
            pltpu.VMEM((4 * atoms, slots), F32),
            pltpu.VMEM((3, atoms, slots), F32),
            pltpu.VMEM((atoms, slots), F32),
            pltpu.VMEM((groups, CHUNK, GROUP * slots), BF16),
            pltpu.VMEM((groups, rows_two, GROUP * slots), BF16),
            pltpu.VMEM((groups, rows_three, GROUP * slots), BF16),
            pltpu.VMEM((groups, rows_three, GROUP * slots), BF16),
            pltpu.VMEM((4 * atoms, rows_three), F32),
            pltpu.VMEM((4, rows_three, atoms), F32),
            pltpu.VMEM((e3 * M2, atoms), BF16),
            pltpu.VMEM((e3 * M2, atoms), F32),
            pltpu.VMEM(weights[6].shape[::-1], BF16),
            pltpu.VMEM((e3 * M2, 4 * atoms), BF16),
            pltpu.VMEM((4 * atoms, slots), F32),
            pltpu.VMEM((atoms, slots), F32),
            pltpu.VMEM((atoms, LANES), F32),
            pltpu.VMEM((OCTET, entries), F32),
        ]
        + [pltpu.VMEM(w.shape, w.dtype) for w in weights[6:]]
        + [pltpu.VMEM((OCTET, atoms), F32), pltpu.VMEM((OCTET, entries - atoms), F32)]
        + [pltpu.SemaphoreType.DMA((len(weights) - 6,))],
        compiler_params=pltpu.CompilerParams(vmem_limit_bytes=VMEM_LIMIT),
        name="force",
    )(live_atoms, near, far, neighbours, *weights, velocities)


def row(array):
    return array.reshape(1, -1)


def local(
    positions,
    velocities,
    atom_types,
    live_atoms,
    halo_rows,
    neighbours,
    type_scale,
    type_shift,
    embed_two,
    embed_bias_two,
    embed_three,
    embed_bias_three,
    fit_first,
    fit_bias_first,
    fit_second,
    fit_bias_second,
    fit_third,
    fit_bias_third,
    fit_readout,
):
    weights = (
        type_scale,
        type_shift,
        embed_two,
        row(embed_bias_two),
        embed_three,
        row(embed_bias_three),
        fit_first.T,
        row(fit_bias_first),
        fit_second,
        row(fit_bias_second),
        fit_third,
        row(fit_bias_third),
        fit_readout,
    )
    atoms = positions.shape[2]
    half = halo_rows.shape[1] // 2
    beads = lax.axis_size("bead")
    slabs = lax.axis_size("slab")
    to_next = [(i, (i + 1) % slabs) for i in range(slabs)]
    to_last = [((i + 1) % slabs, i) for i in range(slabs)]

    def exchange(outgoing, up, down):
        return jnp.concatenate(
            [
                lax.ppermute(outgoing[:, up], "slab", to_next),
                lax.ppermute(outgoing[:, down], "slab", to_last),
            ],
            axis=1,
        )

    low, high = slice(0, half), slice(half, 2 * half)
    types = row(atom_types)
    place = jnp.stack([lax.axis_index("bead"), lax.axis_index("slab")]).astype(jnp.int32)
    scalars = jnp.concatenate([live_atoms, place[1:]])
    table = jnp.asarray(bead_tables(beads))
    sharded_shape = shape(*positions.shape)
    if slabs == 2:
        far = tuple(lax.ppermute(a, "slab", to_next) for a in (positions, types, halo_rows))
        part, parcels = call_force(
            scalars, (positions, types), far, neighbours, weights, velocities, beads * slabs
        )
        gathered = lax.all_to_all(
            parcels, ("bead", "slab"), split_axis=0, concat_axis=0, tiled=True
        )
        return pl.pallas_call(
            settle_kernel,
            out_shape=(sharded_shape,) * 3,
            in_specs=[SMEM_SPEC] * 2 + [VMEM_SPEC] * 4,
            out_specs=(VMEM_SPEC,) * 3,
            compiler_params=SMALL,
            name="settle",
        )(place, table, part, gathered, halo_rows, types)
    own, sent = pl.pallas_call(
        outgoing_kernel,
        out_shape=(shape(OCTET, atoms), shape(OCTET, 2 * half)),
        in_specs=[VMEM_SPEC] * 3,
        out_specs=(VMEM_SPEC, VMEM_SPEC),
        compiler_params=SMALL,
        name="outgoing",
    )(positions, types, halo_rows)
    halo = exchange(sent, low, high)
    part, _ = call_force(scalars, (own,), (halo,), neighbours, weights, velocities)
    back = exchange(part[:, atoms:], high, low)
    back = jnp.concatenate([back[:, high], back[:, low]], axis=1)
    forces, kicked = pl.pallas_call(
        kick_kernel,
        out_shape=(sharded_shape, shape(beads, OCTET, atoms)),
        in_specs=[VMEM_SPEC] * 6,
        out_specs=(VMEM_SPEC, VMEM_SPEC),
        compiler_params=SMALL,
        name="kick",
    )(part, back, halo_rows, types, positions, velocities)
    gathered = lax.all_to_all(kicked, "bead", split_axis=0, concat_axis=0, tiled=True)
    positions_new, velocities_new = pl.pallas_call(
        mix_kernel,
        out_shape=(sharded_shape, sharded_shape),
        in_specs=[SMEM_SPEC, SMEM_SPEC, VMEM_SPEC],
        out_specs=(VMEM_SPEC, VMEM_SPEC),
        compiler_params=SMALL,
        name="mix",
    )(place, table, gathered)
    return positions_new, velocities_new, forces


def solution(mesh):
    sharded = P(None, "bead", "slab")
    return jax.shard_map(
        local,
        mesh=mesh,
        in_specs=(
            sharded,
            sharded,
            P("slab"),
            P("slab"),
            P("slab", None),
            P("slab", None),
        )
        + (P(),) * 13,
        out_specs=(sharded, sharded, sharded),
        check_vma=False,
    )
```

```python
import functools
import math

import jax
import jax.numpy as jnp
import numpy as np
from jax import lax
from jax.experimental import pallas as pl
from jax.experimental.pallas import tpu as pltpu
from jax.sharding import PartitionSpec as P

M2 = 16
step_size = 0.25
phase_rate = 1.2
cutoff_sq = 16.0
softening = 0.25
heavy_mass = 16.0

F32 = jnp.float32
BF16 = jnp.bfloat16
LANES = 128
OCTET = 8
UNROLL = 16
DIGIT = 16
GROUP = 2
CHUNK = 32
ONE_AT = 20.0
VMEM_LIMIT = 55168 * 1024
SMALL_LIMIT = 4 * 1024 * 1024


def bead_tables(count):
    index = np.arange(count)
    angles = 2.0 * np.pi * np.outer(index, index) / count
    norm = math.sqrt(2.0 / count)
    edge = 1.0 / math.sqrt(count)
    middle = count // 2
    basis = np.where(
        index[None, :] == 0,
        edge,
        np.where(
            index[None, :] < middle,
            norm * np.cos(angles),
            np.where(
                index[None, :] == middle, np.cos(np.pi * index)[:, None] * edge, norm * np.sin(angles)
            ),
        ),
    )
    sine = np.sin(np.pi * index / count)
    ratio = 2.0 * sine
    phases = phase_rate * count * sine
    travel = np.where(index == 0, 1.0, np.sin(phases) / np.where(index == 0, 1.0, ratio))

    def assemble(diagonal):
        return (basis * diagonal[None, :]) @ basis.T

    return np.concatenate(
        [assemble(np.cos(phases)), assemble(travel), assemble(ratio * np.sin(phases))], axis=1
    ).astype(np.float32)


def lookup(table, indices):
    return jnp.take_along_axis(table, indices, axis=1, mode="promise_in_bounds")


def turned_rows(rows_ref):
    rows = rows_ref[...]
    half = rows.shape[1] // 2
    return jnp.concatenate([rows[:, half:], rows[:, :half]], axis=1)


def field_table(positions_ref, types_ref):
    hydrogen = (types_ref[...] == 1).astype(F32)
    return jnp.concatenate(
        [positions_ref[0], positions_ref[1], positions_ref[2], hydrogen]
        + [jnp.zeros((OCTET - 4, hydrogen.shape[1]), F32)],
        axis=0,
    )


def outgoing_kernel(positions_ref, types_ref, rows_ref, own_ref, send_ref):
    own = field_table(positions_ref, types_ref)
    own_ref[...] = own
    send_ref[...] = lookup(own, jnp.broadcast_to(turned_rows(rows_ref), own.shape))


def force_kernel(
    live_ref,
    near_refs,
    far_refs,
    listed_ref,
    scale_ref,
    shift_ref,
    two_ref,
    bias_two_ref,
    three_ref,
    bias_three_ref,
    first_hbm,
    fit_bias_first_hbm,
    second_hbm,
    fit_bias_second_hbm,
    third_hbm,
    fit_bias_third_hbm,
    readout_hbm,
    velocities_ref,
    out_ref,
    parcels_ref,
    own_t,
    padded,
    two_in,
    two_out,
    three_in,
    three_out,
    consts,
    environ,
    offset,
    around,
    kept_one,
    kept_two,
    kept_three,
    kept_sum,
    features,
    features_t,
    descriptor,
    grad_descriptor,
    first_rows,
    products,
    grad_environ,
    grad_strength,
    centre_terms,
    scattered,
    first_ref,
    fit_bias_first_ref,
    second_ref,
    fit_bias_second_ref,
    third_ref,
    fit_bias_third_ref,
    readout_ref,
    own_ref,
    halo_ref,
    arrived,
):
    late = [
        pltpu.make_async_copy(source, target, arrived.at[k])
        for k, (source, target) in enumerate(
            (
                (first_hbm, first_ref),
                (fit_bias_first_hbm, fit_bias_first_ref),
                (second_hbm, second_ref),
                (fit_bias_second_hbm, fit_bias_second_ref),
                (third_hbm, third_ref),
                (fit_bias_third_hbm, fit_bias_third_ref),
                (readout_hbm, readout_ref),
            )
        )
    ]
    for copy in late:
        copy.start()
    if len(near_refs) > 1:
        own_ref[...] = field_table(*near_refs[:2])
        table = field_table(*far_refs[:2])
        halo_ref[...] = lookup(table, jnp.broadcast_to(turned_rows(far_refs[2]), table.shape))
    else:
        own_ref[...] = near_refs[0][...]
        halo_ref[...] = far_refs[0][...]
    live = live_ref[0]
    octets = (live + (OCTET - 1)) // OCTET
    atoms, slots = listed_ref.shape
    e1 = scale_ref.shape[1]
    e2 = two_ref.shape[1]
    e3 = three_ref.shape[1]
    rows_one, rows_two, rows_three = two_in.shape[0], three_in.shape[0], three_out.shape[0]
    copies_two, copies_three = e2 // e1, e3 // e1

    def split_bias(bias):
        high = bias.astype(BF16).astype(F32)
        return high, bias - high

    padded[...] = jnp.zeros_like(padded)
    bias_high, bias_low = split_bias(bias_two_ref[...])
    for k in range(copies_two):
        cols = slice(k * e1, (k + 1) * e1)
        padded[0:e1, k * CHUNK : k * CHUNK + e1] = two_ref[:, cols].astype(F32)
        padded[e1 : e1 + 1, k * CHUNK : k * CHUNK + e1] = bias_high[:, cols]
        padded[e1 + 1 : e1 + 2, k * CHUNK : k * CHUNK + e1] = bias_low[:, cols]
    table = padded[...]
    two_in[...] = table[:rows_one, :rows_two].astype(BF16)
    two_out[...] = table.T[:rows_two, :rows_one].astype(BF16)

    padded[...] = jnp.zeros_like(padded)
    bias_high, bias_low = split_bias(bias_three_ref[...])
    for k in range(copies_three):
        cols = slice(k * e1, (k + 1) * e1)
        for m in range(copies_two):
            padded[m * CHUNK : m * CHUNK + e1, k * CHUNK : k * CHUNK + e1] = three_ref[
                m * e1 : (m + 1) * e1, cols
            ].astype(F32)
        padded[e1 : e1 + 1, k * CHUNK : k * CHUNK + e1] = bias_high[:, cols]
        padded[e1 + 1 : e1 + 2, k * CHUNK : k * CHUNK + e1] = bias_low[:, cols]
    table = padded[...]
    three_in[...] = table[:rows_two, :rows_three].astype(BF16)
    three_out[...] = table.T[:rows_three, :rows_two].astype(BF16)

    padded[...] = jnp.zeros_like(padded)
    padded[0:2, 0:e1] = scale_ref[...]
    padded[2:4, 0:e1] = shift_ref[...]
    padded[2:3, e1 : e1 + 2] = jnp.full((1, 2), ONE_AT, F32)
    padded[3:4, e1 : e1 + 2] = jnp.full((1, 2), ONE_AT, F32)
    table = padded[...].T
    for k in range(4):
        column = table[:CHUNK, k : k + 1]
        if k % 2 == 1:
            column = column - table[:CHUNK, k - 1 : k]
        consts[k] = jnp.broadcast_to(column, (CHUNK, slots))

    padded[...] = jnp.zeros_like(padded)
    padded[0:OCTET, :] = own_ref[...]
    own_t[...] = padded[...].T

    features[...] = jnp.zeros_like(features)
    def gather_octet(first):
        listed = listed_ref[pl.ds(first, OCTET), :]
        low = jnp.bitwise_and(listed, LANES - 1)
        is_own = listed < atoms
        centre = own_t[pl.ds(first, OCTET), :]
        fetched = []
        for c in range(4):
            near = lookup(jnp.broadcast_to(own_ref[c : c + 1, :], (OCTET, LANES)), low)
            far = lookup(jnp.broadcast_to(halo_ref[c : c + 1, :], (OCTET, LANES)), low)
            fetched.append(jnp.where(is_own, near, far))
        deltas = [fetched[c] - centre[:, c : c + 1] for c in range(3)]
        return listed, deltas, fetched[3]

    def geometry(listed, deltas):
        filled = (listed >= 0).astype(F32)
        dist_sq = deltas[0] * deltas[0] + deltas[1] * deltas[1] + deltas[2] * deltas[2]
        inverse = lax.rsqrt(dist_sq + softening)
        switch = jnp.maximum(1.0 - dist_sq * (1.0 / cutoff_sq), 0.0)
        base = filled * switch * inverse
        return inverse, switch, base, base * switch

    def run_octets(step, carry=0):
        def body(turn, carry):
            for u in range(UNROLL):
                carry = step(turn * UNROLL + u, carry)
            return carry

        return lax.fori_loop(0, (octets + UNROLL - 1) // UNROLL, body, carry)

    def run_skewed(stages, skew):
        def body(turn, carry):
            waiting = [stages(turn * UNROLL + u) for u in range(UNROLL)]
            begun = 0
            active = []
            step = 0
            while begun < UNROLL or active:
                if begun < UNROLL and step % skew == 0:
                    active.append(waiting[begun])
                    begun += 1
                still = []
                for one in active:
                    try:
                        next(one)
                        still.append(one)
                    except StopIteration:
                        pass
                active = still
                step += 1
            return carry

        lax.fori_loop(0, (octets + UNROLL - 1) // UNROLL, body, 0)

    def surround(octet, carry):
        first = pl.multiple_of(octet * OCTET, OCTET)
        listed, deltas, hydrogen = gather_octet(first)
        inverse, _, _, strength = geometry(listed, deltas)
        around[pl.ds(first, OCTET), :] = hydrogen
        scaled = strength * inverse
        environ[pl.ds(first * 4, OCTET, stride=4), :] = strength
        for c in range(3):
            offset[c, pl.ds(first, OCTET), :] = deltas[c]
            environ[pl.ds(first * 4 + 1 + c, OCTET, stride=4), :] = scaled * deltas[c]
        return carry

    run_octets(surround)

    def forward(octet):
        first = pl.multiple_of(octet * OCTET, OCTET)
        hydrogen = around[pl.ds(first, OCTET), :]
        rows = pl.ds(pl.multiple_of(first * 4, OCTET * 4), OCTET * 4)
        groups = range(OCTET // GROUP)
        ones, twos, threes = [], [], []
        for g in groups:
            inputs = []
            for a in range(g * GROUP, (g + 1) * GROUP):
                line, kind = environ[pl.ds(first * 4 + 4 * a, 1), :], hydrogen[a : a + 1]
                inputs.append(
                    line * consts[0] + consts[2] + kind * (line * consts[1] + consts[3])
                )
            ones.append(jnp.tanh(jnp.concatenate(inputs, axis=1).astype(BF16)))
            yield
        for g in groups:
            kept_one[octet * len(groups) + g] = ones[g]
            two = jnp.tanh(
                jnp.dot(two_out[...], ones[g], preferred_element_type=F32).astype(BF16)
            )
            kept_two[octet * len(groups) + g] = two
            twos.append(two + jnp.concatenate([ones[g]] * copies_two, axis=0))
            yield
        by_slot = environ[rows, :].T.astype(BF16)
        column = lax.broadcasted_iota(jnp.int32, by_slot.shape, 1) // 4
        total = jnp.zeros((rows_three, OCTET * 4), F32)
        for g in groups:
            three = jnp.tanh(
                jnp.dot(three_out[...], twos[g], preferred_element_type=F32).astype(BF16)
            )
            kept_three[octet * len(groups) + g] = three
            sum_three = three + jnp.concatenate([twos[g]] * 2, axis=0)
            kept_sum[octet * len(groups) + g] = sum_three
            blocks = jnp.concatenate(
                [
                    jnp.where(column == a, by_slot, jnp.zeros_like(by_slot))
                    for a in range(g * GROUP, (g + 1) * GROUP)
                ],
                axis=0,
            )
            total = total + jnp.dot(sum_three, blocks, preferred_element_type=F32)
            yield
        features[rows, :] = total.T

    run_skewed(forward, 2)

    for copy in late:
        copy.wait()
    first_rows[...] = first_ref[...].T
    for c in range(4):
        features_t[c] = features[pl.ds(c, atoms, stride=4), :].T * (1.0 / slots)

    unit_rows = [q * CHUNK + r for q in range(copies_three) for r in range(e1)]
    leading = [features_t[c, 0:M2, :] for c in range(4)]
    for e, at in enumerate(unit_rows):
        total = None
        for c in range(4):
            term = features_t[c, at : at + 1, :] * leading[c]
            total = term if total is None else total + term
        descriptor[e * M2 : (e + 1) * M2, :] = total.astype(BF16)

    fit_one = jnp.tanh(
        jnp.dot(first_ref[...], descriptor[...], preferred_element_type=F32).T
        + fit_bias_first_ref[...]
    )
    tanh_two = jnp.tanh(
        jnp.dot(fit_one.astype(BF16), second_ref[...], preferred_element_type=F32)
        + fit_bias_second_ref[...]
    )
    fit_two = tanh_two + fit_one
    tanh_three = jnp.tanh(
        jnp.dot(fit_two.astype(BF16), third_ref[...], preferred_element_type=F32)
        + fit_bias_third_ref[...]
    )
    living = (lax.broadcasted_iota(jnp.int32, (atoms, 1), 0) < live).astype(F32)
    readout = readout_ref[0:1, :] + own_t[:, 3:4] * (readout_ref[1:2, :] - readout_ref[0:1, :])
    grad = living * readout
    contract_last = (((1,), (1,)), ((), ()))
    inner = (grad * (1.0 - tanh_three * tanh_three)).astype(BF16)
    grad = grad + lax.dot_general(inner, third_ref[...], contract_last, preferred_element_type=F32)
    inner = (grad * (1.0 - tanh_two * tanh_two)).astype(BF16)
    grad = grad + lax.dot_general(inner, second_ref[...], contract_last, preferred_element_type=F32)
    inner = (grad * (1.0 - fit_one * fit_one)).astype(BF16)
    grad_descriptor[...] = lax.dot_general(
        first_rows[...], inner, contract_last, preferred_element_type=F32
    )

    shared = [jnp.zeros((M2, atoms), F32) for _ in range(4)]
    short = [tile.astype(BF16) for tile in leading]
    for e, at in enumerate(unit_rows):
        rows = grad_descriptor[e * M2 : (e + 1) * M2, :]
        packed = rows.astype(BF16)
        for c in range(4):
            shared[c] = shared[c] + rows * features_t[c, at : at + 1, :]
            products[e * M2 : (e + 1) * M2, c * atoms : (c + 1) * atoms] = packed * short[c]
    unit = lax.broadcasted_iota(jnp.int32, (rows_three, 1), 0)
    unit = jnp.where(unit % CHUNK < e1, unit // CHUNK * e1 + unit % CHUNK, -1)
    gather = (lax.broadcasted_iota(jnp.int32, (1, e3 * M2), 1) // M2 == unit).astype(F32)
    sums = jnp.dot(gather.astype(BF16), products[...], preferred_element_type=F32)
    for c in range(4):
        total = sums[:, c * atoms : (c + 1) * atoms] + jnp.concatenate(
            [shared[c], jnp.zeros((rows_three - M2, atoms), F32)], axis=0
        )
        features[pl.ds(c, atoms, stride=4), :] = (total * (1.0 / slots)).T

    scattered[...] = jnp.zeros_like(scattered)
    centre_terms[...] = jnp.zeros_like(centre_terms)
    lane = lax.broadcasted_iota(jnp.int32, (OCTET, LANES), 1)

    def backward(octet):
        first = pl.multiple_of(octet * OCTET, OCTET)
        grad_rows = features[pl.ds(pl.multiple_of(first * 4, OCTET * 4), OCTET * 4), :]
        grad_cols = grad_rows.T.astype(BF16)
        grad_rows = grad_rows.astype(BF16)
        groups = range(OCTET // GROUP)
        rows = pl.ds(pl.multiple_of(first * 4, OCTET * 4), OCTET * 4)
        quads = environ[rows, :]
        owner = lax.broadcasted_iota(jnp.int32, quads.shape, 0) // 4
        by_quad = jnp.zeros_like(quads)
        inners, grad_threes, grad_twos = [], [], []
        for g in groups:
            at = octet * len(groups) + g
            blocks = jnp.concatenate(
                [
                    jnp.where(owner == a, quads, 0.0).astype(BF16)
                    for a in range(g * GROUP, (g + 1) * GROUP)
                ],
                axis=1,
            )
            grad_three = jnp.dot(grad_cols, blocks, preferred_element_type=F32).astype(BF16)
            three = kept_three[at]
            inners.append(grad_three * (1.0 - three * three))
            grad_threes.append(grad_three[:rows_two] + grad_three[rows_two:])
            yield
        for g in groups:
            at = octet * len(groups) + g
            grad_two = (
                jnp.dot(three_in[...], inners[g], preferred_element_type=F32).astype(BF16)
                + grad_threes[g]
            )
            two = kept_two[at]
            inners[g] = grad_two * (1.0 - two * two)
            folded = grad_two[:CHUNK]
            for k in range(1, copies_two):
                folded = folded + grad_two[k * CHUNK : (k + 1) * CHUNK]
            grad_twos.append(folded)
            both = jnp.dot(grad_rows, kept_sum[at], preferred_element_type=F32)
            for k in range(GROUP):
                by_quad = jnp.where(
                    owner == g * GROUP + k, both[:, k * LANES : (k + 1) * LANES], by_quad
                )
            yield
        grad_environ[rows, :] = by_quad
        for g in groups:
            at = octet * len(groups) + g
            grad_one = jnp.dot(two_in[...], inners[g], preferred_element_type=F32) + grad_twos[g]
            one = kept_one[at].astype(F32)
            grad_one = grad_one * (1.0 - one * one)
            for k in range(GROUP):
                line = first + g * GROUP + k
                kind = around[pl.ds(line, 1), :]
                weighed = grad_one[:, k * LANES : (k + 1) * LANES] * (
                    consts[0] + kind * consts[1]
                )
                grad_strength[pl.ds(line, 1), :] = jnp.sum(weighed, axis=0, keepdims=True)


    run_skewed(backward, 1)

    numbers = lax.broadcasted_iota(jnp.int32, (DIGIT, LANES), 0).astype(F32).astype(BF16)

    def tall(line):
        return jnp.broadcast_to(line, (DIGIT, LANES)).astype(BF16)

    def disperse(octet, total):
        first = pl.multiple_of(octet * OCTET, OCTET)
        listed = listed_ref[pl.ds(first, OCTET), :]
        deltas = [offset[c, pl.ds(first, OCTET), :] for c in range(3)]
        inverse, switch, base, strength = geometry(listed, deltas)
        by_environ = [
            grad_environ[pl.ds(first * 4 + c, OCTET, stride=4), :] for c in range(4)
        ]
        along = (
            by_environ[1] * deltas[0] + by_environ[2] * deltas[1] + by_environ[3] * deltas[2]
        )
        by_strength = (
            grad_strength[pl.ds(first, OCTET), :] + by_environ[0] + along * inverse
        )
        filled = (listed >= 0).astype(F32)
        by_inverse = strength * along + filled * switch * switch * by_strength
        by_dist = (-2.0 / cutoff_sq) * base * by_strength - (
            0.5 * inverse * inverse * inverse
        ) * by_inverse
        scaled = strength * inverse
        centre = jnp.zeros((OCTET, LANES), F32)
        terms = []
        for c in range(3):
            term = by_environ[1 + c] * scaled + 2.0 * deltas[c] * by_dist
            terms.append(term)
            centre = jnp.where(lane == c, jnp.sum(term, axis=1, keepdims=True), centre)
        centre_terms[pl.ds(first, OCTET), :] = centre
        upper_digit = (listed // DIGIT).astype(F32)
        lower_digit = jnp.bitwise_and(listed, DIGIT - 1).astype(F32)
        spread, hits = [], []
        for a in range(OCTET):
            here = numbers == tall(upper_digit[a : a + 1])
            zero = jnp.zeros((DIGIT, LANES), BF16)
            spread.append(
                jnp.concatenate([jnp.where(here, tall(t[a : a + 1]), zero) for t in terms], axis=0)
            )
            hits.append(
                jnp.where(numbers == tall(lower_digit[a : a + 1]), jnp.ones_like(zero), zero)
            )
        return total + lax.dot_general(
            jnp.concatenate(spread, axis=1),
            jnp.concatenate(hits, axis=1),
            contract_last,
            preferred_element_type=F32,
        )

    total = run_octets(disperse, jnp.zeros((3 * DIGIT, DIGIT), F32))
    for c in range(3):
        for d in range(DIGIT):
            scattered[c : c + 1, d * DIGIT : (d + 1) * DIGIT] = total[
                c * DIGIT + d : c * DIGIT + d + 1, :
            ]
    total = scattered[0:OCTET, :]
    force = centre_terms[...].T[0:OCTET, :] - total[:, 0:atoms]
    beyond = -total[:, atoms:]
    out_ref[:, 0:atoms] = force
    out_ref[:, atoms:] = beyond
    if parcels_ref.shape[0] > 1:
        mine = live_ref[1]
        kick = step_size * jnp.where(own_ref[3:4, :] == 1.0, 1.0, 1.0 / heavy_mass)
        moving = [own_ref[c : c + 1, :] for c in range(3)] + [
            velocities_ref[c] + kick * force[c : c + 1] for c in range(3)
        ]
        moving = jnp.concatenate(moving + [jnp.zeros((OCTET - 6, atoms), F32)], axis=0)
        out_ref[3:4, 0:atoms] = kick
        out_ref[4:5, 0:atoms] = turned_rows(near_refs[2]).astype(F32)
        for s in range(2):
            tile = jnp.where(mine == s, moving, beyond)
            for b in range(parcels_ref.shape[0] // 2):
                parcels_ref[2 * b + s] = tile


def kick_kernel(part_ref, back_ref, rows_ref, types_ref, positions_ref, velocities_ref, forces_ref, out_ref):
    atoms = types_ref.shape[1]
    rows = turned_rows(rows_ref)
    hits = (
        lax.broadcasted_iota(jnp.int32, (atoms, rows.shape[1]), 0) == rows
    ).astype(F32)
    returned = lax.dot_general(
        back_ref[...],
        hits,
        (((1,), (1,)), ((), ())),
        preferred_element_type=F32,
        precision=lax.Precision.HIGHEST,
    )
    force = part_ref[:, 0:atoms] + returned
    inverse_mass = jnp.where(types_ref[...] == 1, 1.0, 1.0 / heavy_mass)
    rows = []
    for c in range(3):
        forces_ref[c] = force[c : c + 1]
        rows.append(positions_ref[c])
    for c in range(3):
        rows.append(velocities_ref[c] + step_size * inverse_mass * force[c : c + 1])
    tile = jnp.concatenate(rows + [jnp.zeros((2, atoms), F32)], axis=0)
    for b in range(out_ref.shape[0]):
        out_ref[b] = tile


def mix_kernel(place_ref, table_ref, gathered_ref, positions_ref, velocities_ref):
    mine = place_ref[0]
    count = gathered_ref.shape[0]
    tile_shape = gathered_ref.shape[1:]
    is_position = lax.broadcasted_iota(jnp.int32, tile_shape, 0) < 3
    turned = jnp.zeros(tile_shape, F32)
    crossed = jnp.zeros(tile_shape, F32)
    for b in range(count):
        tile = gathered_ref[b]
        turned = turned + table_ref[mine, b] * tile
        crossed = crossed + jnp.where(
            is_position, -table_ref[mine, 2 * count + b], table_ref[mine, count + b]
        ) * tile
    for c in range(3):
        positions_ref[c] = turned[c : c + 1] + crossed[3 + c : 4 + c]
        velocities_ref[c] = turned[3 + c : 4 + c] + crossed[c : c + 1]


def settle_kernel(
    place_ref, table_ref, part_ref, gathered_ref, positions_ref, velocities_ref, forces_ref
):
    mine, slab = place_ref[0], place_ref[1]
    count = gathered_ref.shape[0] // 2
    tile_shape = gathered_ref.shape[1:]
    is_position = lax.broadcasted_iota(jnp.int32, tile_shape, 0) < 3
    zero = jnp.zeros(tile_shape, F32)
    turned, crossed, halo_turned, halo_travel = zero, zero, zero, zero
    for b in range(count):
        tile = gathered_ref[2 * b + slab]
        beyond = gathered_ref[2 * b + 1 - slab]
        cosine, travel = table_ref[mine, b], table_ref[mine, count + b]
        spring = table_ref[mine, 2 * count + b]
        turned = turned + cosine * tile
        crossed = crossed + jnp.where(is_position, -spring, travel) * tile
        halo_turned = halo_turned + cosine * beyond
        halo_travel = halo_travel + travel * beyond
    atoms = part_ref.shape[1] - gathered_ref.shape[2]
    rows = part_ref[4:5, 0:atoms].astype(jnp.int32)
    hits = lax.broadcasted_iota(jnp.int32, (atoms, rows.shape[1]), 0) == rows
    own_beyond = gathered_ref[2 * mine + 1 - slab]
    rest = jnp.concatenate([halo_travel, halo_turned, own_beyond], axis=0)
    parts = []
    for _ in range(3):
        parts.append(rest.astype(BF16))
        rest = rest - parts[-1].astype(F32)
    sums = lax.dot_general(
        jnp.concatenate(parts, axis=0),
        hits.astype(F32).astype(BF16),
        (((1,), (1,)), ((), ())),
        preferred_element_type=F32,
    )
    tall = 3 * OCTET
    returned = sums[:tall] + sums[tall : 2 * tall] + sums[2 * tall :]
    kick = part_ref[3:4, 0:atoms]
    for c in range(3):
        positions_ref[c] = (
            turned[c : c + 1] + crossed[3 + c : 4 + c] + kick * returned[c : c + 1]
        )
        velocities_ref[c] = (
            turned[3 + c : 4 + c]
            + crossed[c : c + 1]
            + kick * returned[OCTET + c : OCTET + c + 1]
        )
        forces_ref[c] = part_ref[c : c + 1, 0:atoms] + returned[2 * OCTET + c : 2 * OCTET + c + 1]


VMEM_SPEC = pl.BlockSpec(memory_space=pltpu.VMEM)
HBM_SPEC = pl.BlockSpec(memory_space=pltpu.HBM)
SMEM_SPEC = pl.BlockSpec(memory_space=pltpu.SMEM)
SMALL = pltpu.CompilerParams(vmem_limit_bytes=SMALL_LIMIT)


def shape(*dims, dtype=F32):
    return jax.ShapeDtypeStruct(dims, dtype)


def call_force(live_atoms, near, far, neighbours, weights, velocities, parcels=1):
    atoms, slots = neighbours.shape
    entries = atoms + far[-1].shape[1]
    e1 = weights[0].shape[1]
    e2 = weights[2].shape[1]
    e3 = weights[4].shape[1]
    rows_two = e2 // e1 * CHUNK
    rows_three = e3 // e1 * CHUNK
    assert entries <= DIGIT * DIGIT and slots == LANES and atoms == LANES and entries == 2 * LANES
    assert e3 == 2 * e2 and e2 == 2 * e1 and rows_three <= LANES and M2 <= e1
    groups = atoms // GROUP
    return pl.pallas_call(
        force_kernel,
        out_shape=(shape(OCTET, entries), shape(parcels, OCTET, atoms)),
        in_specs=(SMEM_SPEC, (VMEM_SPEC,) * len(near), (VMEM_SPEC,) * len(far))
        + (VMEM_SPEC,) * 7
        + (HBM_SPEC,) * (len(weights) - 6)
        + (VMEM_SPEC,),
        out_specs=(VMEM_SPEC, VMEM_SPEC),
        scratch_shapes=[
            pltpu.VMEM((atoms, LANES), F32),
            pltpu.VMEM((LANES, LANES), F32),
            pltpu.VMEM((CHUNK, rows_two), BF16),
            pltpu.VMEM((rows_two, CHUNK), BF16),
            pltpu.VMEM((rows_two, rows_three), BF16),
            pltpu.VMEM((rows_three, rows_two), BF16),
            pltpu.VMEM((4, CHUNK, slots), F32),
            pltpu.VMEM((4 * atoms, slots), F32),
            pltpu.VMEM((3, atoms, slots), F32),
            pltpu.VMEM((atoms, slots), F32),
            pltpu.VMEM((groups, CHUNK, GROUP * slots), BF16),
            pltpu.VMEM((groups, rows_two, GROUP * slots), BF16),
            pltpu.VMEM((groups, rows_three, GROUP * slots), BF16),
            pltpu.VMEM((groups, rows_three, GROUP * slots), BF16),
            pltpu.VMEM((4 * atoms, rows_three), F32),
            pltpu.VMEM((4, rows_three, atoms), F32),
            pltpu.VMEM((e3 * M2, atoms), BF16),
            pltpu.VMEM((e3 * M2, atoms), F32),
            pltpu.VMEM(weights[6].shape[::-1], BF16),
            pltpu.VMEM((e3 * M2, 4 * atoms), BF16),
            pltpu.VMEM((4 * atoms, slots), F32),
            pltpu.VMEM((atoms, slots), F32),
            pltpu.VMEM((atoms, LANES), F32),
            pltpu.VMEM((OCTET, entries), F32),
        ]
        + [pltpu.VMEM(w.shape, w.dtype) for w in weights[6:]]
        + [pltpu.VMEM((OCTET, atoms), F32), pltpu.VMEM((OCTET, entries - atoms), F32)]
        + [pltpu.SemaphoreType.DMA((len(weights) - 6,))],
        compiler_params=pltpu.CompilerParams(vmem_limit_bytes=VMEM_LIMIT),
        name="force",
    )(live_atoms, near, far, neighbours, *weights, velocities)


def row(array):
    return array.reshape(1, -1)


def local(
    positions,
    velocities,
    atom_types,
    live_atoms,
    halo_rows,
    neighbours,
    type_scale,
    type_shift,
    embed_two,
    embed_bias_two,
    embed_three,
    embed_bias_three,
    fit_first,
    fit_bias_first,
    fit_second,
    fit_bias_second,
    fit_third,
    fit_bias_third,
    fit_readout,
):
    weights = (
        type_scale,
        type_shift,
        embed_two,
        row(embed_bias_two),
        embed_three,
        row(embed_bias_three),
        fit_first.T,
        row(fit_bias_first),
        fit_second,
        row(fit_bias_second),
        fit_third,
        row(fit_bias_third),
        fit_readout,
    )
    atoms = positions.shape[2]
    half = halo_rows.shape[1] // 2
    beads = lax.axis_size("bead")
    slabs = lax.axis_size("slab")
    to_next = [(i, (i + 1) % slabs) for i in range(slabs)]
    to_last = [((i + 1) % slabs, i) for i in range(slabs)]

    def exchange(outgoing, up, down):
        return jnp.concatenate(
            [
                lax.ppermute(outgoing[:, up], "slab", to_next),
                lax.ppermute(outgoing[:, down], "slab", to_last),
            ],
            axis=1,
        )

    low, high = slice(0, half), slice(half, 2 * half)
    types = row(atom_types)
    place = jnp.stack([lax.axis_index("bead"), lax.axis_index("slab")]).astype(jnp.int32)
    scalars = jnp.concatenate([live_atoms, place[1:]])
    table = jnp.asarray(bead_tables(beads))
    sharded_shape = shape(*positions.shape)
    if slabs == 2:
        far = tuple(lax.ppermute(a, "slab", to_next) for a in (positions, types, halo_rows))
        part, parcels = call_force(
            scalars, (positions, types, halo_rows), far, neighbours, weights, velocities, beads * slabs
        )
        gathered = lax.all_to_all(
            parcels, ("bead", "slab"), split_axis=0, concat_axis=0, tiled=True
        )
        return pl.pallas_call(
            settle_kernel,
            out_shape=(sharded_shape,) * 3,
            in_specs=[SMEM_SPEC] * 2 + [VMEM_SPEC] * 2,
            out_specs=(VMEM_SPEC,) * 3,
            compiler_params=SMALL,
            name="settle",
        )(place, table, part, gathered)
    own, sent = pl.pallas_call(
        outgoing_kernel,
        out_shape=(shape(OCTET, atoms), shape(OCTET, 2 * half)),
        in_specs=[VMEM_SPEC] * 3,
        out_specs=(VMEM_SPEC, VMEM_SPEC),
        compiler_params=SMALL,
        name="outgoing",
    )(positions, types, halo_rows)
    halo = exchange(sent, low, high)
    part, _ = call_force(scalars, (own,), (halo,), neighbours, weights, velocities)
    back = exchange(part[:, atoms:], high, low)
    back = jnp.concatenate([back[:, high], back[:, low]], axis=1)
    forces, kicked = pl.pallas_call(
        kick_kernel,
        out_shape=(sharded_shape, shape(beads, OCTET, atoms)),
        in_specs=[VMEM_SPEC] * 6,
        out_specs=(VMEM_SPEC, VMEM_SPEC),
        compiler_params=SMALL,
        name="kick",
    )(part, back, halo_rows, types, positions, velocities)
    gathered = lax.all_to_all(kicked, "bead", split_axis=0, concat_axis=0, tiled=True)
    positions_new, velocities_new = pl.pallas_call(
        mix_kernel,
        out_shape=(sharded_shape, sharded_shape),
        in_specs=[SMEM_SPEC, SMEM_SPEC, VMEM_SPEC],
        out_specs=(VMEM_SPEC, VMEM_SPEC),
        compiler_params=SMALL,
        name="mix",
    )(place, table, gathered)
    return positions_new, velocities_new, forces


def solution(mesh):
    sharded = P(None, "bead", "slab")
    return jax.shard_map(
        local,
        mesh=mesh,
        in_specs=(
            sharded,
            sharded,
            P("slab"),
            P("slab"),
            P("slab", None),
            P("slab", None),
        )
        + (P(),) * 13,
        out_specs=(sharded, sharded, sharded),
        check_vma=False,
    )
```

```python
import functools
import math

import jax
import jax.numpy as jnp
import numpy as np
from jax import lax
from jax.experimental import pallas as pl
from jax.experimental.pallas import tpu as pltpu
from jax.sharding import PartitionSpec as P

M2 = 16
step_size = 0.25
phase_rate = 1.2
cutoff_sq = 16.0
softening = 0.25
heavy_mass = 16.0

F32 = jnp.float32
BF16 = jnp.bfloat16
LANES = 128
OCTET = 8
UNROLL = 16
DIGIT = 16
GROUP = 2
CHUNK = 32
ONE_AT = 20.0
VMEM_LIMIT = 55168 * 1024
SMALL_LIMIT = 4 * 1024 * 1024


def bead_tables(count):
    index = np.arange(count)
    angles = 2.0 * np.pi * np.outer(index, index) / count
    norm = math.sqrt(2.0 / count)
    edge = 1.0 / math.sqrt(count)
    middle = count // 2
    basis = np.where(
        index[None, :] == 0,
        edge,
        np.where(
            index[None, :] < middle,
            norm * np.cos(angles),
            np.where(
                index[None, :] == middle, np.cos(np.pi * index)[:, None] * edge, norm * np.sin(angles)
            ),
        ),
    )
    sine = np.sin(np.pi * index / count)
    ratio = 2.0 * sine
    phases = phase_rate * count * sine
    travel = np.where(index == 0, 1.0, np.sin(phases) / np.where(index == 0, 1.0, ratio))

    def assemble(diagonal):
        return (basis * diagonal[None, :]) @ basis.T

    return np.concatenate(
        [assemble(np.cos(phases)), assemble(travel), assemble(ratio * np.sin(phases))], axis=1
    ).astype(np.float32)


def lookup(table, indices):
    return jnp.take_along_axis(table, indices, axis=1, mode="promise_in_bounds")


def turned_rows(rows_ref):
    rows = rows_ref[...]
    half = rows.shape[1] // 2
    return jnp.concatenate([rows[:, half:], rows[:, :half]], axis=1)


def field_table(positions_ref, types_ref):
    hydrogen = (types_ref[...] == 1).astype(F32)
    return jnp.concatenate(
        [positions_ref[0], positions_ref[1], positions_ref[2], hydrogen]
        + [jnp.zeros((OCTET - 4, hydrogen.shape[1]), F32)],
        axis=0,
    )


def outgoing_kernel(positions_ref, types_ref, rows_ref, own_ref, send_ref):
    own = field_table(positions_ref, types_ref)
    own_ref[...] = own
    send_ref[...] = lookup(own, jnp.broadcast_to(turned_rows(rows_ref), own.shape))


def force_kernel(
    live_ref,
    near_refs,
    far_refs,
    listed_ref,
    scale_ref,
    shift_ref,
    two_ref,
    bias_two_ref,
    three_ref,
    bias_three_ref,
    first_hbm,
    fit_bias_first_hbm,
    second_hbm,
    fit_bias_second_hbm,
    third_hbm,
    fit_bias_third_hbm,
    readout_hbm,
    velocities_ref,
    out_ref,
    parcels_ref,
    own_t,
    padded,
    two_in,
    two_out,
    three_in,
    three_out,
    consts,
    environ,
    offset,
    around,
    kept_one,
    kept_two,
    kept_three,
    kept_sum,
    features,
    features_t,
    descriptor,
    grad_descriptor,
    first_rows,
    products,
    grad_environ,
    grad_strength,
    centre_terms,
    scattered,
    first_ref,
    fit_bias_first_ref,
    second_ref,
    fit_bias_second_ref,
    third_ref,
    fit_bias_third_ref,
    readout_ref,
    own_ref,
    halo_ref,
    arrived,
):
    late = [
        pltpu.make_async_copy(source, target, arrived.at[k])
        for k, (source, target) in enumerate(
            (
                (first_hbm, first_ref),
                (fit_bias_first_hbm, fit_bias_first_ref),
                (second_hbm, second_ref),
                (fit_bias_second_hbm, fit_bias_second_ref),
                (third_hbm, third_ref),
                (fit_bias_third_hbm, fit_bias_third_ref),
                (readout_hbm, readout_ref),
            )
        )
    ]
    for copy in late:
        copy.start()
    if len(near_refs) > 1:
        own_ref[...] = field_table(*near_refs[:2])
        table = field_table(*far_refs[:2])
        halo_ref[...] = lookup(table, jnp.broadcast_to(turned_rows(far_refs[2]), table.shape))
    else:
        own_ref[...] = near_refs[0][...]
        halo_ref[...] = far_refs[0][...]
    live = live_ref[0]
    octets = (live + (OCTET - 1)) // OCTET
    atoms, slots = listed_ref.shape
    e1 = scale_ref.shape[1]
    e2 = two_ref.shape[1]
    e3 = three_ref.shape[1]
    rows_one, rows_two, rows_three = two_in.shape[0], three_in.shape[0], three_out.shape[0]
    copies_two, copies_three = e2 // e1, e3 // e1

    def split_bias(bias):
        high = bias.astype(BF16).astype(F32)
        return high, bias - high

    padded[...] = jnp.zeros_like(padded)
    bias_high, bias_low = split_bias(bias_two_ref[...])
    for k in range(copies_two):
        cols = slice(k * e1, (k + 1) * e1)
        padded[0:e1, k * CHUNK : k * CHUNK + e1] = two_ref[:, cols].astype(F32)
        padded[e1 : e1 + 1, k * CHUNK : k * CHUNK + e1] = bias_high[:, cols]
        padded[e1 + 1 : e1 + 2, k * CHUNK : k * CHUNK + e1] = bias_low[:, cols]
    table = padded[...]
    two_in[...] = table[:rows_one, :rows_two].astype(BF16)
    two_out[...] = table.T[:rows_two, :rows_one].astype(BF16)

    padded[...] = jnp.zeros_like(padded)
    bias_high, bias_low = split_bias(bias_three_ref[...])
    three = three_ref[...].astype(F32)
    for k in range(copies_three):
        cols = slice(k * e1, (k + 1) * e1)
        for m in range(copies_two):
            padded[m * CHUNK : m * CHUNK + e1, k * CHUNK : k * CHUNK + e1] = three[
                m * e1 : (m + 1) * e1, cols
            ]
        padded[e1 : e1 + 1, k * CHUNK : k * CHUNK + e1] = bias_high[:, cols]
        padded[e1 + 1 : e1 + 2, k * CHUNK : k * CHUNK + e1] = bias_low[:, cols]
    table = padded[...]
    three_in[...] = table[:rows_two, :rows_three].astype(BF16)
    three_out[...] = table.T[:rows_three, :rows_two].astype(BF16)

    padded[...] = jnp.zeros_like(padded)
    padded[0:2, 0:e1] = scale_ref[...]
    padded[2:4, 0:e1] = shift_ref[...]
    padded[2:3, e1 : e1 + 2] = jnp.full((1, 2), ONE_AT, F32)
    padded[3:4, e1 : e1 + 2] = jnp.full((1, 2), ONE_AT, F32)
    table = padded[...].T
    for k in range(4):
        column = table[:CHUNK, k : k + 1]
        if k % 2 == 1:
            column = column - table[:CHUNK, k - 1 : k]
        consts[k] = jnp.broadcast_to(column, (CHUNK, slots))

    padded[...] = jnp.zeros_like(padded)
    padded[0:OCTET, :] = own_ref[...]
    own_t[...] = padded[...].T

    features[...] = jnp.zeros_like(features)
    def gather_octet(first):
        listed = listed_ref[pl.ds(first, OCTET), :]
        low = jnp.bitwise_and(listed, LANES - 1)
        is_own = listed < atoms
        centre = own_t[pl.ds(first, OCTET), :]
        fetched = []
        for c in range(4):
            near = lookup(jnp.broadcast_to(own_ref[c : c + 1, :], (OCTET, LANES)), low)
            far = lookup(jnp.broadcast_to(halo_ref[c : c + 1, :], (OCTET, LANES)), low)
            fetched.append(jnp.where(is_own, near, far))
        deltas = [fetched[c] - centre[:, c : c + 1] for c in range(3)]
        return listed, deltas, fetched[3]

    def geometry(listed, deltas):
        filled = (listed >= 0).astype(F32)
        dist_sq = deltas[0] * deltas[0] + deltas[1] * deltas[1] + deltas[2] * deltas[2]
        inverse = lax.rsqrt(dist_sq + softening)
        switch = jnp.maximum(1.0 - dist_sq * (1.0 / cutoff_sq), 0.0)
        base = filled * switch * inverse
        return inverse, switch, base, base * switch

    def run_octets(step, carry=0):
        def body(turn, carry):
            for u in range(UNROLL):
                carry = step(turn * UNROLL + u, carry)
            return carry

        return lax.fori_loop(0, (octets + UNROLL - 1) // UNROLL, body, carry)

    def run_skewed(stages, skew):
        def body(turn, carry):
            waiting = [stages(turn * UNROLL + u) for u in range(UNROLL)]
            begun = 0
            active = []
            step = 0
            while begun < UNROLL or active:
                if begun < UNROLL and step % skew == 0:
                    active.append(waiting[begun])
                    begun += 1
                still = []
                for one in active:
                    try:
                        next(one)
                        still.append(one)
                    except StopIteration:
                        pass
                active = still
                step += 1
            return carry

        lax.fori_loop(0, (octets + UNROLL - 1) // UNROLL, body, 0)

    def surround(octet, carry):
        first = pl.multiple_of(octet * OCTET, OCTET)
        listed, deltas, hydrogen = gather_octet(first)
        inverse, _, _, strength = geometry(listed, deltas)
        around[pl.ds(first, OCTET), :] = hydrogen
        scaled = strength * inverse
        environ[pl.ds(first * 4, OCTET, stride=4), :] = strength
        for c in range(3):
            offset[c, pl.ds(first, OCTET), :] = deltas[c]
            environ[pl.ds(first * 4 + 1 + c, OCTET, stride=4), :] = scaled * deltas[c]
        return carry

    run_octets(surround)

    def forward(octet):
        first = pl.multiple_of(octet * OCTET, OCTET)
        hydrogen = around[pl.ds(first, OCTET), :]
        rows = pl.ds(pl.multiple_of(first * 4, OCTET * 4), OCTET * 4)
        groups = range(OCTET // GROUP)
        ones, twos, threes = [], [], []
        for g in groups:
            inputs = []
            for a in range(g * GROUP, (g + 1) * GROUP):
                line, kind = environ[pl.ds(first * 4 + 4 * a, 1), :], hydrogen[a : a + 1]
                inputs.append(
                    line * consts[0] + consts[2] + kind * (line * consts[1] + consts[3])
                )
            ones.append(jnp.tanh(jnp.concatenate(inputs, axis=1).astype(BF16)))
            yield
        for g in groups:
            kept_one[octet * len(groups) + g] = ones[g]
            two = jnp.tanh(
                jnp.dot(two_out[...], ones[g], preferred_element_type=F32).astype(BF16)
            )
            kept_two[octet * len(groups) + g] = two
            twos.append(two + jnp.concatenate([ones[g]] * copies_two, axis=0))
            yield
        by_slot = environ[rows, :].T.astype(BF16)
        column = lax.broadcasted_iota(jnp.int32, by_slot.shape, 1) // 4
        total = jnp.zeros((rows_three, OCTET * 4), F32)
        for g in groups:
            three = jnp.tanh(
                jnp.dot(three_out[...], twos[g], preferred_element_type=F32).astype(BF16)
            )
            kept_three[octet * len(groups) + g] = three
            sum_three = three + jnp.concatenate([twos[g]] * 2, axis=0)
            kept_sum[octet * len(groups) + g] = sum_three
            blocks = jnp.concatenate(
                [
                    jnp.where(column == a, by_slot, jnp.zeros_like(by_slot))
                    for a in range(g * GROUP, (g + 1) * GROUP)
                ],
                axis=0,
            )
            total = total + jnp.dot(sum_three, blocks, preferred_element_type=F32)
            yield
        features[rows, :] = total.T

    run_skewed(forward, 2)

    for copy in late:
        copy.wait()
    first_rows[...] = first_ref[...].T
    for c in range(4):
        features_t[c] = features[pl.ds(c, atoms, stride=4), :].T * (1.0 / slots)

    unit_rows = [q * CHUNK + r for q in range(copies_three) for r in range(e1)]
    leading = [features_t[c, 0:M2, :] for c in range(4)]
    for e, at in enumerate(unit_rows):
        total = None
        for c in range(4):
            term = features_t[c, at : at + 1, :] * leading[c]
            total = term if total is None else total + term
        descriptor[e * M2 : (e + 1) * M2, :] = total.astype(BF16)

    fit_one = jnp.tanh(
        jnp.dot(first_ref[...], descriptor[...], preferred_element_type=F32).T
        + fit_bias_first_ref[...]
    )
    tanh_two = jnp.tanh(
        jnp.dot(fit_one.astype(BF16), second_ref[...], preferred_element_type=F32)
        + fit_bias_second_ref[...]
    )
    fit_two = tanh_two + fit_one
    tanh_three = jnp.tanh(
        jnp.dot(fit_two.astype(BF16), third_ref[...], preferred_element_type=F32)
        + fit_bias_third_ref[...]
    )
    living = (lax.broadcasted_iota(jnp.int32, (atoms, 1), 0) < live).astype(F32)
    readout = readout_ref[0:1, :] + own_t[:, 3:4] * (readout_ref[1:2, :] - readout_ref[0:1, :])
    grad = living * readout
    contract_last = (((1,), (1,)), ((), ()))
    inner = (grad * (1.0 - tanh_three * tanh_three)).astype(BF16)
    grad = grad + lax.dot_general(inner, third_ref[...], contract_last, preferred_element_type=F32)
    inner = (grad * (1.0 - tanh_two * tanh_two)).astype(BF16)
    grad = grad + lax.dot_general(inner, second_ref[...], contract_last, preferred_element_type=F32)
    inner = (grad * (1.0 - fit_one * fit_one)).astype(BF16)
    grad_descriptor[...] = lax.dot_general(
        first_rows[...], inner, contract_last, preferred_element_type=F32
    )

    shared = [jnp.zeros((M2, atoms), F32) for _ in range(4)]
    short = [tile.astype(BF16) for tile in leading]
    for e, at in enumerate(unit_rows):
        rows = grad_descriptor[e * M2 : (e + 1) * M2, :]
        packed = rows.astype(BF16)
        for c in range(4):
            shared[c] = shared[c] + rows * features_t[c, at : at + 1, :]
            products[e * M2 : (e + 1) * M2, c * atoms : (c + 1) * atoms] = packed * short[c]
    unit = lax.broadcasted_iota(jnp.int32, (rows_three, 1), 0)
    unit = jnp.where(unit % CHUNK < e1, unit // CHUNK * e1 + unit % CHUNK, -1)
    gather = (lax.broadcasted_iota(jnp.int32, (1, e3 * M2), 1) // M2 == unit).astype(F32)
    sums = jnp.dot(gather.astype(BF16), products[...], preferred_element_type=F32)
    for c in range(4):
        total = sums[:, c * atoms : (c + 1) * atoms] + jnp.concatenate(
            [shared[c], jnp.zeros((rows_three - M2, atoms), F32)], axis=0
        )
        features[pl.ds(c, atoms, stride=4), :] = (total * (1.0 / slots)).T

    scattered[...] = jnp.zeros_like(scattered)
    centre_terms[...] = jnp.zeros_like(centre_terms)
    lane = lax.broadcasted_iota(jnp.int32, (OCTET, LANES), 1)

    def backward(octet):
        first = pl.multiple_of(octet * OCTET, OCTET)
        grad_rows = features[pl.ds(pl.multiple_of(first * 4, OCTET * 4), OCTET * 4), :]
        grad_cols = grad_rows.T.astype(BF16)
        grad_rows = grad_rows.astype(BF16)
        groups = range(OCTET // GROUP)
        rows = pl.ds(pl.multiple_of(first * 4, OCTET * 4), OCTET * 4)
        quads = environ[rows, :]
        owner = lax.broadcasted_iota(jnp.int32, quads.shape, 0) // 4
        by_quad = jnp.zeros_like(quads)
        inners, grad_threes, grad_twos = [], [], []
        for g in groups:
            at = octet * len(groups) + g
            blocks = jnp.concatenate(
                [
                    jnp.where(owner == a, quads, 0.0).astype(BF16)
                    for a in range(g * GROUP, (g + 1) * GROUP)
                ],
                axis=1,
            )
            grad_three = jnp.dot(grad_cols, blocks, preferred_element_type=F32).astype(BF16)
            three = kept_three[at]
            inners.append(grad_three * (1.0 - three * three))
            grad_threes.append(grad_three[:rows_two] + grad_three[rows_two:])
            yield
        for g in groups:
            at = octet * len(groups) + g
            grad_two = (
                jnp.dot(three_in[...], inners[g], preferred_element_type=F32).astype(BF16)
                + grad_threes[g]
            )
            two = kept_two[at]
            inners[g] = grad_two * (1.0 - two * two)
            folded = grad_two[:CHUNK]
            for k in range(1, copies_two):
                folded = folded + grad_two[k * CHUNK : (k + 1) * CHUNK]
            grad_twos.append(folded)
            both = jnp.dot(grad_rows, kept_sum[at], preferred_element_type=F32)
            for k in range(GROUP):
                by_quad = jnp.where(
                    owner == g * GROUP + k, both[:, k * LANES : (k + 1) * LANES], by_quad
                )
            yield
        grad_environ[rows, :] = by_quad
        for g in groups:
            at = octet * len(groups) + g
            grad_one = jnp.dot(two_in[...], inners[g], preferred_element_type=F32) + grad_twos[g]
            one = kept_one[at].astype(F32)
            grad_one = grad_one * (1.0 - one * one)
            for k in range(GROUP):
                line = first + g * GROUP + k
                kind = around[pl.ds(line, 1), :]
                weighed = grad_one[:, k * LANES : (k + 1) * LANES] * (
                    consts[0] + kind * consts[1]
                )
                grad_strength[pl.ds(line, 1), :] = jnp.sum(weighed, axis=0, keepdims=True)


    run_skewed(backward, 1)

    numbers = lax.broadcasted_iota(jnp.int32, (DIGIT, LANES), 0).astype(F32).astype(BF16)

    def tall(line):
        return jnp.broadcast_to(line, (DIGIT, LANES)).astype(BF16)

    def disperse(octet, total):
        first = pl.multiple_of(octet * OCTET, OCTET)
        listed = listed_ref[pl.ds(first, OCTET), :]
        deltas = [offset[c, pl.ds(first, OCTET), :] for c in range(3)]
        inverse, switch, base, strength = geometry(listed, deltas)
        by_environ = [
            grad_environ[pl.ds(first * 4 + c, OCTET, stride=4), :] for c in range(4)
        ]
        along = (
            by_environ[1] * deltas[0] + by_environ[2] * deltas[1] + by_environ[3] * deltas[2]
        )
        by_strength = (
            grad_strength[pl.ds(first, OCTET), :] + by_environ[0] + along * inverse
        )
        filled = (listed >= 0).astype(F32)
        by_inverse = strength * along + filled * switch * switch * by_strength
        by_dist = (-2.0 / cutoff_sq) * base * by_strength - (
            0.5 * inverse * inverse * inverse
        ) * by_inverse
        scaled = strength * inverse
        centre = jnp.zeros((OCTET, LANES), F32)
        terms = []
        for c in range(3):
            term = by_environ[1 + c] * scaled + 2.0 * deltas[c] * by_dist
            terms.append(term)
            centre = jnp.where(lane == c, jnp.sum(term, axis=1, keepdims=True), centre)
        centre_terms[pl.ds(first, OCTET), :] = centre
        upper_digit = (listed // DIGIT).astype(F32)
        lower_digit = jnp.bitwise_and(listed, DIGIT - 1).astype(F32)
        spread, hits = [], []
        for a in range(OCTET):
            here = numbers == tall(upper_digit[a : a + 1])
            zero = jnp.zeros((DIGIT, LANES), BF16)
            spread.append(
                jnp.concatenate([jnp.where(here, tall(t[a : a + 1]), zero) for t in terms], axis=0)
            )
            hits.append(
                jnp.where(numbers == tall(lower_digit[a : a + 1]), jnp.ones_like(zero), zero)
            )
        return total + lax.dot_general(
            jnp.concatenate(spread, axis=1),
            jnp.concatenate(hits, axis=1),
            contract_last,
            preferred_element_type=F32,
        )

    total = run_octets(disperse, jnp.zeros((3 * DIGIT, DIGIT), F32))
    for c in range(3):
        for d in range(DIGIT):
            scattered[c : c + 1, d * DIGIT : (d + 1) * DIGIT] = total[
                c * DIGIT + d : c * DIGIT + d + 1, :
            ]
    total = scattered[0:OCTET, :]
    force = centre_terms[...].T[0:OCTET, :] - total[:, 0:atoms]
    beyond = -total[:, atoms:]
    out_ref[:, 0:atoms] = force
    out_ref[:, atoms:] = beyond
    if parcels_ref.shape[0] > 1:
        mine = live_ref[1]
        kick = step_size * jnp.where(own_ref[3:4, :] == 1.0, 1.0, 1.0 / heavy_mass)
        moving = [own_ref[c : c + 1, :] for c in range(3)] + [
            velocities_ref[c] + kick * force[c : c + 1] for c in range(3)
        ]
        moving = jnp.concatenate(moving + [jnp.zeros((OCTET - 6, atoms), F32)], axis=0)
        out_ref[3:4, 0:atoms] = kick
        out_ref[4:5, 0:atoms] = turned_rows(near_refs[2]).astype(F32)
        for s in range(2):
            tile = jnp.where(mine == s, moving, beyond)
            for b in range(parcels_ref.shape[0] // 2):
                parcels_ref[2 * b + s] = tile


def kick_kernel(part_ref, back_ref, rows_ref, types_ref, positions_ref, velocities_ref, forces_ref, out_ref):
    atoms = types_ref.shape[1]
    rows = turned_rows(rows_ref)
    hits = (
        lax.broadcasted_iota(jnp.int32, (atoms, rows.shape[1]), 0) == rows
    ).astype(F32)
    returned = lax.dot_general(
        back_ref[...],
        hits,
        (((1,), (1,)), ((), ())),
        preferred_element_type=F32,
        precision=lax.Precision.HIGHEST,
    )
    force = part_ref[:, 0:atoms] + returned
    inverse_mass = jnp.where(types_ref[...] == 1, 1.0, 1.0 / heavy_mass)
    rows = []
    for c in range(3):
        forces_ref[c] = force[c : c + 1]
        rows.append(positions_ref[c])
    for c in range(3):
        rows.append(velocities_ref[c] + step_size * inverse_mass * force[c : c + 1])
    tile = jnp.concatenate(rows + [jnp.zeros((2, atoms), F32)], axis=0)
    for b in range(out_ref.shape[0]):
        out_ref[b] = tile


def mix_kernel(place_ref, table_ref, gathered_ref, positions_ref, velocities_ref):
    mine = place_ref[0]
    count = gathered_ref.shape[0]
    tile_shape = gathered_ref.shape[1:]
    is_position = lax.broadcasted_iota(jnp.int32, tile_shape, 0) < 3
    turned = jnp.zeros(tile_shape, F32)
    crossed = jnp.zeros(tile_shape, F32)
    for b in range(count):
        tile = gathered_ref[b]
        turned = turned + table_ref[mine, b] * tile
        crossed = crossed + jnp.where(
            is_position, -table_ref[mine, 2 * count + b], table_ref[mine, count + b]
        ) * tile
    for c in range(3):
        positions_ref[c] = turned[c : c + 1] + crossed[3 + c : 4 + c]
        velocities_ref[c] = turned[3 + c : 4 + c] + crossed[c : c + 1]


def settle_kernel(
    place_ref, table_ref, part_ref, gathered_ref, positions_ref, velocities_ref, forces_ref
):
    mine, slab = place_ref[0], place_ref[1]
    count = gathered_ref.shape[0] // 2
    tile_shape = gathered_ref.shape[1:]
    is_position = lax.broadcasted_iota(jnp.int32, tile_shape, 0) < 3
    zero = jnp.zeros(tile_shape, F32)
    turned, crossed, halo_turned, halo_travel = zero, zero, zero, zero
    for b in range(count):
        tile = gathered_ref[2 * b + slab]
        beyond = gathered_ref[2 * b + 1 - slab]
        cosine, travel = table_ref[mine, b], table_ref[mine, count + b]
        spring = table_ref[mine, 2 * count + b]
        turned = turned + cosine * tile
        crossed = crossed + jnp.where(is_position, -spring, travel) * tile
        halo_turned = halo_turned + cosine * beyond
        halo_travel = halo_travel + travel * beyond
    atoms = part_ref.shape[1] - gathered_ref.shape[2]
    rows = part_ref[4:5, 0:atoms].astype(jnp.int32)
    hits = lax.broadcasted_iota(jnp.int32, (atoms, rows.shape[1]), 0) == rows
    own_beyond = gathered_ref[2 * mine + 1 - slab]
    rest = jnp.concatenate([halo_travel, halo_turned, own_beyond], axis=0)
    parts = []
    for _ in range(3):
        parts.append(rest.astype(BF16))
        rest = rest - parts[-1].astype(F32)
    sums = lax.dot_general(
        jnp.concatenate(parts, axis=0),
        hits.astype(F32).astype(BF16),
        (((1,), (1,)), ((), ())),
        preferred_element_type=F32,
    )
    tall = 3 * OCTET
    returned = sums[:tall] + sums[tall : 2 * tall] + sums[2 * tall :]
    kick = part_ref[3:4, 0:atoms]
    for c in range(3):
        positions_ref[c] = (
            turned[c : c + 1] + crossed[3 + c : 4 + c] + kick * returned[c : c + 1]
        )
        velocities_ref[c] = (
            turned[3 + c : 4 + c]
            + crossed[c : c + 1]
            + kick * returned[OCTET + c : OCTET + c + 1]
        )
        forces_ref[c] = part_ref[c : c + 1, 0:atoms] + returned[2 * OCTET + c : 2 * OCTET + c + 1]


VMEM_SPEC = pl.BlockSpec(memory_space=pltpu.VMEM)
HBM_SPEC = pl.BlockSpec(memory_space=pltpu.HBM)
SMEM_SPEC = pl.BlockSpec(memory_space=pltpu.SMEM)
SMALL = pltpu.CompilerParams(vmem_limit_bytes=SMALL_LIMIT)


def shape(*dims, dtype=F32):
    return jax.ShapeDtypeStruct(dims, dtype)


def call_force(live_atoms, near, far, neighbours, weights, velocities, parcels=1):
    atoms, slots = neighbours.shape
    entries = atoms + far[-1].shape[1]
    e1 = weights[0].shape[1]
    e2 = weights[2].shape[1]
    e3 = weights[4].shape[1]
    rows_two = e2 // e1 * CHUNK
    rows_three = e3 // e1 * CHUNK
    assert entries <= DIGIT * DIGIT and slots == LANES and atoms == LANES and entries == 2 * LANES
    assert e3 == 2 * e2 and e2 == 2 * e1 and rows_three <= LANES and M2 <= e1
    groups = atoms // GROUP
    return pl.pallas_call(
        force_kernel,
        out_shape=(shape(OCTET, entries), shape(parcels, OCTET, atoms)),
        in_specs=(SMEM_SPEC, (VMEM_SPEC,) * len(near), (VMEM_SPEC,) * len(far))
        + (VMEM_SPEC,) * 7
        + (HBM_SPEC,) * (len(weights) - 6)
        + (VMEM_SPEC,),
        out_specs=(VMEM_SPEC, VMEM_SPEC),
        scratch_shapes=[
            pltpu.VMEM((atoms, LANES), F32),
            pltpu.VMEM((LANES, LANES), F32),
            pltpu.VMEM((CHUNK, rows_two), BF16),
            pltpu.VMEM((rows_two, CHUNK), BF16),
            pltpu.VMEM((rows_two, rows_three), BF16),
            pltpu.VMEM((rows_three, rows_two), BF16),
            pltpu.VMEM((4, CHUNK, slots), F32),
            pltpu.VMEM((4 * atoms, slots), F32),
            pltpu.VMEM((3, atoms, slots), F32),
            pltpu.VMEM((atoms, slots), F32),
            pltpu.VMEM((groups, CHUNK, GROUP * slots), BF16),
            pltpu.VMEM((groups, rows_two, GROUP * slots), BF16),
            pltpu.VMEM((groups, rows_three, GROUP * slots), BF16),
            pltpu.VMEM((groups, rows_three, GROUP * slots), BF16),
            pltpu.VMEM((4 * atoms, rows_three), F32),
            pltpu.VMEM((4, rows_three, atoms), F32),
            pltpu.VMEM((e3 * M2, atoms), BF16),
            pltpu.VMEM((e3 * M2, atoms), F32),
            pltpu.VMEM(weights[6].shape[::-1], BF16),
            pltpu.VMEM((e3 * M2, 4 * atoms), BF16),
            pltpu.VMEM((4 * atoms, slots), F32),
            pltpu.VMEM((atoms, slots), F32),
            pltpu.VMEM((atoms, LANES), F32),
            pltpu.VMEM((OCTET, entries), F32),
        ]
        + [pltpu.VMEM(w.shape, w.dtype) for w in weights[6:]]
        + [pltpu.VMEM((OCTET, atoms), F32), pltpu.VMEM((OCTET, entries - atoms), F32)]
        + [pltpu.SemaphoreType.DMA((len(weights) - 6,))],
        compiler_params=pltpu.CompilerParams(vmem_limit_bytes=VMEM_LIMIT),
        name="force",
    )(live_atoms, near, far, neighbours, *weights, velocities)


def row(array):
    return array.reshape(1, -1)


def local(
    positions,
    velocities,
    atom_types,
    live_atoms,
    halo_rows,
    neighbours,
    type_scale,
    type_shift,
    embed_two,
    embed_bias_two,
    embed_three,
    embed_bias_three,
    fit_first,
    fit_bias_first,
    fit_second,
    fit_bias_second,
    fit_third,
    fit_bias_third,
    fit_readout,
):
    weights = (
        type_scale,
        type_shift,
        embed_two,
        row(embed_bias_two),
        embed_three,
        row(embed_bias_three),
        fit_first.T,
        row(fit_bias_first),
        fit_second,
        row(fit_bias_second),
        fit_third,
        row(fit_bias_third),
        fit_readout,
    )
    atoms = positions.shape[2]
    half = halo_rows.shape[1] // 2
    beads = lax.axis_size("bead")
    slabs = lax.axis_size("slab")
    to_next = [(i, (i + 1) % slabs) for i in range(slabs)]
    to_last = [((i + 1) % slabs, i) for i in range(slabs)]

    def exchange(outgoing, up, down):
        return jnp.concatenate(
            [
                lax.ppermute(outgoing[:, up], "slab", to_next),
                lax.ppermute(outgoing[:, down], "slab", to_last),
            ],
            axis=1,
        )

    low, high = slice(0, half), slice(half, 2 * half)
    types = row(atom_types)
    place = jnp.stack([lax.axis_index("bead"), lax.axis_index("slab")]).astype(jnp.int32)
    scalars = jnp.concatenate([live_atoms, place[1:]])
    table = jnp.asarray(bead_tables(beads))
    sharded_shape = shape(*positions.shape)
    if slabs == 2:
        far = tuple(lax.ppermute(a, "slab", to_next) for a in (positions, types, halo_rows))
        part, parcels = call_force(
            scalars, (positions, types, halo_rows), far, neighbours, weights, velocities, beads * slabs
        )
        gathered = lax.all_to_all(
            parcels, ("bead", "slab"), split_axis=0, concat_axis=0, tiled=True
        )
        return pl.pallas_call(
            settle_kernel,
            out_shape=(sharded_shape,) * 3,
            in_specs=[SMEM_SPEC] * 2 + [VMEM_SPEC] * 2,
            out_specs=(VMEM_SPEC,) * 3,
            compiler_params=SMALL,
            name="settle",
        )(place, table, part, gathered)
    own, sent = pl.pallas_call(
        outgoing_kernel,
        out_shape=(shape(OCTET, atoms), shape(OCTET, 2 * half)),
        in_specs=[VMEM_SPEC] * 3,
        out_specs=(VMEM_SPEC, VMEM_SPEC),
        compiler_params=SMALL,
        name="outgoing",
    )(positions, types, halo_rows)
    halo = exchange(sent, low, high)
    part, _ = call_force(scalars, (own,), (halo,), neighbours, weights, velocities)
    back = exchange(part[:, atoms:], high, low)
    back = jnp.concatenate([back[:, high], back[:, low]], axis=1)
    forces, kicked = pl.pallas_call(
        kick_kernel,
        out_shape=(sharded_shape, shape(beads, OCTET, atoms)),
        in_specs=[VMEM_SPEC] * 6,
        out_specs=(VMEM_SPEC, VMEM_SPEC),
        compiler_params=SMALL,
        name="kick",
    )(part, back, halo_rows, types, positions, velocities)
    gathered = lax.all_to_all(kicked, "bead", split_axis=0, concat_axis=0, tiled=True)
    positions_new, velocities_new = pl.pallas_call(
        mix_kernel,
        out_shape=(sharded_shape, sharded_shape),
        in_specs=[SMEM_SPEC, SMEM_SPEC, VMEM_SPEC],
        out_specs=(VMEM_SPEC, VMEM_SPEC),
        compiler_params=SMALL,
        name="mix",
    )(place, table, gathered)
    return positions_new, velocities_new, forces


def solution(mesh):
    sharded = P(None, "bead", "slab")
    return jax.shard_map(
        local,
        mesh=mesh,
        in_specs=(
            sharded,
            sharded,
            P("slab"),
            P("slab"),
            P("slab", None),
            P("slab", None),
        )
        + (P(),) * 13,
        out_specs=(sharded, sharded, sharded),
        check_vma=False,
    )
```
